32 devices in a mesh: cells: 16 (over z, y, x), rep: 2 (over core).
Axes of the slice: x: 2, y: 2, z: 4, core: 2. Of those that a mesh axis runs over, the one named last changes fastest.
Arguments:
- cells_x: bfloat16 [18432, 7000], P(('cells', 'rep')), may hold values from -12 to 12
- latent_noise: float32 [18432, 100], P(('cells', 'rep')), may hold values from -6 to 6
- group_ids: int32 [18432], P(('cells', 'rep')), may hold values from 0 to 63, as said below
- owner_table: int32 [16, 4], replicated, may hold values from 0 to 31, as said below
- owner_mask: int32 [16, 4], replicated, may hold values from 0 to 1
- enc_w1: bfloat16 [7000, 800], replicated, may hold values from -0.0625 to 0.0625
- enc_w2: bfloat16 [800, 800], replicated, may hold values from -0.21875 to 0.21875
- head_w: bfloat16 [800, 200], replicated, may hold values from -0.21875 to 0.21875
- head_b: float32 [200], replicated, may hold values from -3 to 3
- dec_w1: bfloat16 [100, 800], replicated, may hold values from -0.625 to 0.625
- dec_w2: bfloat16 [800, 800], replicated, may hold values from -0.21875 to 0.21875
- out_w: bfloat16 [800, 7000], replicated, may hold values from -0.109375 to 0.109375
- out_b: float32 [7000], replicated, may hold values from -0.05 to 0.05
- bn_gain: float32 [4, 800], replicated, may hold values from 0.25 to 1.75
- bn_shift: float32 [4, 800], replicated, may hold values from -0.7 to -0.3
Outputs:
- grad_x: float32 [18432, 7000], P(('cells', 'rep'))
- grad_enc_w1: float32 [6400, 875], P(('cells', 'rep'))
- grad_narrow: float32 [2048, 625], P(('cells', 'rep'))
- grad_head_w: float32 [800, 200], replicated
- grad_dec_w1: float32 [100, 800], replicated
- grad_head_b: float32 [200], replicated
- grad_out_w: float32 [6400, 875], P(('cells', 'rep'))
- grad_out_b: float32 [7000], replicated
- grad_gain: float32 [4, 800], replicated
- grad_shift: float32 [4, 800], replicated
- offsets: float32 [16, 4, 100], P('cells')
The draws below stay inside these ranges and needn't reach their ends.
Inputs may be any that keep to these rules, and one draw needn't show every extreme that they name: `group_ids`: A cell's group is 2 * its population + its condition (1 stimulated, 0 control); populations differ in size, and some groups hold no cells. `owner_table`: each population 0 to 31 stands in exactly one live slot; a row's live slots come first and masked slots hold 0; some rows have all 4 slots live and some none.
All inputs are finite; a program needn't handle non-finite values.
Results may differ from the reference program's by a relative error of at most 0.018.
Values sent between devices are 32-bit elements; how exact they have to be, the bound alone decides.
A program may use at most 256 MiB of HBM per device.

```python
import jax
import jax.numpy as jnp
from jax import lax

GENES = 7000
HIDDEN_SIZE = 800
LATENT = 100
POP_DEV = 2
FLAT_COLS = 875
NARROW_COLS = 625
CELLS = 18432
NPOP = 32
OWNERS = 16
SLOTS = 4
FLAT_ROWS = 6400
NARROW_ROWS = 2048


def owner_layout(key):
    order_key, pop_key = jax.random.split(jax.random.fold_in(key, 17))
    owner_order = jax.random.permutation(order_key, OWNERS)
    quarter = OWNERS // 4
    position = jnp.arange(OWNERS, dtype=jnp.int32)
    by_position = jnp.where(position < quarter, SLOTS, jnp.where(position < 2 * quarter, 0, POP_DEV)).astype(jnp.int32)
    counts = jnp.zeros((OWNERS,), jnp.int32).at[owner_order].set(by_position)
    starts = jnp.cumsum(counts) - counts
    populations = jax.random.permutation(pop_key, NPOP).astype(jnp.int32)
    slot_index = jnp.arange(SLOTS, dtype=jnp.int32)
    live = slot_index[None, :] < counts[:, None]
    index = jnp.minimum(starts[:, None] + slot_index[None, :], NPOP - 1)
    table = jnp.where(live, populations[index], 0)
    return (table.astype(jnp.int32), live.astype(jnp.int32))


def draw_owner_table(key, part):
    return owner_layout(key)[0]


def draw_owner_mask(key, part):
    return owner_layout(key)[1]


def draw_group_ids(key, part):
    weight_key, pick_key, cond_key, force_key, side_key = jax.random.split(jax.random.fold_in(key, 29), 5)
    weights = jax.random.randint(weight_key, (NPOP,), 1, 5)
    bounds = jnp.cumsum(weights)
    picks = jax.random.randint(pick_key, (CELLS,), 0, bounds[-1])
    population = jnp.searchsorted(bounds, picks, side='right').astype(jnp.int32)
    condition = jax.random.randint(cond_key, (CELLS,), 0, 2).astype(jnp.int32)
    forced_count = NPOP // 8 + 1
    chosen = (jax.random.permutation(force_key, NPOP - 2)[:forced_count] + 1).astype(jnp.int32)
    forced = jnp.zeros((NPOP,), jnp.int32).at[chosen].set(1)
    side = jax.random.randint(side_key, (NPOP,), 0, 2).astype(jnp.int32)
    condition = jnp.where(forced[population] == 1, side[population], condition).astype(jnp.int32)
    return (2 * population + condition).astype(jnp.int32)


def block_levels(stream_key, extent, cuts, least, top_value):
    def one(axis_at, shards_of):
        steps = jax.random.uniform(jax.random.fold_in(jax.random.fold_in(stream_key, 6), axis_at), (shards_of,), jnp.float32, least / len(cuts), top_value / len(cuts))
        return jnp.repeat(jnp.exp(steps), extent[axis_at] // shards_of).reshape((-1,) + (1,) * (len(extent) - axis_at - 1))

    factor_of = one(*cuts[0])
    for cut in cuts[1:]:
        factor_of = factor_of * one(*cut)
    return factor_of


def gaussian(key, extent, scale, most, cuts=(), held_as=jnp.bfloat16):
    result = jax.random.normal(key, extent, jnp.float32) * scale
    if len(cuts) > 0:
        result = block_levels(key, extent, cuts, -0.22, 0.18) * result
    return jnp.clip(result, min=-most, max=most).astype(held_as)


def setup_inputs(seed: int = 0) -> dict:
    splits = jax.random.split(jax.random.key(seed), 16)
    cells_x = gaussian(splits[0], (CELLS, GENES), 2.0, 12.0, ((0, 32),))
    latent_noise = gaussian(splits[1], (CELLS, LATENT), 1.0, 6.0, ((0, 32),), jnp.float32)
    group_ids = draw_group_ids(jax.random.fold_in(splits[15], 71), 0)
    owner_table = draw_owner_table(jax.random.fold_in(splits[15], 71), 0)
    owner_mask = draw_owner_mask(jax.random.fold_in(splits[15], 71), 0)
    enc_w1 = gaussian(splits[5], (GENES, HIDDEN_SIZE), GENES ** -0.5, 0.0625)
    enc_w2 = gaussian(splits[6], (HIDDEN_SIZE, HIDDEN_SIZE), HIDDEN_SIZE ** -0.5, 0.21875)
    head_w = gaussian(splits[7], (HIDDEN_SIZE, 2 * LATENT), HIDDEN_SIZE ** -0.5, 0.21875)
    head_b = gaussian(splits[8], (2 * LATENT,), 0.5, 3.0, (), jnp.float32)
    dec_w1 = gaussian(splits[9], (LATENT, HIDDEN_SIZE), LATENT ** -0.5, 0.625)
    dec_w2 = gaussian(splits[10], (HIDDEN_SIZE, HIDDEN_SIZE), HIDDEN_SIZE ** -0.5, 0.21875)
    out_w = gaussian(splits[11], (HIDDEN_SIZE, GENES), (4 * HIDDEN_SIZE) ** -0.5, 0.109375)
    out_b = jnp.clip(jax.random.uniform(splits[12], (GENES,), jnp.float32, -0.05, 0.05), -0.05, 0.05)
    bn_gain = jnp.clip(1.0 + 0.15 * jax.random.normal(splits[13], (4, HIDDEN_SIZE), jnp.float32), 0.25, 1.75)
    bn_shift = jnp.clip(jax.random.uniform(splits[14], (4, HIDDEN_SIZE), jnp.float32, -0.7, -0.3), -0.7, -0.3)
    return dict(cells_x=cells_x, latent_noise=latent_noise, group_ids=group_ids, owner_table=owner_table, owner_mask=owner_mask, enc_w1=enc_w1, enc_w2=enc_w2, head_w=head_w, head_b=head_b, dec_w1=dec_w1, dec_w2=dec_w2, out_w=out_w, out_b=out_b, bn_gain=bn_gain, bn_shift=bn_shift)


NORM_EPSILON = 1e-05
KL_WEIGHT = 5e-05
OFFSET_WEIGHT = 200.0

@jax.custom_vjp
def low(v):
    return lax.optimization_barrier(v.astype(jnp.bfloat16)).astype(jnp.float32)

@jax.custom_vjp
def low_back(v):
    return v

def low_keep(v):
    return (low(v), None)

def low_pass(kept, grad):
    return (grad,)

def back_keep(v):
    return (v, None)

def back_low(kept, grad):
    return (low(grad),)
low.defvjp(low_keep, low_pass)
low_back.defvjp(back_keep, back_low)

def matmul(left, right):
    return jnp.dot(left, right, precision=lax.Precision.HIGHEST, preferred_element_type=jnp.float32)

def batch_norm(values, norm_gain, norm_shift):
    centered = values - lax.optimization_barrier(jnp.mean(values, axis=0))
    spread = lax.optimization_barrier(jnp.mean(centered * centered, axis=0))
    pre_act = norm_gain * (centered * lax.rsqrt(spread + NORM_EPSILON)) + norm_shift
    return jax.nn.silu(pre_act)

def forward(cells_x, enc_w1, enc_w2, head_w, head_b, dec_w1, dec_w2, out_w, out_b, bn_gain, bn_shift, latent_noise, group_ids):
    first_pre = low_back(matmul(cells_x, enc_w1))
    first_act = low(batch_norm(first_pre, bn_gain[0], bn_shift[0]))
    second_pre = low_back(matmul(first_act, enc_w2))
    second_act = low(batch_norm(second_pre, bn_gain[1], bn_shift[1]))
    head_out = low_back(matmul(second_act, head_w) + head_b)
    latent_mean = head_out[:, :LATENT]
    logvar = head_out[:, LATENT:]
    latent_draw = low(latent_mean + jnp.exp(0.5 * logvar) * latent_noise)
    third_pre = low_back(matmul(latent_draw, dec_w1))
    third_act = low(batch_norm(third_pre, bn_gain[2], bn_shift[2]))
    fourth_pre = low_back(matmul(third_act, dec_w2))
    fourth_act = low(batch_norm(fourth_pre, bn_gain[3], bn_shift[3]))
    recon = low_back(matmul(fourth_act, out_w) + out_b)
    cell_total = cells_x.shape[0]
    squared = jnp.sum(jnp.square(recon - cells_x)) / cell_total
    kl_term = 0.5 * jnp.sum(jnp.exp(logvar) + latent_mean * latent_mean - 1.0 - logvar) / cell_total
    sums = jax.ops.segment_sum(latent_mean, group_ids, num_segments=2 * NPOP)
    counts = jax.ops.segment_sum(jnp.ones((cell_total,), jnp.float32), group_ids, num_segments=2 * NPOP)
    group_means = (sums / jnp.maximum(counts, 1.0)[:, None]).reshape(NPOP, 2, LATENT)
    offset = group_means[:, 1] - group_means[:, 0]
    spread = offset - lax.optimization_barrier(jnp.mean(offset, axis=0))
    omega = jnp.sum(spread * spread) / NPOP
    loss = squared + KL_WEIGHT * GENES * kl_term + OFFSET_WEIGHT * omega
    return (loss, offset)

def reference(cells_x, latent_noise, group_ids, owner_table, owner_mask, enc_w1, enc_w2, head_w, head_b, dec_w1, dec_w2, out_w, out_b, bn_gain, bn_shift):
    params = tuple((value.astype(jnp.float32) for value in (cells_x, enc_w1, enc_w2, head_w, head_b, dec_w1, dec_w2, out_w, out_b, bn_gain, bn_shift)))

    def objective(*values):
        return forward(*values, latent_noise, group_ids)
    loss, pull, offset = jax.vjp(objective, *params, has_aux=True)
    grads = pull(jnp.ones_like(loss))
    cell_total = cells_x.shape[0]
    grad_x = grads[0] * cell_total
    grad_enc_w1 = grads[1].reshape(FLAT_ROWS, FLAT_COLS)
    grad_out_w = grads[7].reshape(FLAT_ROWS, FLAT_COLS)
    grad_narrow = jnp.concatenate([grads[2].reshape(-1), grads[6].reshape(-1)]).reshape(NARROW_ROWS, NARROW_COLS)
    offsets = jnp.take(offset, owner_table, axis=0) * owner_mask[..., None].astype(jnp.float32)
    return (grad_x, grad_enc_w1, grad_narrow, grads[3], grads[5], grads[4], grad_out_w, grads[8], grads[9], grads[10], offsets)
```

```python
import functools

import jax
import jax.numpy as jnp
from jax import lax
from jax.experimental import pallas as pl
from jax.experimental.pallas import tpu as pltpu
from jax.sharding import PartitionSpec as P

POP_DEV = 2
FLAT_COLS = 875
NARROW_COLS = 625
FLAT_ROWS = 6400
NARROW_ROWS = 2048

NORM_EPSILON = 1e-05
KL_WEIGHT = 5e-05
OFFSET_WEIGHT = 200.0

MESH_ID = pl.DeviceIdType.MESH
WIN = 1024
ROWS = 48
F32 = jnp.float32
BF16 = jnp.bfloat16


class Slice:
    def __init__(self, cells, rep):
        self.cells, self.rep = cells, rep
        self.n = cells * rep
        self.bits = self.n.bit_length() - 1
        self.digits = []
        low = 0
        while low < self.bits:
            width = min(3, self.bits - low)
            self.digits.append((low, 1 << width))
            low += width

    def me(self):
        return lax.axis_index("cells") * self.rep + lax.axis_index("rep")

    def place(self, index):
        return (index // self.rep, index % self.rep)


def entry_barrier(grid, peers):
    barrier = pltpu.get_barrier_semaphore()
    for peer in peers:
        pl.semaphore_signal(barrier, inc=1, device_id=grid.place(peer), device_id_type=MESH_ID)
    pl.semaphore_wait(barrier, len(peers))


def digit_peers(grid):
    me = grid.me()
    peers = []
    for low, size in grid.digits:
        rank = (me // (1 << low)) % size
        for k in range(1, size):
            other = (rank + k) % size
            peers.append(me + (other - rank) * (1 << low))
    return peers


class Gather:
    def __init__(self, grid, buffers, send_sems, recv_sems):
        self.grid, self.buffers, self.send_sems, self.recv_sems = grid, buffers, send_sems, recv_sems

    def rank(self, level):
        low, size = self.grid.digits[level]
        return (self.grid.me() // (1 << low)) % size

    def copy(self, level, slot, k, arriving=False):
        low, size = self.grid.digits[level]
        rank = self.rank(level)
        to = (rank + k) % size
        buffer = self.buffers[level].at[slot]
        return pltpu.make_async_remote_copy(
            src_ref=buffer.at[rank],
            dst_ref=buffer.at[(rank + size - k) % size if arriving else rank],
            send_sem=self.send_sems[level].at[slot, k - 1],
            recv_sem=self.recv_sems[level].at[slot, k - 1],
            device_id=self.grid.place(self.grid.me() + (to - rank) * (1 << low)),
            device_id_type=MESH_ID,
        )

    def start(self, level, slot):
        for k in range(1, self.grid.digits[level][1]):
            self.copy(level, slot, k).start()

    def wait(self, level, slot):
        for k in range(1, self.grid.digits[level][1]):
            self.copy(level, slot, k, arriving=True).wait_recv()

    def finish(self, level, slot):
        for k in range(1, self.grid.digits[level][1]):
            self.copy(level, slot, k).wait_send()

    def own(self, level, slot):
        return self.buffers[level].at[slot, self.rank(level)]


def put_row(ref, first, row, width):
    full = width // 128
    for c in range(full):
        ref[first + c : first + c + 1, :] = row[:, 128 * c : 128 * (c + 1)]
    rest = width - 128 * full
    if rest:
        ref[first + full : first + full + 1, 0:rest] = row[:, 128 * full : width]


def take_row(block, first, width):
    pieces = []
    for c in range(-(-width // 128)):
        pieces.append(block[first + c : first + c + 1, 0 : min(128, width - 128 * c)])
    return jnp.concatenate(pieces, axis=1)


def row_loop(rows, body, init):
    steps = rows // ROWS

    def step(i, carry):
        return body(pl.ds(pl.multiple_of(i * ROWS, ROWS), ROWS), carry)

    return lax.fori_loop(0, steps, step, init)


def column_sum(value):
    return jnp.sum(value, axis=0, keepdims=True)


def batch_norm(pre, nrm_out, act_out, gather, slot, gain_row, shift_row, inv_out):
    rows, width = pre.shape
    total = row_loop(rows, lambda r, c: c + column_sum(pre[r, :]), jnp.zeros((1, width), F32))
    mean = total * (1.0 / rows)

    def squares(r, c):
        d = pre[r, :] - mean
        return c + column_sum(d * d)

    square = row_loop(rows, squares, jnp.zeros((1, width), F32))
    own = gather.own(0, slot)
    put_row(own, 0, mean, width)
    put_row(own, 8, square, width)
    count = float(rows)
    levels = len(gather.grid.digits)
    for level in range(levels):
        size = gather.grid.digits[level][1]
        gather.start(level, slot)
        gather.wait(level, slot)
        buffer = gather.buffers[level].at[slot]
        means = [buffer[g, 0:8, :] for g in range(size)]
        merged = sum(means[1:], means[0]) * (1.0 / size)
        spread = sum([buffer[g, 8:16, :] for g in range(1, size)], buffer[0, 8:16, :])
        between = sum([(m - merged) * (m - merged) for m in means[1:]], (means[0] - merged) * (means[0] - merged))
        spread = spread + count * between
        count = count * size
        if level + 1 < levels:
            own = gather.own(level + 1, slot)
            own[0:8, :] = merged
            own[8:16, :] = spread
    inv = lax.rsqrt(spread * (1.0 / count) + NORM_EPSILON)
    mean = take_row(merged, 0, width)
    inv = take_row(inv, 0, width)
    inv_out[...] = inv

    def write(r, c):
        nrm = (pre[r, :] - mean) * inv
        nrm_out[r, :] = nrm
        value = gain_row * nrm + shift_row
        act_out[r, :] = (value * jax.nn.sigmoid(value)).astype(BF16)
        return c

    row_loop(rows, write, 0)


def nt(left, right):
    return lax.dot_general(left, right, (((1,), (1,)), ((), ())), preferred_element_type=F32)


def nn(left, right):
    return lax.dot_general(left, right, (((1,), (0,)), ((), ())), preferred_element_type=F32)


def tn(left, right):
    return lax.dot_general(left, right, (((0,), (0,)), ((), ())), preferred_element_type=F32)


def exact(left, right, dims):
    return lax.dot_general(
        left, right, (dims, ((), ())), precision=lax.Precision.HIGHEST, preferred_element_type=F32
    )


def windows(width):
    return [(s, min(WIN, width - s)) for s in range(0, width, WIN)]


def part_of(full, tail, i):
    return full.at[i] if i < full.shape[0] else tail


def forward_kernel(
    grid,
    table_ref,
    mask_ref,
    x_hbm,
    w1_hbm,
    noise_ref,
    gid_ref,
    w2_ref,
    head_ref,
    headb_ref,
    d1_ref,
    d2_ref,
    gain_ref,
    shift_ref,
    nrm0,
    nrm1,
    nrm2,
    nrm3,
    inv_out,
    act1,
    act2,
    zlat,
    act3,
    act4,
    head_out,
    ggroup_out,
    offsets_out,
    x_win,
    x_tail,
    w_win,
    w_tail,
    pre,
    moments,
    *rest,
):
    levels = len(grid.digits)
    small = rest[:levels]
    wide = rest[levels : 2 * levels]
    s_send, s_recv, g_send, g_recv = (
        rest[2 * levels : 3 * levels],
        rest[3 * levels : 4 * levels],
        rest[4 * levels : 5 * levels],
        rest[5 * levels : 6 * levels],
    )
    in_sems = rest[6 * levels]
    gather = Gather(grid, small, s_send, s_recv)
    group_gather = Gather(grid, wide, g_send, g_recv)
    latent = d1_ref.shape[0]
    genes = x_hbm.shape[1]
    spans = windows(genes)

    loads = []
    for i, (s, size) in enumerate(spans):
        a = pltpu.make_async_copy(x_hbm.at[:, pl.ds(s, size)], part_of(x_win, x_tail, i), in_sems.at[0, i])
        b = pltpu.make_async_copy(w1_hbm.at[:, pl.ds(s, size)], part_of(w_win, w_tail, i), in_sems.at[1, i])
        a.start()
        b.start()
        loads.append((a, b))
    entry_barrier(grid, digit_peers(grid))

    for i, (s, size) in enumerate(spans):
        loads[i][0].wait()
        loads[i][1].wait()
        part = nt(part_of(x_win, x_tail, i)[...], part_of(w_win, w_tail, i)[...])
        pre[...] = part if i == 0 else pre[...] + part

    def norm(k, nrm, act):
        batch_norm(
            pre, nrm, act, gather, k, gain_ref[k : k + 1, :], shift_ref[k : k + 1, :], inv_out.at[k : k + 1, :]
        )

    norm(0, nrm0, act1)
    pre[...] = nn(act1[...], w2_ref[...])
    norm(1, nrm1, act2)
    head = nt(act2[...], head_ref[...]) + headb_ref[...]
    head_out[...] = head
    mu = head[:, 0:latent]
    logvar = head[:, latent : 2 * latent]
    zlat[...] = (mu + jnp.exp(0.5 * logvar) * noise_ref[...]).astype(BF16)

    groups = ggroup_out.shape[0]
    pops = groups // 2
    cells_here = gid_ref.shape[1]
    member = (lax.broadcasted_iota(jnp.int32, (groups, cells_here), 0) == gid_ref[...]).astype(F32)
    own = group_gather.own(0, 0)
    own[:, 0:latent] = exact(member, mu, ((1,), (0,)))
    own[:, latent : latent + 1] = jnp.sum(member, axis=1, keepdims=True)
    group_gather.start(0, 0)

    pre[...] = nn(zlat[...], d1_ref[...])
    norm(2, nrm2, act3)
    for level in range(levels):
        group_gather.wait(level, 0)
        size = grid.digits[level][1]
        buffer = wide[level].at[0]
        total = sum([buffer[g] for g in range(1, size)], buffer[0])
        if level + 1 < levels:
            group_gather.own(level + 1, 0)[...] = total
            group_gather.start(level + 1, 0)
        if level == 0:
            pre[...] = nn(act3[...], d2_ref[...])
            norm(3, nrm3, act4)
    counted = jnp.maximum(total[:, latent : latent + 1], 1.0)
    moments[...] = total / counted
    odd, even = pl.ds(1, pops, stride=2), pl.ds(0, pops, stride=2)
    offset = moments[odd, :] - moments[even, :]
    centre = jnp.sum(offset, axis=0, keepdims=True) * (1.0 / pops)
    grad_offset = (2.0 * OFFSET_WEIGHT / pops) * (offset - centre)
    row = lax.axis_index("cells")
    slots = offsets_out.shape[0]
    lane = lax.broadcasted_iota(jnp.int32, (1, pops), 1)
    picks = jnp.concatenate(
        [jnp.where(lane == table_ref[row, s], mask_ref[row, s].astype(F32), 0.0) for s in range(slots)], axis=0
    )
    offsets_out[...] = exact(picks, offset, ((1,), (0,)))[:, 0:latent]
    moments[odd, :] = grad_offset
    moments[even, :] = -grad_offset
    ggroup_out[...] = moments[...] / counted

    for level in range(levels):
        for k in range(4):
            gather.finish(level, k)
        group_gather.finish(level, 0)


def call_forward(grid, cells_x, w1t, noise, gid, table, mask, w2, headt, headb, d1, d2, gain, shift):
    rows, genes = cells_x.shape
    hidden = w2.shape[0]
    latent = d1.shape[0]
    groups = 2 * POP_DEV * grid.cells
    count = len(windows(genes))
    levels = len(grid.digits)
    vm = pl.BlockSpec(memory_space=pltpu.VMEM)
    hbm = pl.BlockSpec(memory_space=pl.ANY)
    sm = pl.BlockSpec(memory_space=pltpu.SMEM)
    wide_f = jax.ShapeDtypeStruct((rows, hidden), F32)
    wide_b = jax.ShapeDtypeStruct((rows, hidden), BF16)
    out_shape = (
        wide_f,
        wide_f,
        wide_f,
        wide_f,
        jax.ShapeDtypeStruct((4, hidden), F32),
        wide_b,
        wide_b,
        jax.ShapeDtypeStruct((rows, latent), BF16),
        wide_b,
        wide_b,
        jax.ShapeDtypeStruct((rows, 2 * latent), F32),
        jax.ShapeDtypeStruct((groups, 128), F32),
        jax.ShapeDtypeStruct((table.shape[1], latent), F32),
    )
    scratch = (
        [
            pltpu.VMEM((count - 1, rows, WIN), BF16),
            pltpu.VMEM((rows, genes - (count - 1) * WIN), BF16),
            pltpu.VMEM((count - 1, hidden, WIN), BF16),
            pltpu.VMEM((hidden, genes - (count - 1) * WIN), BF16),
            pltpu.VMEM((rows, hidden), F32),
            pltpu.VMEM((groups, 128), F32),
        ]
        + [pltpu.VMEM((4, size, 16, 128), F32) for _, size in grid.digits]
        + [pltpu.VMEM((1, size, groups, 128), F32) for _, size in grid.digits]
        + [pltpu.SemaphoreType.DMA((4, size - 1)) for _, size in grid.digits]
        + [pltpu.SemaphoreType.DMA((4, size - 1)) for _, size in grid.digits]
        + [pltpu.SemaphoreType.DMA((1, size - 1)) for _, size in grid.digits]
        + [pltpu.SemaphoreType.DMA((1, size - 1)) for _, size in grid.digits]
        + [pltpu.SemaphoreType.DMA((2, count))]
    )
    return pl.pallas_call(
        functools.partial(forward_kernel, grid),
        out_shape=out_shape,
        in_specs=[sm, sm, hbm, hbm] + [vm] * 9,
        out_specs=[vm] * len(out_shape),
        scratch_shapes=scratch,
        name="forward",
        compiler_params=pltpu.CompilerParams(
            collective_id=0, has_side_effects=True, vmem_limit_bytes=60 * 2**20
        ),
    )(table, mask, cells_x, w1t, noise, gid, w2, headt, headb, d1, d2, gain, shift)


def contract_rows(left, right):
    return lax.dot_general(left, right, (((0,), (0,)), ((), ())), preferred_element_type=F32)


def contract_cols(left, right):
    return lax.dot_general(left, right, (((1,), (1,)), ((), ())), preferred_element_type=F32)


def norm_backward(grad_act, normed, inv_std, norm_gain, norm_shift, cell_total):
    pre_act = norm_gain * normed + norm_shift
    gate_value = jax.nn.sigmoid(pre_act)
    grad_pre = grad_act * gate_value * (1.0 + pre_act * (1.0 - gate_value))
    grad_shift, grad_gain = lax.psum(
        (jnp.sum(grad_pre, axis=0), jnp.sum(grad_pre * normed, axis=0)), ("cells", "rep")
    )
    grad_in = norm_gain * inv_std * (grad_pre - grad_shift / cell_total - normed * (grad_gain / cell_total))
    return (grad_in.astype(BF16), grad_gain, grad_shift)


def shards(
    grid,
    cells_x,
    latent_noise,
    group_ids,
    owner_table,
    owner_mask,
    enc_w1,
    enc_w2,
    head_w,
    head_b,
    dec_w1,
    dec_w2,
    out_w,
    out_b,
    bn_gain,
    bn_shift,
):
    cell_total = float(cells_x.shape[0] * grid.n)
    latent_width = dec_w1.shape[0]
    gene_count = cells_x.shape[1]
    (nrm0, nrm1, nrm2, nrm3, inv, first_act, second_act, latent_draw, third_act, fourth_act, head_out, ggroup, offsets) = (
        call_forward(
            grid,
            cells_x,
            enc_w1.T,
            latent_noise,
            group_ids.reshape(1, -1),
            owner_table,
            owner_mask,
            enc_w2,
            head_w.T,
            head_b.reshape(1, -1),
            dec_w1,
            dec_w2,
            bn_gain,
            bn_shift,
        )
    )
    latent_mean = head_out[:, :latent_width]
    logvar = head_out[:, latent_width:]
    deviation = jnp.exp(0.5 * logvar)
    member = (group_ids[:, None] == jnp.arange(ggroup.shape[0], dtype=jnp.int32)[None, :]).astype(F32)
    grad_group = jnp.dot(member, ggroup, precision=lax.Precision.HIGHEST, preferred_element_type=F32)[:, :latent_width]
    residual = (
        jnp.dot(fourth_act, out_w, preferred_element_type=F32) + out_b - cells_x.astype(F32)
    )
    grad_recon = (residual * (2.0 / cell_total)).astype(BF16)
    grad_out_w = contract_rows(fourth_act, grad_recon)
    grad_out_b = jnp.sum(grad_recon.astype(F32), axis=0)
    grad_fourth = contract_cols(grad_recon, out_w)
    grad_pre4, gain_three, shift_three = norm_backward(grad_fourth, nrm3, inv[3], bn_gain[3], bn_shift[3], cell_total)
    grad_dec_w2 = contract_rows(third_act, grad_pre4)
    grad_third = contract_cols(grad_pre4, dec_w2)
    grad_pre3, gain_two, shift_two = norm_backward(grad_third, nrm2, inv[2], bn_gain[2], bn_shift[2], cell_total)
    grad_dec_w1 = contract_rows(latent_draw, grad_pre3)
    grad_latent = contract_cols(grad_pre3, dec_w1)
    kl_scale = KL_WEIGHT * gene_count / cell_total
    grad_mean = grad_latent + kl_scale * latent_mean + grad_group
    grad_logvar = grad_latent * latent_noise * (0.5 * deviation) + 0.5 * kl_scale * (jnp.exp(logvar) - 1.0)
    grad_head = jnp.concatenate([grad_mean, grad_logvar], axis=1).astype(BF16)
    grad_head_w = contract_rows(second_act, grad_head)
    grad_head_b = jnp.sum(grad_head.astype(F32), axis=0)
    grad_second = contract_cols(grad_head, head_w)
    grad_pre2, gain_one, shift_one = norm_backward(grad_second, nrm1, inv[1], bn_gain[1], bn_shift[1], cell_total)
    grad_enc_w2 = contract_rows(first_act, grad_pre2)
    grad_first = contract_cols(grad_pre2, enc_w2)
    grad_pre1, gain_zero, shift_zero = norm_backward(grad_first, nrm0, inv[0], bn_gain[0], bn_shift[0], cell_total)
    grad_enc_w1 = contract_rows(cells_x, grad_pre1)
    grad_x = cell_total * contract_cols(grad_pre1, enc_w1) - 2.0 * residual
    summed_head_b, summed_out_b, summed_head_w, summed_dec_w1 = lax.psum(
        (grad_head_b, grad_out_b, grad_head_w, grad_dec_w1), ("cells", "rep")
    )
    flat_out = grad_out_w.reshape(FLAT_ROWS, FLAT_COLS)
    flat_enc = grad_enc_w1.reshape(FLAT_ROWS, FLAT_COLS)
    flat_narrow = jnp.concatenate([grad_enc_w2.reshape(-1), grad_dec_w2.reshape(-1)]).reshape(
        NARROW_ROWS, NARROW_COLS
    )
    shard_out, shard_enc, shard_narrow = (
        lax.psum_scatter(flat_out, ("cells", "rep"), scatter_dimension=0, tiled=True),
        lax.psum_scatter(flat_enc, ("cells", "rep"), scatter_dimension=0, tiled=True),
        lax.psum_scatter(flat_narrow, ("cells", "rep"), scatter_dimension=0, tiled=True),
    )
    grad_gain = jnp.stack([gain_zero, gain_one, gain_two, gain_three])
    grad_shift = jnp.stack([shift_zero, shift_one, shift_two, shift_three])
    return (
        grad_x,
        shard_enc,
        shard_narrow,
        summed_head_w,
        summed_dec_w1,
        summed_head_b,
        shard_out,
        summed_out_b,
        grad_gain,
        grad_shift,
        offsets[None],
    )


def solution(mesh):
    grid = Slice(mesh.shape["cells"], mesh.shape["rep"])
    lines = P(("cells", "rep"), None)
    return jax.shard_map(
        functools.partial(shards, grid),
        mesh=mesh,
        in_specs=(lines, lines, P(("cells", "rep"))) + (P(),) * 12,
        out_specs=(lines, lines, lines, P(), P(), P(), lines, P(), P(), P(), P("cells", None, None)),
        check_vma=False,
    )
```

```python
import functools

import jax
import jax.numpy as jnp
from jax import lax
from jax.experimental import pallas as pl
from jax.experimental.pallas import tpu as pltpu
from jax.sharding import PartitionSpec as P

POP_DEV = 2
FLAT_COLS = 875
NARROW_COLS = 625
FLAT_ROWS = 6400
NARROW_ROWS = 2048

NORM_EPSILON = 1e-05
KL_WEIGHT = 5e-05
OFFSET_WEIGHT = 200.0

MESH_ID = pl.DeviceIdType.MESH
WIN = 1024
ROWS = 48
F32 = jnp.float32
BF16 = jnp.bfloat16


class Slice:
    def __init__(self, cells, rep):
        self.cells, self.rep = cells, rep
        self.n = cells * rep
        self.bits = self.n.bit_length() - 1
        self.digits = []
        low = 0
        while low < self.bits:
            width = min(3, self.bits - low)
            self.digits.append((low, 1 << width))
            low += width

    def me(self):
        return lax.axis_index("cells") * self.rep + lax.axis_index("rep")

    def place(self, index):
        return (index // self.rep, index % self.rep)


def entry_barrier(grid, peers):
    barrier = pltpu.get_barrier_semaphore()
    for peer in peers:
        pl.semaphore_signal(barrier, inc=1, device_id=grid.place(peer), device_id_type=MESH_ID)
    pl.semaphore_wait(barrier, len(peers))


def digit_peers(grid):
    me = grid.me()
    peers = []
    for low, size in grid.digits:
        rank = (me // (1 << low)) % size
        for k in range(1, size):
            other = (rank + k) % size
            peers.append(me + (other - rank) * (1 << low))
    return peers


class Gather:
    def __init__(self, grid, buffers, send_sems, recv_sems):
        self.grid, self.buffers, self.send_sems, self.recv_sems = grid, buffers, send_sems, recv_sems

    def rank(self, level):
        low, size = self.grid.digits[level]
        return (self.grid.me() // (1 << low)) % size

    def copy(self, level, slot, k, arriving=False):
        low, size = self.grid.digits[level]
        rank = self.rank(level)
        to = (rank + k) % size
        buffer = self.buffers[level].at[slot]
        return pltpu.make_async_remote_copy(
            src_ref=buffer.at[rank],
            dst_ref=buffer.at[(rank + size - k) % size if arriving else rank],
            send_sem=self.send_sems[level].at[slot, k - 1],
            recv_sem=self.recv_sems[level].at[slot, k - 1],
            device_id=self.grid.place(self.grid.me() + (to - rank) * (1 << low)),
            device_id_type=MESH_ID,
        )

    def start(self, level, slot):
        for k in range(1, self.grid.digits[level][1]):
            self.copy(level, slot, k).start()

    def wait(self, level, slot):
        for k in range(1, self.grid.digits[level][1]):
            self.copy(level, slot, k, arriving=True).wait_recv()

    def finish(self, level, slot):
        for k in range(1, self.grid.digits[level][1]):
            self.copy(level, slot, k).wait_send()

    def own(self, level, slot):
        return self.buffers[level].at[slot, self.rank(level)]


def put_row(ref, first, row, width):
    full = width // 128
    for c in range(full):
        ref[first + c : first + c + 1, :] = row[:, 128 * c : 128 * (c + 1)]
    rest = width - 128 * full
    if rest:
        ref[first + full : first + full + 1, 0:rest] = row[:, 128 * full : width]


def take_row(block, first, width):
    pieces = []
    for c in range(-(-width // 128)):
        pieces.append(block[first + c : first + c + 1, 0 : min(128, width - 128 * c)])
    return jnp.concatenate(pieces, axis=1)


def row_loop(rows, body, init):
    steps = rows // ROWS

    def step(i, carry):
        return body(pl.ds(pl.multiple_of(i * ROWS, ROWS), ROWS), carry)

    return lax.fori_loop(0, steps, step, init)


def column_sum(value):
    return jnp.sum(value, axis=0, keepdims=True)


def batch_norm(pre, nrm_out, act_out, gather, slot, gain_row, shift_row, inv_out):
    rows, width = pre.shape
    total = row_loop(rows, lambda r, c: c + column_sum(pre[r, :]), jnp.zeros((1, width), F32))
    mean = total * (1.0 / rows)

    def squares(r, c):
        d = pre[r, :] - mean
        return c + column_sum(d * d)

    square = row_loop(rows, squares, jnp.zeros((1, width), F32))
    own = gather.own(0, slot)
    put_row(own, 0, mean, width)
    put_row(own, 8, square, width)
    count = float(rows)
    levels = len(gather.grid.digits)
    for level in range(levels):
        size = gather.grid.digits[level][1]
        gather.start(level, slot)
        gather.wait(level, slot)
        buffer = gather.buffers[level].at[slot]
        means = [buffer[g, 0:8, :] for g in range(size)]
        merged = sum(means[1:], means[0]) * (1.0 / size)
        spread = sum([buffer[g, 8:16, :] for g in range(1, size)], buffer[0, 8:16, :])
        between = sum([(m - merged) * (m - merged) for m in means[1:]], (means[0] - merged) * (means[0] - merged))
        spread = spread + count * between
        count = count * size
        if level + 1 < levels:
            own = gather.own(level + 1, slot)
            own[0:8, :] = merged
            own[8:16, :] = spread
    inv = lax.rsqrt(spread * (1.0 / count) + NORM_EPSILON)
    mean = take_row(merged, 0, width)
    inv = take_row(inv, 0, width)
    inv_out[...] = inv

    def write(r, c):
        nrm = (pre[r, :] - mean) * inv
        nrm_out[r, :] = nrm
        value = gain_row * nrm + shift_row
        act_out[r, :] = (value * jax.nn.sigmoid(value)).astype(BF16)
        return c

    row_loop(rows, write, 0)


def nt(left, right):
    return lax.dot_general(left, right, (((1,), (1,)), ((), ())), preferred_element_type=F32)


def nn(left, right):
    return lax.dot_general(left, right, (((1,), (0,)), ((), ())), preferred_element_type=F32)


def tn(left, right):
    return lax.dot_general(left, right, (((0,), (0,)), ((), ())), preferred_element_type=F32)


def exact(left, right, dims):
    return lax.dot_general(
        left, right, (dims, ((), ())), precision=lax.Precision.HIGHEST, preferred_element_type=F32
    )


def windows(width):
    return [(s, min(WIN, width - s)) for s in range(0, width, WIN)]


def part_of(full, tail, i):
    return full.at[i] if i < full.shape[0] else tail


def forward_kernel(
    grid,
    table_ref,
    mask_ref,
    x_hbm,
    w1_hbm,
    noise_ref,
    gid_ref,
    w2_ref,
    head_ref,
    headb_ref,
    d1_ref,
    d2_ref,
    gain_ref,
    shift_ref,
    nrm0,
    nrm1,
    nrm2,
    nrm3,
    inv_out,
    act1,
    act2,
    zlat,
    act3,
    act4,
    head_out,
    ggroup_out,
    offsets_out,
    x_win,
    x_tail,
    w_win,
    w_tail,
    pre,
    moments,
    *rest,
):
    levels = len(grid.digits)
    small = rest[:levels]
    wide = rest[levels : 2 * levels]
    s_send, s_recv, g_send, g_recv = (
        rest[2 * levels : 3 * levels],
        rest[3 * levels : 4 * levels],
        rest[4 * levels : 5 * levels],
        rest[5 * levels : 6 * levels],
    )
    in_sems = rest[6 * levels]
    gather = Gather(grid, small, s_send, s_recv)
    group_gather = Gather(grid, wide, g_send, g_recv)
    latent = d1_ref.shape[0]
    genes = x_hbm.shape[1]
    spans = windows(genes)

    loads = []
    for i, (s, size) in enumerate(spans):
        a = pltpu.make_async_copy(x_hbm.at[:, pl.ds(s, size)], part_of(x_win, x_tail, i), in_sems.at[0, i])
        b = pltpu.make_async_copy(w1_hbm.at[:, pl.ds(s, size)], part_of(w_win, w_tail, i), in_sems.at[1, i])
        a.start()
        b.start()
        loads.append((a, b))
    entry_barrier(grid, digit_peers(grid))

    for i, (s, size) in enumerate(spans):
        loads[i][0].wait()
        loads[i][1].wait()
        part = nt(part_of(x_win, x_tail, i)[...], part_of(w_win, w_tail, i)[...])
        pre[...] = part if i == 0 else pre[...] + part

    def norm(k, nrm, act):
        batch_norm(
            pre, nrm, act, gather, k, gain_ref[k : k + 1, :], shift_ref[k : k + 1, :], inv_out.at[k : k + 1, :]
        )

    norm(0, nrm0, act1)
    pre[...] = nn(act1[...], w2_ref[...])
    norm(1, nrm1, act2)
    head = nt(act2[...], head_ref[...]) + headb_ref[...]
    head_out[...] = head
    mu = head[:, 0:latent]
    logvar = head[:, latent : 2 * latent]
    zlat[...] = (mu + jnp.exp(0.5 * logvar) * noise_ref[...]).astype(BF16)

    groups = ggroup_out.shape[0]
    pops = groups // 2
    cells_here = gid_ref.shape[1]
    member = (lax.broadcasted_iota(jnp.int32, (groups, cells_here), 0) == gid_ref[...]).astype(F32)
    own = group_gather.own(0, 0)
    own[:, 0:latent] = exact(member, mu, ((1,), (0,)))
    own[:, latent : latent + 1] = jnp.sum(member, axis=1, keepdims=True)
    group_gather.start(0, 0)

    pre[...] = nn(zlat[...], d1_ref[...])
    norm(2, nrm2, act3)
    for level in range(levels):
        group_gather.wait(level, 0)
        size = grid.digits[level][1]
        buffer = wide[level].at[0]
        total = sum([buffer[g] for g in range(1, size)], buffer[0])
        if level + 1 < levels:
            group_gather.own(level + 1, 0)[...] = total
            group_gather.start(level + 1, 0)
        if level == 0:
            pre[...] = nn(act3[...], d2_ref[...])
            norm(3, nrm3, act4)
    counted = jnp.maximum(total[:, latent : latent + 1], 1.0)
    moments[...] = total / counted
    odd, even = pl.ds(1, pops, stride=2), pl.ds(0, pops, stride=2)
    offset = moments[odd, :] - moments[even, :]
    centre = jnp.sum(offset, axis=0, keepdims=True) * (1.0 / pops)
    grad_offset = (2.0 * OFFSET_WEIGHT / pops) * (offset - centre)
    row = lax.axis_index("cells")
    slots = offsets_out.shape[0]
    lane = lax.broadcasted_iota(jnp.int32, (1, pops), 1)
    picks = jnp.concatenate(
        [jnp.where(lane == table_ref[row, s], mask_ref[row, s].astype(F32), 0.0) for s in range(slots)], axis=0
    )
    offsets_out[...] = exact(picks, offset, ((1,), (0,)))[:, 0:latent]
    moments[odd, :] = grad_offset
    moments[even, :] = -grad_offset
    ggroup_out[...] = moments[...] / counted

    for level in range(levels):
        for k in range(4):
            gather.finish(level, k)
        group_gather.finish(level, 0)


def call_forward(grid, cells_x, w1t, noise, gid, table, mask, w2, headt, headb, d1, d2, gain, shift):
    rows, genes = cells_x.shape
    hidden = w2.shape[0]
    latent = d1.shape[0]
    groups = 2 * POP_DEV * grid.cells
    count = len(windows(genes))
    levels = len(grid.digits)
    vm = pl.BlockSpec(memory_space=pltpu.VMEM)
    hbm = pl.BlockSpec(memory_space=pl.ANY)
    sm = pl.BlockSpec(memory_space=pltpu.SMEM)
    wide_f = jax.ShapeDtypeStruct((rows, hidden), F32)
    wide_b = jax.ShapeDtypeStruct((rows, hidden), BF16)
    out_shape = (
        wide_f,
        wide_f,
        wide_f,
        wide_f,
        jax.ShapeDtypeStruct((4, hidden), F32),
        wide_b,
        wide_b,
        jax.ShapeDtypeStruct((rows, latent), BF16),
        wide_b,
        wide_b,
        jax.ShapeDtypeStruct((rows, 2 * latent), F32),
        jax.ShapeDtypeStruct((groups, 128), F32),
        jax.ShapeDtypeStruct((table.shape[1], latent), F32),
    )
    scratch = (
        [
            pltpu.VMEM((count - 1, rows, WIN), BF16),
            pltpu.VMEM((rows, genes - (count - 1) * WIN), BF16),
            pltpu.VMEM((count - 1, hidden, WIN), BF16),
            pltpu.VMEM((hidden, genes - (count - 1) * WIN), BF16),
            pltpu.VMEM((rows, hidden), F32),
            pltpu.VMEM((groups, 128), F32),
        ]
        + [pltpu.VMEM((4, size, 16, 128), F32) for _, size in grid.digits]
        + [pltpu.VMEM((1, size, groups, 128), F32) for _, size in grid.digits]
        + [pltpu.SemaphoreType.DMA((4, size - 1)) for _, size in grid.digits]
        + [pltpu.SemaphoreType.DMA((4, size - 1)) for _, size in grid.digits]
        + [pltpu.SemaphoreType.DMA((1, size - 1)) for _, size in grid.digits]
        + [pltpu.SemaphoreType.DMA((1, size - 1)) for _, size in grid.digits]
        + [pltpu.SemaphoreType.DMA((2, count))]
    )
    return pl.pallas_call(
        functools.partial(forward_kernel, grid),
        out_shape=out_shape,
        in_specs=[sm, sm, hbm, hbm] + [vm] * 9,
        out_specs=[vm] * len(out_shape),
        scratch_shapes=scratch,
        name="forward",
        compiler_params=pltpu.CompilerParams(
            collective_id=0, has_side_effects=True, vmem_limit_bytes=60 * 2**20
        ),
    )(table, mask, cells_x, w1t, noise, gid, w2, headt, headb, d1, d2, gain, shift)


ORDERS = ((0, 1, 2, 3, 4), (0, 2, 1, 3, 4), (0, 1, 3, 4, 2), (0, 2, 3, 4, 1))
CHANNELS = len(ORDERS)
PARTS = 32
STAGES = 5
SLOT_ROWS = 200


class Scatter:
    def __init__(self, grid, total, stage, low, landing, stage_sems, send_sems, recv_sems, credits):
        self.grid, self.total = grid, total
        self.stage, self.low, self.landing = stage, low, landing
        self.stage_sems, self.send_sems, self.recv_sems, self.credits = stage_sems, send_sems, recv_sems, credits
        self.shift = grid.bits - STAGES
        self.rows = {}

    def bit(self, b):
        return (self.grid.me() // (1 << (b + self.shift))) % 2

    def partner(self, b):
        return self.grid.place(self.grid.me() + (1 - 2 * self.bit(b)) * (1 << (b + self.shift)))

    def part(self, channel, k):
        out = 0
        for t, b in enumerate(ORDERS[channel]):
            own = self.bit(b)
            out = out + (1 << b) * ((1 - own) if (k >> (STAGES - 1 - t)) & 1 else own)
        return out

    def send(self, q, t):
        channel, rows = q % CHANNELS, self.rows[q]
        size = (16 >> t) * rows
        if t == 0:
            source, sem = self.stage.at[q % 2, 0:size], self.stage_sems.at[q % 2]
        else:
            source, sem = self.landing[t - 1].at[channel, size : 2 * size], self.send_sems.at[channel, t]
        return pltpu.make_async_remote_copy(
            src_ref=source,
            dst_ref=self.landing[t].at[channel, 0:size],
            send_sem=sem,
            recv_sem=self.recv_sems.at[channel, t],
            device_id=self.partner(ORDERS[channel][t]),
            device_id_type=MESH_ID,
        )

    def start(self, q, t):
        if q >= CHANNELS:
            pl.semaphore_wait(self.credits.at[q % CHANNELS, t], 1)
        self.send(q, t).start()

    def free(self, q, t):
        if q + CHANNELS < self.total:
            channel = q % CHANNELS
            pl.semaphore_signal(
                self.credits.at[channel, t],
                inc=1,
                device_id=self.partner(ORDERS[channel][t]),
                device_id_type=MESH_ID,
            )

    def upper(self, q, rows, fill):
        self.rows[q] = rows
        if q >= 2:
            self.send(q - 2, 0).wait_send()
        fill(self.stage.at[q % 2], True)
        self.start(q, 0)

    def lower(self, q, fill):
        channel, rows = q % CHANNELS, self.rows[q]
        fill(self.low, False)
        self.send(q, 0).wait_recv()
        mine = self.landing[0].at[channel]

        def add(i, c):
            r = pl.ds(pl.multiple_of(i * rows, 8), rows)
            mine[r, :] += self.low[r, :]
            return c

        lax.fori_loop(0, 16, add, 0)
        self.start(q, 1)

    def fold(self, q, t):
        channel, rows = q % CHANNELS, self.rows[q]
        self.send(q, t).wait_recv()
        mine, before = self.landing[t].at[channel], self.landing[t - 1].at[channel]

        def add(i, c):
            r = pl.ds(pl.multiple_of(i * rows, 8), rows)
            mine[r, :] += before[r, :]
            return c

        lax.fori_loop(0, 16 >> t, add, 0)
        self.send(q, t).wait_send()
        self.free(q, t - 1)
        self.start(q, t + 1)

    def last(self, q, done):
        channel, rows = q % CHANNELS, self.rows[q]
        t = STAGES - 1
        self.send(q, t).wait_recv()
        done(self.landing[t][channel, 0:rows, :] + self.landing[t - 1][channel, 0:rows, :])
        self.send(q, t).wait_send()
        self.free(q, t - 1)
        self.free(q, t)


class Spread:
    def __init__(self, scatter, block, landing, whole, sems):
        self.scatter, self.block, self.landing, self.whole, self.sems = scatter, block, landing, whole, sems
        self.rows = block.shape[0]

    def begin(self, t):
        out = 0
        for i in range(t):
            out = out + self.scatter.bit(i) * (self.rows >> (i + 1))
        return out

    def halving(self, t):
        size = self.rows >> (t + 1)
        at = self.begin(t) + (1 - self.scatter.bit(t)) * size
        return pltpu.make_async_remote_copy(
            src_ref=self.block.at[pl.ds(pl.multiple_of(at, 8), size)],
            dst_ref=self.landing[t],
            send_sem=self.sems.at[0, t],
            recv_sem=self.sems.at[1, t],
            device_id=self.scatter.partner(t),
            device_id_type=MESH_ID,
        )

    def doubling(self, t, arriving=False):
        size = self.rows >> (t + 1)
        at = self.begin(t + 1)
        there = self.begin(t) + (1 - self.scatter.bit(t)) * size if arriving else at
        return pltpu.make_async_remote_copy(
            src_ref=self.whole.at[pl.ds(pl.multiple_of(at, 8), size)],
            dst_ref=self.whole.at[pl.ds(pl.multiple_of(there, 8), size)],
            send_sem=self.sems.at[2, t],
            recv_sem=self.sems.at[3, t],
            device_id=self.scatter.partner(t),
            device_id_type=MESH_ID,
        )

    def step(self, i):
        if i == 0:
            self.halving(0).start()
        elif i <= STAGES:
            t = i - 1
            self.halving(t).wait_recv()
            size = self.rows >> (t + 1)
            r = pl.ds(pl.multiple_of(self.begin(t + 1), 8), size)
            target = self.whole if i == STAGES else self.block
            target[r, :] = self.block[r, :] + self.landing[t][...]
            self.halving(t).wait_send()
            if i < STAGES:
                self.halving(t + 1).start()
            else:
                self.doubling(t).start()
        else:
            t = 2 * STAGES - i
            self.doubling(t, True).wait_recv()
            self.doubling(t).wait_send()
            if t > 0:
                self.doubling(t - 1).start()


def one_hot(rows, target):
    lane = lax.broadcasted_iota(jnp.int32, (rows, target.shape[1]), 0)
    return jnp.where(lane == target, 1.0, 0.0).astype(BF16)


def column_parts(width, size):
    column = lax.broadcasted_iota(jnp.int32, (1, width), 1)
    part = jnp.zeros((1, width), jnp.int32)
    for m in range(1, width // size):
        part = part + jnp.where(column >= m * size, 1, 0)
    return column, part


def slot_of(scatter, channel, bits, parts, part):
    order = [b for b in ORDERS[channel] if b in bits]
    slot = jnp.zeros_like(part)
    for value in range(parts):
        at = 0
        for t, b in enumerate(order):
            own = scatter.bit(b)
            weight = 1 << (len(order) - 1 - t)
            at = at + weight * ((1 - own) if (value >> bits.index(b)) & 1 else own)
        slot = jnp.where(part == value, at, slot)
    return slot


def sum_blocks(gather, slot, idle):
    levels = len(gather.grid.digits)
    for level in range(levels):
        gather.start(level, slot)
        if level < len(idle):
            idle[level]()
        gather.wait(level, slot)
        size = gather.grid.digits[level][1]
        buffer = gather.buffers[level].at[slot]
        total = sum([buffer[g] for g in range(1, size)], buffer[0])
        if level + 1 < levels:
            gather.own(level + 1, slot)[...] = total
    return total


def norm_gradient(grad, nrm, out, gather, slot, gain_row, shift_row, inv_row, scale, gain_out, shift_out, idle):
    rows, width = grad.shape

    def gate(r, carry):
        n = nrm[r, :]
        value = gain_row * n + shift_row
        sig = jax.nn.sigmoid(value)
        g = grad[r, :] * sig * (1.0 + value * (1.0 - sig))
        grad[r, :] = g
        return carry[0] + column_sum(g), carry[1] + column_sum(g * n)

    zero = jnp.zeros((1, width), F32)
    shift_sum, gain_sum = row_loop(rows, gate, (zero, zero))
    own = gather.own(0, slot)
    put_row(own, 0, shift_sum, width)
    put_row(own, 8, gain_sum, width)
    total = sum_blocks(gather, slot, idle)
    shift_sum = take_row(total, 0, width)
    gain_sum = take_row(total, 8, width)
    shift_out[...] = shift_sum
    gain_out[...] = gain_sum
    factor = gain_row * inv_row
    shift_mean = shift_sum * scale
    gain_mean = gain_sum * scale

    def write(r, c):
        out[r, :] = (factor * (grad[r, :] - shift_mean - nrm[r, :] * gain_mean)).astype(BF16)
        return c

    row_loop(rows, write, 0)


D1_ROWS = 104
REP_ROWS = 2304


def backward_kernel(
    grid,
    latent,
    x_hbm,
    outw_hbm,
    nrm_hbm0,
    nrm_hbm1,
    nrm_hbm2,
    nrm_hbm3,
    act1_hbm,
    act2_hbm,
    act3_hbm,
    act4_ref,
    zlat_ref,
    head_ref_in,
    noise_ref,
    gid_ref,
    ggroup_ref,
    inv_ref,
    outb_ref,
    w2_ref,
    head_ref,
    d1_ref,
    d2_ref,
    gain_ref,
    shift_ref,
    g_out,
    gpre1,
    out25,
    enc_part,
    nar_part,
    d1_out,
    headw_out,
    outb_out,
    headb_out,
    gain_out,
    shift_out,
    *rest,
):
    levels = len(grid.digits)
    rest = list(rest)

    def take(n):
        got = rest[:n]
        del rest[:n]
        return got

    small, s_send, s_recv = take(levels), take(levels), take(levels)
    stage, low, *landing = take(2 + STAGES)
    stage_sems, send_sems, recv_sems, credits = take(4)
    rep_block, rep_whole, *rep_landing = take(2 + STAGES)
    (rep_sems,) = take(1)
    g_win, wide, gact, gpre4, gpre3, gpre2, ghead, gcell, lhs, nrm_buf, fin = take(11)
    picked = lhs.at[0:512]
    in_sems, g_sems, nrm_sems, x_sems, act_sems = take(5)

    rows, genes = x_hbm.shape
    hidden = w2_ref.shape[0]
    spans = windows(genes)
    count = len(spans)
    cell_total = float(rows * grid.n)
    total = 2 * count + 2
    gather = Gather(grid, small, s_send, s_recv)
    scatter = Scatter(grid, total, stage, low, landing, stage_sems, send_sems, recv_sems, credits)
    spread = Spread(scatter, rep_block, rep_landing, rep_whole, rep_sems)
    rep_outb = 7 * (D1_ROWS + 2 * latent)
    rep_headb = rep_outb + 8 * count

    entry_barrier(grid, digit_peers(grid))
    nrm_loads = {
        k: pltpu.make_async_copy(ref, nrm_buf.at[(k + 1) % 2], nrm_sems.at[k])
        for k, ref in enumerate((nrm_hbm0, nrm_hbm1, nrm_hbm2, nrm_hbm3))
    }
    nrm_loads[3].start()
    nrm_loads[2].start()


    def out_fill(s):
        buffer = g_win.at[s % 3]

        def fill(target, is_upper):
            first = hidden // 2 if is_upper else 0
            part = nn(lhs[first : first + hidden // 2, :], buffer[...])
            for c in range(WIN // 128):
                target[pl.ds(c, hidden // 2, stride=8), :] = part[:, 128 * c : 128 * (c + 1)]

        return fill

    def out_lhs(q):
        column, part = column_parts(hidden, hidden // PARTS)
        slot = slot_of(scatter, q % CHANNELS, (0, 1, 2, 3, 4), PARTS, part)
        target = column + (hidden // PARTS) * (slot - part)
        block = hidden // 5

        def some(i, c):
            at = pl.multiple_of(i * block, block)
            lhs[pl.ds(at, block), :] = nt(one_hot(block, target - at), act4_ref[...]).astype(BF16)
            return c

        lax.fori_loop(0, 5, some, 0)

    def out_piece(s):
        out_lhs(s)
        made(s, SLOT_ROWS, out_fill(s))

    done = {}
    state = {}

    def reach(q, t):
        while q in state and state[q] <= t:
            stage_now = state[q]
            if stage_now < STAGES - 1:
                reach(q - CHANNELS, min(stage_now + 2, STAGES - 1))
                scatter.fold(q, stage_now)
            else:
                scatter.last(q, done[q])
            state[q] = stage_now + 1

    def fold(q, t):
        reach(q, t)

    def made(q, rows_here, fill):
        reach(q - CHANNELS, 1)
        scatter.upper(q, rows_here, fill)
        reach(q - CHANNELS, 2)
        scatter.lower(q, fill)
        state[q] = 1

    def out_done(s):
        def done(value):
            fin[...] = value
            for c in range(WIN // 128):
                out25[:, WIN * s + 128 * c : WIN * s + 128 * (c + 1)] = fin[pl.ds(c, hidden // PARTS, stride=8), :]

        return done

    for s in range(count):
        done[s] = out_done(s)

    def output_layer(w_ring, w_tail, x_ring, x_tail):
        def load(s):
            at, size = spans[s]
            tail = s == count - 1
            return (
                pltpu.make_async_copy(
                    outw_hbm.at[:, pl.ds(at, size)], w_tail if tail else w_ring.at[s % 3], in_sems.at[0, s]
                ),
                pltpu.make_async_copy(
                    x_hbm.at[:, pl.ds(at, size)], x_tail if tail else x_ring.at[s % 2], in_sems.at[1, s]
                ),
            )

        def save(s):
            return pltpu.make_async_copy(g_win.at[s % 3], g_out.at[:, pl.ds(WIN * s, WIN)], g_sems.at[s])

        for s in range(2):
            for copy in load(s):
                copy.start()
        for s, (at, size) in enumerate(spans):
            tail = s == count - 1
            w = w_tail if tail else w_ring.at[s % 3]
            x = x_tail if tail else x_ring.at[s % 2]
            for copy in load(s):
                copy.wait()
            wide[:, 0:size] = nn(act4_ref[...], w[...])
            bias = outb_ref[:, at : at + size]
            if s >= 3:
                save(s - 3).wait()
            g = g_win.at[s % 3]

            def residual(r, c):
                value = wide[r, 0:size] + bias - x[r, :].astype(F32)
                value = (value * (2.0 / cell_total)).astype(BF16)
                g[r, 0:size] = value
                return c + column_sum(value.astype(F32))

            put_row(rep_block, rep_outb + 8 * s, row_loop(rows, residual, jnp.zeros((1, size), F32)), size)
            if size < WIN:
                g[:, size:WIN] = jnp.zeros((rows, WIN - size), BF16)
            save(s).start()
            if s + 2 < count:
                for copy in load(s + 2):
                    copy.start()
            if s < CHANNELS:
                out_piece(s)
            part = nt(g[:, 0:size], w[...])
            gact[...] = part if s == 0 else gact[...] + part
            if s == count - 2:
                fold(0, 1)
        for s in range(count - 3, count):
            save(s).wait()

    pl.run_scoped(
        output_layer,
        pltpu.VMEM((3, hidden, WIN), BF16),
        pltpu.VMEM((hidden, spans[-1][1]), BF16),
        pltpu.VMEM((2, rows, WIN), BF16),
        pltpu.VMEM((rows, spans[-1][1]), BF16),
    )


    def pack(target, at, source, row, height):
        full = hidden // 128
        for c in range(full):
            target[pl.ds(pl.multiple_of(at + height * c, 8), height), :] = source[
                pl.ds(row, height), 128 * c : 128 * (c + 1)
            ]
        rest_width = hidden - 128 * full
        pieces = [source[pl.ds(row + 8 * i, 8), 128 * full : hidden] for i in range(height // 8)]
        target[pl.ds(pl.multiple_of(at + height * full, 8), 8), 0 : rest_width * len(pieces)] = jnp.concatenate(
            pieces, axis=1
        )

    def unpack(value, out, row, height):
        full = hidden // 128
        rest_width = hidden - 128 * full
        for c in range(full):
            out[row : row + height, 128 * c : 128 * (c + 1)] = value[height * c : height * (c + 1), :]
        for i in range(height // 8):
            out[row + 8 * i : row + 8 * i + 8, 128 * full : hidden] = value[
                height * full : height * full + 8, rest_width * i : rest_width * (i + 1)
            ]

    def finish(xt, x_part, x_last, act_buf):
        window = x_part.shape[2]
        height = xt.shape[1]
        starts = [(genes * j) // PARTS for j in range(PARTS)]

        def x_place(j):
            at = starts[j] // 128 * 128
            return (at, window) if at + window <= genes else (at, genes - at)

        def x_load(j):
            at, size = x_place(j)
            target = x_part.at[j % 3] if size == window else x_last
            return pltpu.make_async_copy(x_hbm.at[:, pl.ds(at, size)], target, x_sems.at[j])

        def transpose(j):
            x_load(j).wait()
            at, size = x_place(j)
            source = x_part.at[j % 3] if size == window else x_last
            lane = lax.broadcasted_iota(jnp.int32, (height, size), 1)
            line = lax.broadcasted_iota(jnp.int32, (height, size), 0)
            select = jnp.where(lane == line + (starts[j] - at), 1.0, 0.0).astype(BF16)
            xt[j] = nt(select, source[...]).astype(BF16)
            if j + 3 < PARTS:
                x_load(j + 3).start()

        def transposes(first, number):
            def run():
                for j in range(first, first + number):
                    transpose(j)

            return run

        def enc_fill(q, s):
            def fill(target, is_upper):
                for i in range(16):
                    j = scatter.part(q % CHANNELS, 16 + i if is_upper else i)
                    picked[32 * i : 32 * i + 32, :] = xt[j, 32 * s : 32 * s + 32, :]
                wide[0:512, 0:hidden] = nn(picked[...], gpre1[...])

                def one(i, c):
                    pack(target, i * SLOT_ROWS, wide, pl.multiple_of(i * 32, 32), 32)
                    return c

                lax.fori_loop(0, 16, one, 0)

            return fill

        def enc_piece(q, s):
            made(q, SLOT_ROWS, enc_fill(q, s))

        def enc_done(s):
            return lambda value: unpack(value, enc_part, 32 * s, 32)

        each = 2 * hidden // PARTS
        skip = (0, 32)

        def nar_fill(q, which):
            height_here = 32 if which == 0 else 24
            rows_here = 25 * 8 if which == 0 else 19 * 8
            channel = q % CHANNELS
            place = STAGES - 1 - ORDERS[channel].index(4)

            def fill(target, is_upper):
                column, part = column_parts(hidden, each)
                slot = slot_of(scatter, channel, (0, 1, 2, 3), PARTS // 2, part)
                line = column - each * part - skip[which]
                inside = (line >= 0) & (line < height_here)
                base = 8 if is_upper else 0
                place_in = jnp.where(inside, (slot - base) * height_here + line, -1)
                place_in = jnp.where((slot >= base) & (slot < base + 8), place_in, -1)
                select = one_hot(8 * height_here, place_in)
                for matrix, act_slot, grad in ((0, 0, gpre2), (1, 1, gpre4)):
                    size = 8 * height_here
                    picked[0:size, :] = nt(select, act_buf[act_slot]).astype(BF16)
                    wide[0:size, 0:hidden] = nn(picked[0:size, :], grad[...])
                    flip = scatter.bit(4) if matrix == 0 else 1 - scatter.bit(4)
                    for i in range(8):
                        k = (i >> place) * (2 << place) + (i & ((1 << place) - 1)) + flip * (1 << place)
                        pack(target, k * rows_here, wide, i * height_here, height_here)

            return rows_here, fill

        def nar_piece(q, which):
            rows_here, fill = nar_fill(q, which)
            made(q, rows_here, fill)

        def nar_done(which):
            if which == 0:
                return lambda value: unpack(value, nar_part, 0, 32)
            return lambda value: unpack(value, nar_part, 32, 24)

        first = count
        done[first] = nar_done(0)
        done[first + 1] = nar_done(1)
        for s in range(count):
            done[first + 2 + s] = enc_done(s)

        def row(ref, k):
            return ref[k : k + 1, :]

        def back(k, grad, out, idle):
            nrm_loads[k].wait()
            norm_gradient(
                grad,
                nrm_buf.at[(k + 1) % 2],
                out,
                gather,
                k,
                row(gain_ref, k),
                row(shift_ref, k),
                row(inv_ref, k),
                1.0 / cell_total,
                gain_out.at[k : k + 1, :],
                shift_out.at[k : k + 1, :],
                idle,
            )

        act_loads = [
            pltpu.make_async_copy(ref, act_buf.at[at], act_sems.at[i])
            for i, (ref, at) in enumerate(((act1_hbm, 0), (act3_hbm, 1), (act2_hbm, 0)))
        ]
        act_loads[1].start()
        act_loads[2].start()
        for j in range(3):
            x_load(j).start()

        groups = ggroup_ref.shape[0]
        member = (lax.broadcasted_iota(jnp.int32, (groups, rows), 0) == gid_ref[...]).astype(F32)
        gcell[...] = exact(member, ggroup_ref[...], ((0,), (0,)))

        back(3, gact, gpre4, [transposes(0, 4), transposes(4, 4)])
        nrm_loads[1].start()
        gact[...] = nt(gpre4[...], d2_ref[...])
        fold(1, 1)
        back(2, gact, gpre3, [transposes(8, 4), transposes(12, 4)])
        nrm_loads[0].start()
        grad_z = nt(gpre3[...], d1_ref[...])
        mu = head_ref_in[:, 0:latent]
        logvar = head_ref_in[:, latent : 2 * latent]
        kl = KL_WEIGHT * genes / cell_total
        deviation = jnp.exp(0.5 * logvar)
        grad_mu = grad_z + kl * mu + gcell[:, 0:latent]
        grad_logvar = grad_z * noise_ref[...] * (0.5 * deviation) + 0.5 * kl * (jnp.exp(logvar) - 1.0)
        ghead[...] = jnp.concatenate([grad_mu, grad_logvar], axis=1).astype(BF16)
        gact[...] = nn(ghead[...], head_ref[...])
        fold(0, 2)
        out_piece(4)
        fold(2, 1)

        def latent_side():
            act_loads[2].wait()
            d1_grad = tn(zlat_ref[...], gpre3[...])
            headw_grad = tn(ghead[...], act_buf[0])
            act_loads[0].start()
            for c in range(-(-hidden // 128)):
                size = min(128, hidden - 128 * c)
                at = D1_ROWS * c
                rep_block[at : at + latent, 0:size] = d1_grad[:, 128 * c : 128 * c + size]
                at = 7 * D1_ROWS + 2 * latent * c
                rep_block[at : at + 2 * latent, 0:size] = headw_grad[:, 128 * c : 128 * c + size]
            put_row(rep_block, rep_headb, column_sum(ghead[...].astype(F32)), 2 * latent)
            spread.step(0)

        back(1, gact, gpre2, [transposes(16, 4), transposes(20, 4)])
        gact[...] = nt(gpre2[...], w2_ref[...])
        latent_side()
        fold(1, 2)
        out_piece(5)
        fold(3, 1)
        back(0, gact, gpre1, [transposes(24, 4), transposes(28, 4)])
        fold(0, 3)
        fold(2, 2)
        out_piece(6)
        for copy in act_loads[:2]:
            copy.wait()

        steps = list(range(1, 2 * STAGES + 1))
        for q in range(count, total):
            if q < first + 2:
                nar_piece(q, q - first)
            else:
                enc_piece(q, q - first - 2)
            for lag, t in ((3, 1), (4, 2), (5, 3), (6, 4)):
                if q - lag >= 0:
                    fold(q - lag, t)
            if steps:
                spread.step(steps.pop(0))
        for q in range(total, total + 6):
            for lag, t in ((6, 4), (5, 3), (4, 2), (3, 1)):
                if 0 <= q - lag < total:
                    fold(q - lag, t)
            if steps:
                spread.step(steps.pop(0))
        for i in steps:
            spread.step(i)
        for q in (total - 2, total - 1):
            scatter.send(q, 0).wait_send()
        for c in range(-(-hidden // 128)):
            size = min(128, hidden - 128 * c)
            at = D1_ROWS * c
            d1_out[:, 128 * c : 128 * c + size] = rep_whole[at : at + latent, 0:size]
            at = 7 * D1_ROWS + 2 * latent * c
            headw_out[:, 128 * c : 128 * c + size] = rep_whole[at : at + 2 * latent, 0:size]
        outb_out[...] = rep_whole[rep_outb : rep_outb + 8 * count, :]
        headb_out[...] = rep_whole[rep_headb : rep_headb + 8, :]
        for level in range(levels):
            for k in range(4):
                gather.finish(level, k)

    last = genes - (genes * (PARTS - 1)) // PARTS // 128 * 128
    pl.run_scoped(
        finish,
        pltpu.VMEM((PARTS, 224, rows), BF16),
        pltpu.VMEM((3, rows, 384), BF16),
        pltpu.VMEM((rows, last), BF16),
        pltpu.VMEM((2, rows, hidden), BF16),
    )


def call_backward(grid, kept, cells_x, out_w, noise, gid, out_b, w2, headt, d1, d2, gain, shift):
    (nrm0, nrm1, nrm2, nrm3, inv, act1, act2, zlat, act3, act4, head, ggroup) = kept
    rows, genes = cells_x.shape
    hidden, latent = w2.shape[0], d1.shape[0]
    spans = windows(genes)
    count = len(spans)
    vm = pl.BlockSpec(memory_space=pltpu.VMEM)
    hbm = pl.BlockSpec(memory_space=pl.ANY)
    shape = jax.ShapeDtypeStruct
    out_shape = (
        shape((rows, WIN * count), BF16),
        shape((rows, hidden), BF16),
        shape((hidden // PARTS, WIN * count), F32),
        shape((32 * count, hidden), F32),
        shape((56, hidden), F32),
        shape((latent, hidden), F32),
        shape((2 * latent, hidden), F32),
        shape((8 * count, 128), F32),
        shape((8, 128), F32),
        shape((4, hidden), F32),
        shape((4, hidden), F32),
    )
    dma = pltpu.SemaphoreType.DMA
    scratch = (
        [pltpu.VMEM((4, size, 16, 128), F32) for _, size in grid.digits]
        + [dma((4, size - 1)) for _, size in grid.digits]
        + [dma((4, size - 1)) for _, size in grid.digits]
        + [pltpu.VMEM((2, 16 * SLOT_ROWS, 128), F32), pltpu.VMEM((16 * SLOT_ROWS, 128), F32)]
        + [pltpu.VMEM((CHANNELS, (16 >> t) * SLOT_ROWS, 128), F32) for t in range(STAGES)]
        + [dma((2,)), dma((CHANNELS, STAGES)), dma((CHANNELS, STAGES)), pltpu.SemaphoreType.REGULAR((CHANNELS, STAGES))]
        + [pltpu.VMEM((REP_ROWS, 128), F32), pltpu.VMEM((REP_ROWS, 128), F32)]
        + [pltpu.VMEM((REP_ROWS >> (t + 1), 128), F32) for t in range(STAGES)]
        + [dma((4, STAGES))]
        + [
            pltpu.VMEM((3, rows, WIN), BF16),
            pltpu.VMEM((rows, WIN), F32),
            pltpu.VMEM((rows, hidden), F32),
            pltpu.VMEM((rows, hidden), BF16),
            pltpu.VMEM((rows, hidden), BF16),
            pltpu.VMEM((rows, hidden), BF16),
            pltpu.VMEM((rows, 2 * latent), BF16),
            pltpu.VMEM((rows, 128), F32),
            pltpu.VMEM((hidden, rows), BF16),
            pltpu.VMEM((2, rows, hidden), F32),
            pltpu.VMEM((SLOT_ROWS, 128), F32),
        ]
        + [dma((2, count)), dma((count,)), dma((4,)), dma((PARTS,)), dma((3,))]
    )
    return pl.pallas_call(
        functools.partial(backward_kernel, grid, latent),
        out_shape=out_shape,
        in_specs=[hbm] * 9 + [vm] * 14,
        out_specs=[hbm] + [vm] * (len(out_shape) - 1),
        scratch_shapes=scratch,
        name="backward",
        compiler_params=pltpu.CompilerParams(
            collective_id=1, has_side_effects=True, vmem_limit_bytes=62 * 2**20
        ),
    )(
        cells_x,
        out_w,
        nrm0,
        nrm1,
        nrm2,
        nrm3,
        act1,
        act2,
        act3,
        act4,
        zlat,
        head,
        noise,
        gid,
        ggroup,
        inv,
        out_b,
        w2,
        headt,
        d1,
        d2,
        gain,
        shift,
    )


def flat_shard(grid, flat, columns, rows_in_all):
    value = flat.reshape(rows_in_all // PARTS, columns)
    size = grid.n // PARTS
    if size > 1:
        groups = [list(range(size * p, size * p + size)) for p in range(PARTS)]
        value = lax.psum_scatter(
            value, ("cells", "rep"), scatter_dimension=0, axis_index_groups=groups, tiled=True
        )
    return value


def group_sum(grid, values):
    size = grid.n // PARTS
    if size > 1:
        groups = [list(range(size * p, size * p + size)) for p in range(PARTS)]
        values = lax.psum(values, ("cells", "rep"), axis_index_groups=groups)
    return values


def shards(
    grid,
    cells_x,
    latent_noise,
    group_ids,
    owner_table,
    owner_mask,
    enc_w1,
    enc_w2,
    head_w,
    head_b,
    dec_w1,
    dec_w2,
    out_w,
    out_b,
    bn_gain,
    bn_shift,
):
    cell_total = float(cells_x.shape[0] * grid.n)
    genes = cells_x.shape[1]
    hidden = enc_w2.shape[0]
    gid = group_ids.reshape(1, -1)
    headt = head_w.T
    *kept, offsets = call_forward(
        grid,
        cells_x,
        enc_w1.T,
        latent_noise,
        gid,
        owner_table,
        owner_mask,
        enc_w2,
        headt,
        head_b.reshape(1, -1),
        dec_w1,
        dec_w2,
        bn_gain,
        bn_shift,
    )
    g, gpre1, out25, enc_part, nar_part, d1_grad, headw_grad, outb_grad, headb_grad, grad_gain, grad_shift = call_backward(
        grid,
        kept,
        cells_x,
        out_w,
        latent_noise,
        gid,
        out_b.reshape(1, -1),
        enc_w2,
        headt,
        dec_w1,
        dec_w2,
        bn_gain,
        bn_shift,
    )
    product = lax.dot_general(gpre1, enc_w1, (((1,), (1,)), ((), ())), preferred_element_type=F32)
    grad_x = cell_total * (product - g[:, :genes].astype(F32))
    part = grid.me() // (grid.n // PARTS)
    each = genes * hidden // PARTS
    enc_flat = lax.dynamic_slice_in_dim(enc_part.reshape(-1), (genes * part) % PARTS * (hidden // PARTS), each)
    shard_enc = flat_shard(grid, enc_flat, FLAT_COLS, FLAT_ROWS)
    shard_out = flat_shard(grid, out25[:, :genes], FLAT_COLS, FLAT_ROWS)
    shard_narrow = flat_shard(grid, nar_part[: 2 * hidden // PARTS], NARROW_COLS, NARROW_ROWS)
    headw_grad, d1_grad, headb_grad, outb_grad = group_sum(
        grid,
        (headw_grad.T, d1_grad, headb_grad.reshape(-1)[: head_b.shape[0]], outb_grad.reshape(-1)[:genes]),
    )
    return (
        grad_x,
        shard_enc,
        shard_narrow,
        headw_grad,
        d1_grad,
        headb_grad,
        shard_out,
        outb_grad,
        grad_gain,
        grad_shift,
        offsets[None],
    )


def solution(mesh):
    grid = Slice(mesh.shape["cells"], mesh.shape["rep"])
    lines = P(("cells", "rep"), None)
    return jax.shard_map(
        functools.partial(shards, grid),
        mesh=mesh,
        in_specs=(lines, lines, P(("cells", "rep"))) + (P(),) * 12,
        out_specs=(lines, lines, lines, P(), P(), P(), lines, P(), P(), P(), P("cells", None, None)),
        check_vma=False,
    )
```

```python
import functools

import jax
import jax.numpy as jnp
from jax import lax
from jax.experimental import pallas as pl
from jax.experimental.pallas import tpu as pltpu
from jax.sharding import PartitionSpec as P

POP_DEV = 2
FLAT_COLS = 875
NARROW_COLS = 625
FLAT_ROWS = 6400
NARROW_ROWS = 2048

NORM_EPSILON = 1e-05
KL_WEIGHT = 5e-05
OFFSET_WEIGHT = 200.0

MESH_ID = pl.DeviceIdType.MESH
WIN = 1024
ROWS = 48
F32 = jnp.float32
BF16 = jnp.bfloat16


class Slice:
    def __init__(self, cells, rep):
        self.cells, self.rep = cells, rep
        self.n = cells * rep
        self.bits = self.n.bit_length() - 1
        self.digits = []
        low = 0
        while low < self.bits:
            width = min(3, self.bits - low)
            self.digits.append((low, 1 << width))
            low += width

    def me(self):
        return lax.axis_index("cells") * self.rep + lax.axis_index("rep")

    def place(self, index):
        return (index // self.rep, index % self.rep)


def entry_barrier(grid, peers):
    barrier = pltpu.get_barrier_semaphore()
    for peer in peers:
        pl.semaphore_signal(barrier, inc=1, device_id=grid.place(peer), device_id_type=MESH_ID)
    pl.semaphore_wait(barrier, len(peers))


def digit_peers(grid):
    me = grid.me()
    peers = []
    for low, size in grid.digits:
        rank = (me // (1 << low)) % size
        for k in range(1, size):
            other = (rank + k) % size
            peers.append(me + (other - rank) * (1 << low))
    return peers


class Gather:
    def __init__(self, grid, buffers, send_sems, recv_sems):
        self.grid, self.buffers, self.send_sems, self.recv_sems = grid, buffers, send_sems, recv_sems

    def rank(self, level):
        low, size = self.grid.digits[level]
        return (self.grid.me() // (1 << low)) % size

    def copy(self, level, slot, k, arriving=False):
        low, size = self.grid.digits[level]
        rank = self.rank(level)
        to = (rank + k) % size
        buffer = self.buffers[level].at[slot]
        return pltpu.make_async_remote_copy(
            src_ref=buffer.at[rank],
            dst_ref=buffer.at[(rank + size - k) % size if arriving else rank],
            send_sem=self.send_sems[level].at[slot, k - 1],
            recv_sem=self.recv_sems[level].at[slot, k - 1],
            device_id=self.grid.place(self.grid.me() + (to - rank) * (1 << low)),
            device_id_type=MESH_ID,
        )

    def start(self, level, slot):
        for k in range(1, self.grid.digits[level][1]):
            self.copy(level, slot, k).start()

    def wait(self, level, slot):
        for k in range(1, self.grid.digits[level][1]):
            self.copy(level, slot, k, arriving=True).wait_recv()

    def finish(self, level, slot):
        for k in range(1, self.grid.digits[level][1]):
            self.copy(level, slot, k).wait_send()

    def own(self, level, slot):
        return self.buffers[level].at[slot, self.rank(level)]


def put_row(ref, first, row, width):
    full = width // 128
    for c in range(full):
        ref[first + c : first + c + 1, :] = row[:, 128 * c : 128 * (c + 1)]
    rest = width - 128 * full
    if rest:
        ref[first + full : first + full + 1, 0:rest] = row[:, 128 * full : width]


def take_row(block, first, width):
    pieces = []
    for c in range(-(-width // 128)):
        pieces.append(block[first + c : first + c + 1, 0 : min(128, width - 128 * c)])
    return jnp.concatenate(pieces, axis=1)


def row_loop(rows, body, init):
    steps = rows // ROWS

    def step(i, carry):
        return body(pl.ds(pl.multiple_of(i * ROWS, ROWS), ROWS), carry)

    return lax.fori_loop(0, steps, step, init)


def column_sum(value):
    return jnp.sum(value, axis=0, keepdims=True)


PARTS = 32


def batch_norm(pre, nrm_out, act_out, gather, slot, gain_row, shift_row, inv_out, idle):
    rows, width = pre.shape
    total = row_loop(rows, lambda r, c: c + column_sum(pre[r, :]), jnp.zeros((1, width), F32))
    mean = total * (1.0 / rows)

    def squares(r, c):
        d = pre[r, :] - mean
        return c + column_sum(d * d)

    square = row_loop(rows, squares, jnp.zeros((1, width), F32))
    own = gather.own(0, slot)
    put_row(own, 0, mean, width)
    put_row(own, 8, square, width)
    count = float(rows)
    levels = len(gather.grid.digits)
    for level in range(levels):
        size = gather.grid.digits[level][1]
        gather.start(level, slot)
        idle()
        gather.wait(level, slot)
        buffer = gather.buffers[level].at[slot]
        means = [buffer[g, 0:8, :] for g in range(size)]
        merged = sum(means[1:], means[0]) * (1.0 / size)
        spread = sum([buffer[g, 8:16, :] for g in range(1, size)], buffer[0, 8:16, :])
        between = sum([(m - merged) * (m - merged) for m in means[1:]], (means[0] - merged) * (means[0] - merged))
        spread = spread + count * between
        count = count * size
        if level + 1 < levels:
            own = gather.own(level + 1, slot)
            own[0:8, :] = merged
            own[8:16, :] = spread
    inv = lax.rsqrt(spread * (1.0 / count) + NORM_EPSILON)
    mean = take_row(merged, 0, width)
    inv = take_row(inv, 0, width)
    inv_out[...] = inv

    def write(r, c):
        nrm = (pre[r, :] - mean) * inv
        nrm_out[r, :] = nrm
        value = gain_row * nrm + shift_row
        act_out[r, :] = (value * jax.nn.sigmoid(value)).astype(BF16)
        return c

    row_loop(rows, write, 0)


def nt(left, right):
    return lax.dot_general(left, right, (((1,), (1,)), ((), ())), preferred_element_type=F32)


def nn(left, right):
    return lax.dot_general(left, right, (((1,), (0,)), ((), ())), preferred_element_type=F32)


def tn(left, right):
    return lax.dot_general(left, right, (((0,), (0,)), ((), ())), preferred_element_type=F32)


def exact(left, right, dims):
    return lax.dot_general(
        left, right, (dims, ((), ())), precision=lax.Precision.HIGHEST, preferred_element_type=F32
    )


def windows(width):
    return [(s, min(WIN, width - s)) for s in range(0, width, WIN)]


def part_of(full, tail, i):
    return full.at[i] if i < full.shape[0] else tail


def forward_kernel(
    grid,
    table_ref,
    mask_ref,
    x_hbm,
    w1_hbm,
    noise_ref,
    gid_ref,
    w2_ref,
    head_ref,
    headb_ref,
    d1_ref,
    d2_ref,
    gain_ref,
    shift_ref,
    nrm0,
    nrm1,
    nrm2,
    nrm3,
    inv_out,
    act1,
    act2,
    zlat,
    act3,
    act4,
    head_out,
    ggroup_out,
    xt_out,
    offsets_out,
    x_all,
    xt,
    w_win,
    w_tail,
    pre,
    moments,
    *rest,
):
    levels = len(grid.digits)
    small = rest[:levels]
    wide = rest[levels : 2 * levels]
    s_send, s_recv, g_send, g_recv = (
        rest[2 * levels : 3 * levels],
        rest[3 * levels : 4 * levels],
        rest[4 * levels : 5 * levels],
        rest[5 * levels : 6 * levels],
    )
    in_sems, xt_sems = rest[6 * levels :]
    gather = Gather(grid, small, s_send, s_recv)
    group_gather = Gather(grid, wide, g_send, g_recv)
    latent = d1_ref.shape[0]
    genes = x_hbm.shape[1]
    spans = windows(genes)

    loads = []
    for i, (s, size) in enumerate(spans):
        a = pltpu.make_async_copy(x_hbm.at[:, pl.ds(s, size)], x_all.at[:, pl.ds(s, size)], in_sems.at[0, i])
        b = pltpu.make_async_copy(w1_hbm.at[:, pl.ds(s, size)], part_of(w_win, w_tail, i), in_sems.at[1, i])
        a.start()
        b.start()
        loads.append((a, b))
    entry_barrier(grid, digit_peers(grid))

    for i, (s, size) in enumerate(spans):
        loads[i][0].wait()
        loads[i][1].wait()
        part = nt(x_all[:, s : s + size], part_of(w_win, w_tail, i)[...])
        pre[...] = part if i == 0 else pre[...] + part

    starts = [(genes * j) // PARTS for j in range(PARTS)]
    parts_left = list(range(PARTS))

    def save(j):
        return pltpu.make_async_copy(xt.at[j], xt_out.at[j], xt_sems.at[j])

    def transpose():
        for j in parts_left[: -(-PARTS // (4 * levels))]:
            at = starts[j] // 128 * 128
            size = min(384, genes - at)
            lane = lax.broadcasted_iota(jnp.int32, (xt.shape[1], size), 1)
            line = lax.broadcasted_iota(jnp.int32, (xt.shape[1], size), 0)
            select = jnp.where(lane == line + (starts[j] - at), 1.0, 0.0).astype(BF16)
            xt[j] = nt(select, x_all[:, at : at + size]).astype(BF16)
            save(j).start()
            parts_left.remove(j)

    def norm(k, nrm, act):
        batch_norm(
            pre,
            nrm,
            act,
            gather,
            k,
            gain_ref[k : k + 1, :],
            shift_ref[k : k + 1, :],
            inv_out.at[k : k + 1, :],
            transpose,
        )

    norm(0, nrm0, act1)
    pre[...] = nn(act1[...], w2_ref[...])
    norm(1, nrm1, act2)
    head = nt(act2[...], head_ref[...]) + headb_ref[...]
    head_out[...] = head
    mu = head[:, 0:latent]
    logvar = head[:, latent : 2 * latent]
    zlat[...] = (mu + jnp.exp(0.5 * logvar) * noise_ref[...]).astype(BF16)

    groups = ggroup_out.shape[0]
    pops = groups // 2
    cells_here = gid_ref.shape[1]
    member = (lax.broadcasted_iota(jnp.int32, (groups, cells_here), 0) == gid_ref[...]).astype(F32)
    own = group_gather.own(0, 0)
    own[:, 0:latent] = exact(member, mu, ((1,), (0,)))
    own[:, latent : latent + 1] = jnp.sum(member, axis=1, keepdims=True)
    group_gather.start(0, 0)

    pre[...] = nn(zlat[...], d1_ref[...])
    norm(2, nrm2, act3)
    for level in range(levels):
        group_gather.wait(level, 0)
        size = grid.digits[level][1]
        buffer = wide[level].at[0]
        total = sum([buffer[g] for g in range(1, size)], buffer[0])
        if level + 1 < levels:
            group_gather.own(level + 1, 0)[...] = total
            group_gather.start(level + 1, 0)
        if level == 0:
            pre[...] = nn(act3[...], d2_ref[...])
            norm(3, nrm3, act4)
    counted = jnp.maximum(total[:, latent : latent + 1], 1.0)
    moments[...] = total / counted
    odd, even = pl.ds(1, pops, stride=2), pl.ds(0, pops, stride=2)
    offset = moments[odd, :] - moments[even, :]
    centre = jnp.sum(offset, axis=0, keepdims=True) * (1.0 / pops)
    grad_offset = (2.0 * OFFSET_WEIGHT / pops) * (offset - centre)
    row = lax.axis_index("cells")
    slots = offsets_out.shape[0]
    lane = lax.broadcasted_iota(jnp.int32, (1, pops), 1)
    picks = jnp.concatenate(
        [jnp.where(lane == table_ref[row, s], mask_ref[row, s].astype(F32), 0.0) for s in range(slots)], axis=0
    )
    offsets_out[...] = exact(picks, offset, ((1,), (0,)))[:, 0:latent]
    moments[odd, :] = grad_offset
    moments[even, :] = -grad_offset
    ggroup_out[...] = moments[...] / counted

    for j in range(PARTS):
        save(j).wait()
    for level in range(levels):
        for k in range(4):
            gather.finish(level, k)
        group_gather.finish(level, 0)


def call_forward(grid, cells_x, w1t, noise, gid, table, mask, w2, headt, headb, d1, d2, gain, shift):
    rows, genes = cells_x.shape
    hidden = w2.shape[0]
    latent = d1.shape[0]
    groups = 2 * POP_DEV * grid.cells
    count = len(windows(genes))
    levels = len(grid.digits)
    vm = pl.BlockSpec(memory_space=pltpu.VMEM)
    hbm = pl.BlockSpec(memory_space=pl.ANY)
    sm = pl.BlockSpec(memory_space=pltpu.SMEM)
    wide_f = jax.ShapeDtypeStruct((rows, hidden), F32)
    wide_b = jax.ShapeDtypeStruct((rows, hidden), BF16)
    out_shape = (
        wide_f,
        wide_f,
        wide_f,
        wide_f,
        jax.ShapeDtypeStruct((4, hidden), F32),
        wide_b,
        wide_b,
        jax.ShapeDtypeStruct((rows, latent), BF16),
        wide_b,
        wide_b,
        jax.ShapeDtypeStruct((rows, 2 * latent), F32),
        jax.ShapeDtypeStruct((groups, 128), F32),
        jax.ShapeDtypeStruct((PARTS, 32 * count, rows), BF16),
        jax.ShapeDtypeStruct((table.shape[1], latent), F32),
    )
    scratch = (
        [
            pltpu.VMEM((rows, genes), BF16),
            pltpu.VMEM((PARTS, 32 * count, rows), BF16),
            pltpu.VMEM((count - 1, hidden, WIN), BF16),
            pltpu.VMEM((hidden, genes - (count - 1) * WIN), BF16),
            pltpu.VMEM((rows, hidden), F32),
            pltpu.VMEM((groups, 128), F32),
        ]
        + [pltpu.VMEM((4, size, 16, 128), F32) for _, size in grid.digits]
        + [pltpu.VMEM((1, size, groups, 128), F32) for _, size in grid.digits]
        + [pltpu.SemaphoreType.DMA((4, size - 1)) for _, size in grid.digits]
        + [pltpu.SemaphoreType.DMA((4, size - 1)) for _, size in grid.digits]
        + [pltpu.SemaphoreType.DMA((1, size - 1)) for _, size in grid.digits]
        + [pltpu.SemaphoreType.DMA((1, size - 1)) for _, size in grid.digits]
        + [pltpu.SemaphoreType.DMA((2, count)), pltpu.SemaphoreType.DMA((PARTS,))]
    )
    return pl.pallas_call(
        functools.partial(forward_kernel, grid),
        out_shape=out_shape,
        in_specs=[sm, sm, hbm, hbm] + [vm] * 9,
        out_specs=[vm] * (len(out_shape) - 2) + [hbm, vm],
        scratch_shapes=scratch,
        name="forward",
        compiler_params=pltpu.CompilerParams(
            collective_id=0, has_side_effects=True, vmem_limit_bytes=60 * 2**20
        ),
    )(table, mask, cells_x, w1t, noise, gid, w2, headt, headb, d1, d2, gain, shift)


ORDERS = (
    (0, 2, 3, 4, 1),
    (0, 3, 1, 2, 4),
    (0, 2, 3, 1, 4),
    (0, 1, 3, 2, 4),
    (0, 2, 3, 1, 4),
    (0, 1, 2, 3, 4),
    (0, 2, 1, 3, 4),
    (0, 1, 2, 3, 4),
    (0, 2, 1, 3, 4),
    (0, 3, 1, 2, 4),
    (0, 1, 3, 2, 4),
    (0, 2, 3, 1, 4),
    (0, 1, 3, 2, 4),
    (0, 2, 1, 3, 4),
    (0, 2, 3, 1, 4),
    (0, 1, 2, 3, 4),
)
C, U, L, S, F = range(5)
PLAN = (
    (C,),
    (U, 0),
    (C,),
    (C,),
    (L, 0),
    (S, 0, 1, 0, 1),
    (S, 0, 1, 1, 2),
    (U, 1),
    (S, 0, 1, 3, 1),
    (C,),
    (S, 0, 1, 4, 1),
    (C,),
    (L, 1),
    (S, 1, 1, 0, 1),
    (S, 0, 1, 5, 1),
    (S, 1, 1, 1, 1),
    (C,),
    (S, 0, 1, 6, 1),
    (S, 1, 1, 2, 1),
    (C,),
    (S, 1, 1, 3, 1),
    (C,),
    (S, 0, 1, 7, 1),
    (S, 1, 1, 4, 1),
    (C,),
    (C,),
    (S, 1, 1, 5, 2),
    (U, 2),
    (F, 0, 1),
    (S, 1, 1, 7, 1),
    (C,),
    (S, 0, 2, 0, 1),
    (C,),
    (L, 2),
    (S, 2, 1, 0, 1),
    (S, 2, 1, 1, 2),
    (S, 0, 2, 1, 2),
    (U, 3),
    (F, 1, 1),
    (S, 1, 2, 0, 1),
    (S, 1, 2, 1, 1),
    (S, 2, 1, 3, 2),
    (S, 0, 2, 3, 1),
    (C,),
    (S, 1, 2, 2, 1),
    (C,),
    (L, 3),
    (C,),
    (C,),
    (S, 1, 2, 3, 1),
    (S, 3, 1, 0, 1),
    (S, 2, 1, 5, 2),
    (F, 0, 2),
    (S, 0, 3, 0, 1),
    (S, 3, 1, 1, 2),
    (S, 2, 1, 7, 1),
    (S, 0, 3, 1, 1),
    (U, 4),
    (C,),
    (S, 3, 1, 3, 1),
    (F, 1, 2),
    (S, 1, 3, 0, 1),
    (F, 2, 1),
    (S, 1, 3, 1, 1),
    (S, 2, 2, 0, 1),
    (L, 4),
    (S, 3, 1, 4, 2),
    (S, 4, 1, 0, 2),
    (S, 2, 2, 1, 2),
    (U, 5),
    (F, 0, 3),
    (F, 1, 3),
    (S, 3, 1, 6, 2),
    (S, 4, 1, 2, 2),
    (S, 2, 2, 3, 1),
    (S, 1, 4, 0, 1),
    (C,),
    (L, 5),
    (C,),
    (C,),
    (S, 0, 4, 0, 1),
    (S, 5, 1, 0, 1),
    (S, 4, 1, 4, 2),
    (F, 2, 2),
    (S, 5, 1, 1, 2),
    (S, 4, 1, 6, 2),
    (U, 6),
    (C,),
    (S, 5, 1, 3, 1),
    (F, 0, 4),
    (F, 1, 4),
    (F, 3, 1),
    (S, 3, 2, 0, 1),
    (S, 3, 2, 1, 1),
    (L, 6),
    (S, 6, 1, 0, 1),
    (S, 5, 1, 4, 2),
    (S, 6, 1, 1, 2),
    (S, 3, 2, 2, 2),
    (C,),
    (F, 4, 1),
    (C,),
    (C,),
    (S, 5, 1, 6, 2),
    (S, 6, 1, 3, 2),
    (S, 4, 2, 0, 2),
    (F, 3, 2),
    (C,),
    (S, 2, 3, 0, 2),
    (S, 6, 1, 5, 2),
    (S, 4, 2, 2, 2),
    (F, 5, 1),
    (S, 6, 1, 7, 1),
    (S, 3, 3, 0, 1),
    (C,),
    (F, 2, 3),
    (S, 2, 4, 0, 1),
    (F, 4, 2),
    (S, 4, 3, 0, 1),
    (C,),
    (C,),
    (S, 4, 3, 1, 1),
    (S, 3, 3, 1, 1),
    (S, 5, 2, 0, 1),
    (F, 6, 1),
    (S, 6, 2, 0, 1),
    (F, 2, 4),
    (C,),
    (S, 6, 2, 1, 2),
    (S, 5, 2, 1, 2),
    (F, 3, 3),
    (S, 3, 4, 0, 1),
    (F, 4, 3),
    (S, 6, 2, 3, 1),
    (S, 5, 2, 3, 1),
    (S, 4, 4, 0, 1),
    (C,),
    (F, 3, 4),
    (U, 7),
    (F, 5, 2),
    (S, 5, 3, 0, 2),
    (F, 6, 2),
    (S, 6, 3, 0, 2),
    (F, 4, 4),
    (L, 7),
    (S, 7, 1, 0, 2),
    (S, 7, 1, 2, 2),
    (S, 7, 1, 4, 2),
    (U, 8),
    (F, 5, 3),
    (S, 7, 1, 6, 1),
    (S, 5, 4, 0, 1),
    (L, 8),
    (S, 7, 1, 7, 1),
    (S, 8, 1, 0, 2),
    (S, 8, 1, 2, 2),
    (S, 8, 1, 4, 2),
    (S, 8, 1, 6, 2),
    (U, 9),
    (F, 6, 3),
    (S, 6, 4, 0, 1),
    (F, 5, 4),
    (L, 9),
    (S, 9, 1, 0, 2),
    (S, 9, 1, 2, 2),
    (S, 9, 1, 4, 1),
    (U, 10),
    (S, 9, 1, 5, 1),
    (F, 6, 4),
    (S, 9, 1, 6, 1),
    (L, 10),
    (S, 10, 1, 0, 2),
    (S, 10, 1, 2, 2),
    (S, 10, 1, 4, 2),
    (S, 9, 1, 7, 1),
    (F, 7, 1),
    (S, 10, 1, 6, 1),
    (S, 7, 2, 0, 2),
    (S, 7, 2, 2, 2),
    (F, 8, 1),
    (U, 11),
    (S, 10, 1, 7, 1),
    (S, 8, 2, 0, 1),
    (L, 11),
    (S, 8, 2, 1, 1),
    (U, 12),
    (S, 8, 2, 2, 2),
    (F, 7, 2),
    (S, 7, 3, 0, 2),
    (S, 11, 1, 0, 2),
    (S, 11, 1, 2, 2),
    (S, 11, 1, 4, 2),
    (L, 12),
    (F, 9, 1),
    (S, 9, 2, 0, 2),
    (S, 11, 1, 6, 1),
    (U, 13),
    (F, 10, 1),
    (S, 9, 2, 2, 2),
    (S, 11, 1, 7, 1),
    (S, 10, 2, 0, 2),
    (S, 10, 2, 2, 2),
    (F, 7, 3),
    (S, 7, 4, 0, 1),
    (L, 13),
    (U, 14),
    (F, 8, 2),
    (S, 8, 3, 0, 2),
    (S, 12, 1, 0, 2),
    (S, 12, 1, 2, 1),
    (L, 14),
    (S, 12, 1, 3, 1),
    (F, 10, 2),
    (S, 10, 3, 0, 2),
    (S, 12, 1, 4, 1),
    (S, 14, 1, 0, 2),
    (S, 14, 1, 2, 2),
    (F, 11, 1),
    (S, 12, 1, 5, 1),
    (S, 14, 1, 4, 1),
    (S, 11, 2, 0, 2),
    (S, 11, 2, 2, 2),
    (U, 15),
    (F, 7, 4),
    (S, 12, 1, 6, 1),
    (S, 14, 1, 5, 1),
    (F, 9, 2),
    (F, 10, 3),
    (S, 14, 1, 6, 1),
    (S, 10, 4, 0, 1),
    (S, 12, 1, 7, 1),
    (F, 8, 3),
    (S, 8, 4, 0, 1),
    (L, 15),
    (S, 14, 1, 7, 1),
    (F, 11, 2),
    (S, 11, 3, 0, 2),
    (S, 9, 3, 0, 2),
    (S, 13, 1, 0, 1),
    (S, 15, 1, 0, 2),
    (F, 10, 4),
    (S, 15, 1, 2, 2),
    (S, 13, 1, 1, 2),
    (F, 12, 1),
    (S, 15, 1, 4, 1),
    (S, 13, 1, 3, 1),
    (S, 12, 2, 0, 2),
    (S, 12, 2, 2, 2),
    (F, 8, 4),
    (F, 14, 1),
    (S, 15, 1, 5, 1),
    (S, 13, 1, 4, 1),
    (S, 14, 2, 0, 2),
    (S, 14, 2, 2, 1),
    (F, 11, 3),
    (S, 15, 1, 6, 1),
    (S, 13, 1, 5, 1),
    (S, 14, 2, 3, 1),
    (F, 9, 3),
    (S, 13, 1, 6, 1),
    (S, 9, 4, 0, 1),
    (S, 15, 1, 7, 1),
    (F, 12, 2),
    (S, 13, 1, 7, 1),
    (S, 11, 4, 0, 1),
    (F, 14, 2),
    (S, 14, 3, 0, 2),
    (S, 12, 3, 0, 2),
    (F, 15, 1),
    (S, 15, 2, 0, 2),
    (S, 15, 2, 2, 2),
    (F, 9, 4),
    (F, 13, 1),
    (S, 13, 2, 0, 2),
    (S, 13, 2, 2, 2),
    (F, 14, 3),
    (S, 14, 4, 0, 1),
    (F, 11, 4),
    (F, 12, 3),
    (S, 12, 4, 0, 1),
    (F, 14, 4),
    (F, 13, 2),
    (S, 13, 3, 0, 2),
    (F, 12, 4),
    (F, 15, 2),
    (S, 15, 3, 0, 2),
    (F, 13, 3),
    (S, 13, 4, 0, 1),
    (F, 15, 3),
    (S, 15, 4, 0, 1),
    (F, 13, 4),
    (F, 15, 4),
)
CHANNELS = 4
STAGES = 5
SLOT_ROWS = 200


class Scatter:
    def __init__(self, grid, total, stage, low, landing, stage_sems, send_sems, recv_sems, credits):
        self.grid, self.total = grid, total
        self.stage, self.low, self.landing = stage, low, landing
        self.stage_sems, self.send_sems, self.recv_sems, self.credits = stage_sems, send_sems, recv_sems, credits
        self.shift = grid.bits - STAGES
        self.rows = {}

    def bit(self, b):
        return (self.grid.me() // (1 << (b + self.shift))) % 2

    def partner(self, b):
        return self.grid.place(self.grid.me() + (1 - 2 * self.bit(b)) * (1 << (b + self.shift)))

    def part(self, q, k):
        out = 0
        for t, b in enumerate(ORDERS[q]):
            own = self.bit(b)
            out = out + (1 << b) * ((1 - own) if (k >> (STAGES - 1 - t)) & 1 else own)
        return out

    def send(self, q, t, first=0, number=None):
        channel, rows = q % CHANNELS, self.rows[q]
        slots = 16 >> t
        at, size = first * rows, (slots if number is None else number) * rows
        if t == 0:
            source, sem = self.stage.at[q % 2, at : at + size], self.stage_sems.at[q % 2]
        else:
            start = slots * rows + at
            source, sem = self.landing[t - 1].at[channel, start : start + size], self.send_sems.at[channel, t]
        return pltpu.make_async_remote_copy(
            src_ref=source,
            dst_ref=self.landing[t].at[channel, at : at + size],
            send_sem=sem,
            recv_sem=self.recv_sems.at[channel, t],
            device_id=self.partner(ORDERS[q][t]),
            device_id_type=MESH_ID,
        )

    def feed(self, q, t, first, number):
        if first == 0 and q >= CHANNELS:
            pl.semaphore_wait(self.credits.at[q - CHANNELS, t], 1)
        self.send(q, t, first, number).start()

    def free(self, q, t):
        if q + CHANNELS < self.total:
            pl.semaphore_signal(
                self.credits.at[q, t],
                inc=1,
                device_id=self.partner(ORDERS[q + CHANNELS][t]),
                device_id_type=MESH_ID,
            )

    def upper(self, q, rows, fill):
        self.rows[q] = rows
        if q >= 2:
            self.send(q - 2, 0).wait_send()
        fill(self.stage.at[q % 2], True)
        self.feed(q, 0, 0, 16)
        fill(self.low, False)

    def lower(self, q):
        channel, rows = q % CHANNELS, self.rows[q]
        self.send(q, 0).wait_recv()
        mine = self.landing[0].at[channel]

        def add(i, c):
            r = pl.ds(pl.multiple_of(i * rows, 8), rows)
            mine[r, :] += self.low[r, :]
            return c

        lax.fori_loop(0, 16, add, 0)

    def fold(self, q, t):
        channel, rows = q % CHANNELS, self.rows[q]
        self.send(q, t).wait_recv()
        mine, before = self.landing[t].at[channel], self.landing[t - 1].at[channel]

        def add(i, c):
            r = pl.ds(pl.multiple_of(i * rows, 8), rows)
            mine[r, :] += before[r, :]
            return c

        lax.fori_loop(0, 16 >> t, add, 0)
        self.send(q, t).wait_send()
        self.free(q, t - 1)

    def last(self, q, done):
        channel, rows = q % CHANNELS, self.rows[q]
        t = STAGES - 1
        self.send(q, t).wait_recv()
        done(self.landing[t][channel, 0:rows, :] + self.landing[t - 1][channel, 0:rows, :])
        self.send(q, t).wait_send()
        self.free(q, t - 1)
        self.free(q, t)


class Spread:
    def __init__(self, scatter, block, landing, whole, sems):
        self.scatter, self.block, self.landing, self.whole, self.sems = scatter, block, landing, whole, sems
        self.rows = block.shape[0]

    def begin(self, t):
        out = 0
        for i in range(t):
            out = out + self.scatter.bit(i) * (self.rows >> (i + 1))
        return out

    def halving(self, t):
        size = self.rows >> (t + 1)
        at = self.begin(t) + (1 - self.scatter.bit(t)) * size
        return pltpu.make_async_remote_copy(
            src_ref=self.block.at[pl.ds(pl.multiple_of(at, 8), size)],
            dst_ref=self.landing[t],
            send_sem=self.sems.at[0, t],
            recv_sem=self.sems.at[1, t],
            device_id=self.scatter.partner(t),
            device_id_type=MESH_ID,
        )

    def doubling(self, t, arriving=False):
        size = self.rows >> (t + 1)
        at = self.begin(t + 1)
        there = self.begin(t) + (1 - self.scatter.bit(t)) * size if arriving else at
        return pltpu.make_async_remote_copy(
            src_ref=self.whole.at[pl.ds(pl.multiple_of(at, 8), size)],
            dst_ref=self.whole.at[pl.ds(pl.multiple_of(there, 8), size)],
            send_sem=self.sems.at[2, t],
            recv_sem=self.sems.at[3, t],
            device_id=self.scatter.partner(t),
            device_id_type=MESH_ID,
        )

    def step(self, i):
        if i == 0:
            self.halving(0).start()
        elif i <= STAGES:
            t = i - 1
            self.halving(t).wait_recv()
            size = self.rows >> (t + 1)
            r = pl.ds(pl.multiple_of(self.begin(t + 1), 8), size)
            target = self.whole if i == STAGES else self.block
            target[r, :] = self.block[r, :] + self.landing[t][...]
            self.halving(t).wait_send()
            if i < STAGES:
                self.halving(t + 1).start()
            else:
                self.doubling(t).start()
        else:
            t = 2 * STAGES - i
            self.doubling(t, True).wait_recv()
            self.doubling(t).wait_send()
            if t > 0:
                self.doubling(t - 1).start()


def one_hot(rows, target):
    lane = lax.broadcasted_iota(jnp.int32, (rows, target.shape[1]), 0)
    return jnp.where(lane == target, 1.0, 0.0).astype(BF16)


def column_parts(width, size):
    column = lax.broadcasted_iota(jnp.int32, (1, width), 1)
    part = jnp.zeros((1, width), jnp.int32)
    for m in range(1, width // size):
        part = part + jnp.where(column >= m * size, 1, 0)
    return column, part


def slot_of(scatter, q, bits, parts, part):
    order = [b for b in ORDERS[q] if b in bits]
    slot = jnp.zeros_like(part)
    for value in range(parts):
        at = 0
        for t, b in enumerate(order):
            own = scatter.bit(b)
            weight = 1 << (len(order) - 1 - t)
            at = at + weight * ((1 - own) if (value >> bits.index(b)) & 1 else own)
        slot = jnp.where(part == value, at, slot)
    return slot


def sum_blocks(gather, slot):
    levels = len(gather.grid.digits)
    yield
    for level in range(levels):
        gather.start(level, slot)
        if level < 2:
            yield
        gather.wait(level, slot)
        size = gather.grid.digits[level][1]
        buffer = gather.buffers[level].at[slot]
        total = sum([buffer[g] for g in range(1, size)], buffer[0])
        if level + 1 < levels:
            gather.own(level + 1, slot)[...] = total
    return total


def norm_gradient(grad, nrm, out, gather, slot, gain_row, shift_row, inv_row, scale, gain_out, shift_out):
    rows, width = grad.shape

    def gate(r, carry):
        n = nrm[r, :]
        value = gain_row * n + shift_row
        sig = jax.nn.sigmoid(value)
        g = grad[r, :] * sig * (1.0 + value * (1.0 - sig))
        grad[r, :] = g
        return carry[0] + column_sum(g), carry[1] + column_sum(g * n)

    zero = jnp.zeros((1, width), F32)
    shift_sum, gain_sum = row_loop(rows, gate, (zero, zero))
    own = gather.own(0, slot)
    put_row(own, 0, shift_sum, width)
    put_row(own, 8, gain_sum, width)
    total = yield from sum_blocks(gather, slot)
    shift_sum = take_row(total, 0, width)
    gain_sum = take_row(total, 8, width)
    shift_out[...] = shift_sum
    gain_out[...] = gain_sum
    factor = gain_row * inv_row
    shift_mean = shift_sum * scale
    gain_mean = gain_sum * scale

    def write(r, c):
        out[r, :] = (factor * (grad[r, :] - shift_mean - nrm[r, :] * gain_mean)).astype(BF16)
        return c

    row_loop(rows, write, 0)


D1_ROWS = 104
REP_ROWS = 2304


def backward_kernel(
    grid,
    latent,
    x_hbm,
    outw_hbm,
    nrm_hbm0,
    nrm_hbm1,
    nrm_hbm2,
    nrm_hbm3,
    act1_hbm,
    act2_hbm,
    act3_hbm,
    xt_hbm,
    act4_ref,
    zlat_ref,
    head_ref_in,
    noise_ref,
    gid_ref,
    ggroup_ref,
    inv_ref,
    outb_ref,
    w2_ref,
    head_ref,
    d1_ref,
    d2_ref,
    gain_ref,
    shift_ref,
    g_out,
    gpre1,
    out25,
    enc_part,
    nar_part,
    d1_out,
    headw_out,
    outb_out,
    headb_out,
    gain_out,
    shift_out,
    *rest,
):
    levels = len(grid.digits)
    rest = list(rest)

    def take(n):
        got = rest[:n]
        del rest[:n]
        return got

    small, s_send, s_recv = take(levels), take(levels), take(levels)
    stage, low, *landing = take(2 + STAGES)
    stage_sems, send_sems, recv_sems, credits = take(4)
    rep_block, rep_whole, *rep_landing = take(2 + STAGES)
    (rep_sems,) = take(1)
    g_win, wide, gact, gpre4, gpre3, gpre2, ghead, gcell, lhs, nrm_buf, fin = take(11)
    picked = lhs.at[0:512]
    in_sems, g_sems, nrm_sems, xt_sem, act_sems = take(5)

    rows, genes = x_hbm.shape
    hidden = w2_ref.shape[0]
    spans = windows(genes)
    count = len(spans)
    cell_total = float(rows * grid.n)
    total = 2 * count + 2
    gather = Gather(grid, small, s_send, s_recv)
    first = count
    scatter = Scatter(grid, total, stage, low, landing, stage_sems, send_sems, recv_sems, credits)
    spread = Spread(scatter, rep_block, rep_landing, rep_whole, rep_sems)
    rep_outb = 7 * (D1_ROWS + 2 * latent)
    rep_headb = rep_outb + 8 * count

    entry_barrier(grid, digit_peers(grid))
    nrm_loads = {
        k: pltpu.make_async_copy(ref, nrm_buf.at[(k + 1) % 2], nrm_sems.at[k])
        for k, ref in enumerate((nrm_hbm0, nrm_hbm1, nrm_hbm2, nrm_hbm3))
    }
    nrm_loads[3].start()
    nrm_loads[2].start()


    def out_fill(s):
        buffer = g_win.at[s % 3]

        def fill(target, is_upper):
            first = hidden // 2 if is_upper else 0
            part = nn(lhs[first : first + hidden // 2, :], buffer[...])
            for c in range(WIN // 128):
                target[pl.ds(c, hidden // 2, stride=8), :] = part[:, 128 * c : 128 * (c + 1)]

        return fill

    def out_lhs(q):
        column, part = column_parts(hidden, hidden // PARTS)
        slot = slot_of(scatter, q, (0, 1, 2, 3, 4), PARTS, part)
        target = column + (hidden // PARTS) * (slot - part)
        block = hidden // 5

        def some(i, c):
            at = pl.multiple_of(i * block, block)
            lhs[pl.ds(at, block), :] = nt(one_hot(block, target - at), act4_ref[...]).astype(BF16)
            return c

        lax.fori_loop(0, 5, some, 0)

    def out_done(s):
        def done(value):
            fin[...] = value
            for c in range(WIN // 128):
                out25[:, WIN * s + 128 * c : WIN * s + 128 * (c + 1)] = fin[pl.ds(c, hidden // PARTS, stride=8), :]

        return done

    done = {s: out_done(s) for s in range(count)}
    pieces = {}
    for s in range(count):
        pieces[s] = (SLOT_ROWS, out_fill(s))

    plan = list(PLAN)

    def run(chain, more=None):
        while plan:
            what, *which = plan[0]
            if what == C:
                if next(chain, None) is None:
                    return
            elif what == U:
                if which[0] < count:
                    out_lhs(which[0])
                scatter.upper(which[0], *pieces[which[0]])
            elif what == L:
                scatter.lower(which[0])
            elif what == S:
                scatter.feed(*which)
            elif which[1] < STAGES - 1:
                scatter.fold(*which)
            else:
                scatter.last(which[0], done[which[0]])
            del plan[0]
            if more is not None:
                more()

    def output_layer(w_ring, w_tail, x_ring, x_tail):
        def load(s):
            at, size = spans[s]
            tail = s == count - 1
            return (
                pltpu.make_async_copy(
                    outw_hbm.at[:, pl.ds(at, size)], w_tail if tail else w_ring.at[s % 3], in_sems.at[0, s]
                ),
                pltpu.make_async_copy(
                    x_hbm.at[:, pl.ds(at, size)], x_tail if tail else x_ring.at[s % 2], in_sems.at[1, s]
                ),
            )

        def save(s):
            return pltpu.make_async_copy(g_win.at[s % 3], g_out.at[:, pl.ds(WIN * s, WIN)], g_sems.at[s])

        def layers():
            for s in range(2):
                for copy in load(s):
                    copy.start()
            for s in range(count):
                yield from layer(s)

        def layer(s):
            at, size = spans[s]
            tail = s == count - 1
            w = w_tail if tail else w_ring.at[s % 3]
            x = x_tail if tail else x_ring.at[s % 2]
            for copy in load(s):
                copy.wait()
            wide[:, 0:size] = nn(act4_ref[...], w[...])
            bias = outb_ref[:, at : at + size]
            if s >= 3:
                save(s - 3).wait()
            g = g_win.at[s % 3]

            def residual(r, c):
                value = wide[r, 0:size] + bias - x[r, :].astype(F32)
                value = (value * (2.0 / cell_total)).astype(BF16)
                g[r, 0:size] = value
                return c + column_sum(value.astype(F32))

            put_row(rep_block, rep_outb + 8 * s, row_loop(rows, residual, jnp.zeros((1, size), F32)), size)
            if size < WIN:
                g[:, size:WIN] = jnp.zeros((rows, WIN - size), BF16)
            save(s).start()
            if s + 2 < count:
                for copy in load(s + 2):
                    copy.start()
            yield 0
            part = nt(g[:, 0:size], w[...])
            gact[...] = part if s == 0 else gact[...] + part
            yield 0

        run(layers())
        for s in range(count - 3, count):
            save(s).wait()

    pl.run_scoped(
        output_layer,
        pltpu.VMEM((3, hidden, WIN), BF16),
        pltpu.VMEM((hidden, spans[-1][1]), BF16),
        pltpu.VMEM((2, rows, WIN), BF16),
        pltpu.VMEM((rows, spans[-1][1]), BF16),
    )


    def pack(target, at, source, row, height):
        full = hidden // 128
        for c in range(full):
            target[pl.ds(pl.multiple_of(at + height * c, 8), height), :] = source[
                pl.ds(row, height), 128 * c : 128 * (c + 1)
            ]
        rest_width = hidden - 128 * full
        pieces = [source[pl.ds(row + 8 * i, 8), 128 * full : hidden] for i in range(height // 8)]
        target[pl.ds(pl.multiple_of(at + height * full, 8), 8), 0 : rest_width * len(pieces)] = jnp.concatenate(
            pieces, axis=1
        )

    def unpack(value, out, row, height):
        full = hidden // 128
        rest_width = hidden - 128 * full
        for c in range(full):
            out[row : row + height, 128 * c : 128 * (c + 1)] = value[height * c : height * (c + 1), :]
        for i in range(height // 8):
            out[row + 8 * i : row + 8 * i + 8, 128 * full : hidden] = value[
                height * full : height * full + 8, rest_width * i : rest_width * (i + 1)
            ]

    def finish(xt, act_buf):
        xt_load = pltpu.make_async_copy(xt_hbm, xt, xt_sem)
        xt_load.start()

        def enc_fill(q, s):
            def fill(target, is_upper):
                for i in range(16):
                    j = scatter.part(q, 16 + i if is_upper else i)
                    picked[32 * i : 32 * i + 32, :] = xt[j, 32 * s : 32 * s + 32, :]
                wide[0:512, 0:hidden] = nn(picked[...], gpre1[...])

                def one(i, c):
                    pack(target, i * SLOT_ROWS, wide, pl.multiple_of(i * 32, 32), 32)
                    return c

                lax.fori_loop(0, 16, one, 0)

            return fill

        def enc_done(s):
            return lambda value: unpack(value, enc_part, 32 * s, 32)

        each = 2 * hidden // PARTS
        skip = (0, 32)

        def nar_fill(q, which):
            height_here = 32 if which == 0 else 24
            rows_here = 25 * 8 if which == 0 else 19 * 8
            place = STAGES - 1 - ORDERS[q].index(4)

            def fill(target, is_upper):
                column, part = column_parts(hidden, each)
                slot = slot_of(scatter, q, (0, 1, 2, 3), PARTS // 2, part)
                line = column - each * part - skip[which]
                inside = (line >= 0) & (line < height_here)
                base = 8 if is_upper else 0
                place_in = jnp.where(inside, (slot - base) * height_here + line, -1)
                place_in = jnp.where((slot >= base) & (slot < base + 8), place_in, -1)
                select = one_hot(8 * height_here, place_in)
                for matrix, act_slot, grad in ((0, 0, gpre2), (1, 1, gpre4)):
                    size = 8 * height_here
                    picked[0:size, :] = nt(select, act_buf[act_slot]).astype(BF16)
                    wide[0:size, 0:hidden] = nn(picked[0:size, :], grad[...])
                    flip = scatter.bit(4) if matrix == 0 else 1 - scatter.bit(4)
                    for i in range(8):
                        k = (i >> place) * (2 << place) + (i & ((1 << place) - 1)) + flip * (1 << place)
                        pack(target, k * rows_here, wide, i * height_here, height_here)

            return rows_here, fill

        def nar_done(which):
            if which == 0:
                return lambda value: unpack(value, nar_part, 0, 32)
            return lambda value: unpack(value, nar_part, 32, 24)

        for which in range(2):
            done[first + which] = nar_done(which)
            pieces[first + which] = nar_fill(first + which, which)
        for s in range(count):
            done[first + 2 + s] = enc_done(s)
            pieces[first + 2 + s] = (SLOT_ROWS, enc_fill(first + 2 + s, s))

        def row(ref, k):
            return ref[k : k + 1, :]

        def back(k, grad, out):
            nrm_loads[k].wait()
            return norm_gradient(
                grad,
                nrm_buf.at[(k + 1) % 2],
                out,
                gather,
                k,
                row(gain_ref, k),
                row(shift_ref, k),
                row(inv_ref, k),
                1.0 / cell_total,
                gain_out.at[k : k + 1, :],
                shift_out.at[k : k + 1, :],
            )

        act_loads = [
            pltpu.make_async_copy(ref, act_buf.at[at], act_sems.at[i])
            for i, (ref, at) in enumerate(((act1_hbm, 0), (act3_hbm, 1), (act2_hbm, 0)))
        ]
        act_loads[1].start()
        act_loads[2].start()

        def latent_side():
            act_loads[2].wait()
            d1_grad = tn(zlat_ref[...], gpre3[...])
            headw_grad = tn(ghead[...], act_buf[0])
            act_loads[0].start()
            for c in range(-(-hidden // 128)):
                size = min(128, hidden - 128 * c)
                at = D1_ROWS * c
                rep_block[at : at + latent, 0:size] = d1_grad[:, 128 * c : 128 * c + size]
                at = 7 * D1_ROWS + 2 * latent * c
                rep_block[at : at + 2 * latent, 0:size] = headw_grad[:, 128 * c : 128 * c + size]
            put_row(rep_block, rep_headb, column_sum(ghead[...].astype(F32)), 2 * latent)

        def chain():
            for k, out in ((3, gpre4), (2, gpre3), (1, gpre2), (0, gpre1)):
                waits = back(k, gact, out)
                for at, _ in enumerate(waits):
                    if (k, at) == (3, 1):
                        groups = ggroup_ref.shape[0]
                        member = (lax.broadcasted_iota(jnp.int32, (groups, rows), 0) == gid_ref[...]).astype(F32)
                        gcell[...] = exact(member, ggroup_ref[...], ((0,), (0,)))
                    if (k, at) == (1, 1):
                        latent_side()
                    yield 0
                if k == 3:
                    nrm_loads[1].start()
                    gact[...] = nt(gpre4[...], d2_ref[...])
                elif k == 2:
                    nrm_loads[0].start()
                    grad_z = nt(gpre3[...], d1_ref[...])
                    mu = head_ref_in[:, 0:latent]
                    logvar = head_ref_in[:, latent : 2 * latent]
                    kl = KL_WEIGHT * genes / cell_total
                    deviation = jnp.exp(0.5 * logvar)
                    grad_mu = grad_z + kl * mu + gcell[:, 0:latent]
                    grad_logvar = grad_z * noise_ref[...] * (0.5 * deviation) + 0.5 * kl * (jnp.exp(logvar) - 1.0)
                    ghead[...] = jnp.concatenate([grad_mu, grad_logvar], axis=1).astype(BF16)
                    gact[...] = nn(ghead[...], head_ref[...])
                elif k == 1:
                    gact[...] = nt(gpre2[...], w2_ref[...])
                else:
                    for copy in act_loads[:2]:
                        copy.wait()
                    xt_load.wait()
                    waiting.extend(range(2 * STAGES + 1))
                yield 0

        waiting = []

        def more():
            if waiting and len(plan) % 12 == 0:
                spread.step(waiting.pop(0))

        run(chain(), more)
        for i in waiting:
            spread.step(i)
        for q in (total - 2, total - 1):
            scatter.send(q, 0).wait_send()
        for c in range(-(-hidden // 128)):
            size = min(128, hidden - 128 * c)
            at = D1_ROWS * c
            d1_out[:, 128 * c : 128 * c + size] = rep_whole[at : at + latent, 0:size]
            at = 7 * D1_ROWS + 2 * latent * c
            headw_out[:, 128 * c : 128 * c + size] = rep_whole[at : at + 2 * latent, 0:size]
        outb_out[...] = rep_whole[rep_outb : rep_outb + 8 * count, :]
        headb_out[...] = rep_whole[rep_headb : rep_headb + 8, :]
        for level in range(levels):
            for k in range(4):
                gather.finish(level, k)

    pl.run_scoped(finish, pltpu.VMEM(xt_hbm.shape, BF16), pltpu.VMEM((2, rows, hidden), BF16))


def call_backward(grid, kept, cells_x, out_w, noise, gid, out_b, w2, headt, d1, d2, gain, shift):
    (nrm0, nrm1, nrm2, nrm3, inv, act1, act2, zlat, act3, act4, head, ggroup, xt) = kept
    rows, genes = cells_x.shape
    hidden, latent = w2.shape[0], d1.shape[0]
    spans = windows(genes)
    count = len(spans)
    vm = pl.BlockSpec(memory_space=pltpu.VMEM)
    hbm = pl.BlockSpec(memory_space=pl.ANY)
    shape = jax.ShapeDtypeStruct
    out_shape = (
        shape((rows, WIN * count), BF16),
        shape((rows, hidden), BF16),
        shape((hidden // PARTS, WIN * count), F32),
        shape((32 * count, hidden), F32),
        shape((56, hidden), F32),
        shape((latent, hidden), F32),
        shape((2 * latent, hidden), F32),
        shape((8 * count, 128), F32),
        shape((8, 128), F32),
        shape((4, hidden), F32),
        shape((4, hidden), F32),
    )
    dma = pltpu.SemaphoreType.DMA
    scratch = (
        [pltpu.VMEM((4, size, 16, 128), F32) for _, size in grid.digits]
        + [dma((4, size - 1)) for _, size in grid.digits]
        + [dma((4, size - 1)) for _, size in grid.digits]
        + [pltpu.VMEM((2, 16 * SLOT_ROWS, 128), F32), pltpu.VMEM((16 * SLOT_ROWS, 128), F32)]
        + [pltpu.VMEM((CHANNELS, (16 >> t) * SLOT_ROWS, 128), F32) for t in range(STAGES)]
        + [dma((2,)), dma((CHANNELS, STAGES)), dma((CHANNELS, STAGES)), pltpu.SemaphoreType.REGULAR((2 * count + 2 - CHANNELS, STAGES))]
        + [pltpu.VMEM((REP_ROWS, 128), F32), pltpu.VMEM((REP_ROWS, 128), F32)]
        + [pltpu.VMEM((REP_ROWS >> (t + 1), 128), F32) for t in range(STAGES)]
        + [dma((4, STAGES))]
        + [
            pltpu.VMEM((3, rows, WIN), BF16),
            pltpu.VMEM((rows, WIN), F32),
            pltpu.VMEM((rows, hidden), F32),
            pltpu.VMEM((rows, hidden), BF16),
            pltpu.VMEM((rows, hidden), BF16),
            pltpu.VMEM((rows, hidden), BF16),
            pltpu.VMEM((rows, 2 * latent), BF16),
            pltpu.VMEM((rows, 128), F32),
            pltpu.VMEM((hidden, rows), BF16),
            pltpu.VMEM((2, rows, hidden), F32),
            pltpu.VMEM((SLOT_ROWS, 128), F32),
        ]
        + [dma((2, count)), dma((count,)), dma((4,)), dma, dma((3,))]
    )
    return pl.pallas_call(
        functools.partial(backward_kernel, grid, latent),
        out_shape=out_shape,
        in_specs=[hbm] * 10 + [vm] * 14,
        out_specs=[hbm] + [vm] * (len(out_shape) - 1),
        scratch_shapes=scratch,
        name="backward",
        compiler_params=pltpu.CompilerParams(
            collective_id=1, has_side_effects=True, vmem_limit_bytes=62 * 2**20
        ),
    )(
        cells_x,
        out_w,
        nrm0,
        nrm1,
        nrm2,
        nrm3,
        act1,
        act2,
        act3,
        xt,
        act4,
        zlat,
        head,
        noise,
        gid,
        ggroup,
        inv,
        out_b,
        w2,
        headt,
        d1,
        d2,
        gain,
        shift,
    )


def flat_shard(grid, flat, columns, rows_in_all):
    value = flat.reshape(rows_in_all // PARTS, columns)
    size = grid.n // PARTS
    if size > 1:
        groups = [list(range(size * p, size * p + size)) for p in range(PARTS)]
        value = lax.psum_scatter(
            value, ("cells", "rep"), scatter_dimension=0, axis_index_groups=groups, tiled=True
        )
    return value


def group_sum(grid, values):
    size = grid.n // PARTS
    if size > 1:
        groups = [list(range(size * p, size * p + size)) for p in range(PARTS)]
        values = lax.psum(values, ("cells", "rep"), axis_index_groups=groups)
    return values


def shards(
    grid,
    cells_x,
    latent_noise,
    group_ids,
    owner_table,
    owner_mask,
    enc_w1,
    enc_w2,
    head_w,
    head_b,
    dec_w1,
    dec_w2,
    out_w,
    out_b,
    bn_gain,
    bn_shift,
):
    cell_total = float(cells_x.shape[0] * grid.n)
    genes = cells_x.shape[1]
    hidden = enc_w2.shape[0]
    gid = group_ids.reshape(1, -1)
    headt = head_w.T
    *kept, offsets = call_forward(
        grid,
        cells_x,
        enc_w1.T,
        latent_noise,
        gid,
        owner_table,
        owner_mask,
        enc_w2,
        headt,
        head_b.reshape(1, -1),
        dec_w1,
        dec_w2,
        bn_gain,
        bn_shift,
    )
    g, gpre1, out25, enc_part, nar_part, d1_grad, headw_grad, outb_grad, headb_grad, grad_gain, grad_shift = call_backward(
        grid,
        kept,
        cells_x,
        out_w,
        latent_noise,
        gid,
        out_b.reshape(1, -1),
        enc_w2,
        headt,
        dec_w1,
        dec_w2,
        bn_gain,
        bn_shift,
    )
    product = lax.dot_general(gpre1, enc_w1, (((1,), (1,)), ((), ())), preferred_element_type=F32)
    grad_x = cell_total * (product - g[:, :genes].astype(F32))
    part = grid.me() // (grid.n // PARTS)
    each = genes * hidden // PARTS
    enc_flat = lax.dynamic_slice_in_dim(enc_part.reshape(-1), (genes * part) % PARTS * (hidden // PARTS), each)
    shard_enc = flat_shard(grid, enc_flat, FLAT_COLS, FLAT_ROWS)
    shard_out = flat_shard(grid, out25[:, :genes], FLAT_COLS, FLAT_ROWS)
    shard_narrow = flat_shard(grid, nar_part[: 2 * hidden // PARTS], NARROW_COLS, NARROW_ROWS)
    headw_grad, d1_grad, headb_grad, outb_grad = group_sum(
        grid,
        (headw_grad.T, d1_grad, headb_grad.reshape(-1)[: head_b.shape[0]], outb_grad.reshape(-1)[:genes]),
    )
    return (
        grad_x,
        shard_enc,
        shard_narrow,
        headw_grad,
        d1_grad,
        headb_grad,
        shard_out,
        outb_grad,
        grad_gain,
        grad_shift,
        offsets[None],
    )


def solution(mesh):
    grid = Slice(mesh.shape["cells"], mesh.shape["rep"])
    lines = P(("cells", "rep"), None)
    return jax.shard_map(
        functools.partial(shards, grid),
        mesh=mesh,
        in_specs=(lines, lines, P(("cells", "rep"))) + (P(),) * 12,
        out_specs=(lines, lines, lines, P(), P(), P(), lines, P(), P(), P(), P("cells", None, None)),
        check_vma=False,
    )
```

```python
import functools

import jax
import jax.numpy as jnp
from jax import lax
from jax.experimental import pallas as pl
from jax.experimental.pallas import tpu as pltpu
from jax.sharding import PartitionSpec as P

POP_DEV = 2
FLAT_COLS = 875
NARROW_COLS = 625
FLAT_ROWS = 6400
NARROW_ROWS = 2048

NORM_EPSILON = 1e-05
KL_WEIGHT = 5e-05
OFFSET_WEIGHT = 200.0

MESH_ID = pl.DeviceIdType.MESH
WIN = 1024
ROWS = 48
F32 = jnp.float32
BF16 = jnp.bfloat16


class Slice:
    def __init__(self, cells, rep):
        self.cells, self.rep = cells, rep
        self.n = cells * rep
        self.bits = self.n.bit_length() - 1
        self.digits = []
        low = 0
        while low < self.bits:
            width = min(3, self.bits - low)
            self.digits.append((low, 1 << width))
            low += width

    def me(self):
        return lax.axis_index("cells") * self.rep + lax.axis_index("rep")

    def place(self, index):
        return (index // self.rep, index % self.rep)


def entry_barrier(grid, peers):
    barrier = pltpu.get_barrier_semaphore()
    for peer in peers:
        pl.semaphore_signal(barrier, inc=1, device_id=grid.place(peer), device_id_type=MESH_ID)
    pl.semaphore_wait(barrier, len(peers))


def digit_peers(grid):
    me = grid.me()
    peers = []
    for low, size in grid.digits:
        rank = (me // (1 << low)) % size
        for k in range(1, size):
            other = (rank + k) % size
            peers.append(me + (other - rank) * (1 << low))
    return peers


class Gather:
    def __init__(self, grid, buffers, send_sems, recv_sems):
        self.grid, self.buffers, self.send_sems, self.recv_sems = grid, buffers, send_sems, recv_sems

    def rank(self, level):
        low, size = self.grid.digits[level]
        return (self.grid.me() // (1 << low)) % size

    def copy(self, level, slot, k, arriving=False):
        low, size = self.grid.digits[level]
        rank = self.rank(level)
        to = (rank + k) % size
        buffer = self.buffers[level].at[slot]
        return pltpu.make_async_remote_copy(
            src_ref=buffer.at[rank],
            dst_ref=buffer.at[(rank + size - k) % size if arriving else rank],
            send_sem=self.send_sems[level].at[slot, k - 1],
            recv_sem=self.recv_sems[level].at[slot, k - 1],
            device_id=self.grid.place(self.grid.me() + (to - rank) * (1 << low)),
            device_id_type=MESH_ID,
        )

    def start(self, level, slot):
        for k in range(1, self.grid.digits[level][1]):
            self.copy(level, slot, k).start()

    def wait(self, level, slot):
        for k in range(1, self.grid.digits[level][1]):
            self.copy(level, slot, k, arriving=True).wait_recv()

    def finish(self, level, slot):
        for k in range(1, self.grid.digits[level][1]):
            self.copy(level, slot, k).wait_send()

    def own(self, level, slot):
        return self.buffers[level].at[slot, self.rank(level)]


def put_row(ref, first, row, width):
    full = width // 128
    for c in range(full):
        ref[first + c : first + c + 1, :] = row[:, 128 * c : 128 * (c + 1)]
    rest = width - 128 * full
    if rest:
        ref[first + full : first + full + 1, 0:rest] = row[:, 128 * full : width]


def take_row(block, first, width):
    pieces = []
    for c in range(-(-width // 128)):
        pieces.append(block[first + c : first + c + 1, 0 : min(128, width - 128 * c)])
    return jnp.concatenate(pieces, axis=1)


def row_loop(rows, body, init):
    steps = rows // ROWS

    def step(i, carry):
        return body(pl.ds(pl.multiple_of(i * ROWS, ROWS), ROWS), carry)

    return lax.fori_loop(0, steps, step, init)


def column_sum(value):
    return jnp.sum(value, axis=0, keepdims=True)


PARTS = 32


def batch_norm(pre, nrm_out, act_out, gather, slot, gain_row, shift_row, inv_out, idle):
    rows, width = pre.shape
    total = row_loop(rows, lambda r, c: c + column_sum(pre[r, :]), jnp.zeros((1, width), F32))
    mean = total * (1.0 / rows)

    def squares(r, c):
        d = pre[r, :] - mean
        return c + column_sum(d * d)

    square = row_loop(rows, squares, jnp.zeros((1, width), F32))
    own = gather.own(0, slot)
    put_row(own, 0, mean, width)
    put_row(own, 8, square, width)
    count = float(rows)
    levels = len(gather.grid.digits)
    for level in range(levels):
        size = gather.grid.digits[level][1]
        gather.start(level, slot)
        idle(level)
        gather.wait(level, slot)
        buffer = gather.buffers[level].at[slot]
        means = [buffer[g, 0:8, :] for g in range(size)]
        merged = sum(means[1:], means[0]) * (1.0 / size)
        spread = sum([buffer[g, 8:16, :] for g in range(1, size)], buffer[0, 8:16, :])
        between = sum([(m - merged) * (m - merged) for m in means[1:]], (means[0] - merged) * (means[0] - merged))
        spread = spread + count * between
        count = count * size
        if level + 1 < levels:
            own = gather.own(level + 1, slot)
            own[0:8, :] = merged
            own[8:16, :] = spread
    inv = lax.rsqrt(spread * (1.0 / count) + NORM_EPSILON)
    mean = take_row(merged, 0, width)
    inv = take_row(inv, 0, width)
    inv_out[...] = inv

    def write(r, c):
        nrm = (pre[r, :] - mean) * inv
        nrm_out[r, :] = nrm
        value = gain_row * nrm + shift_row
        act_out[r, :] = (value * jax.nn.sigmoid(value)).astype(BF16)
        return c

    row_loop(rows, write, 0)


def nt(left, right):
    return lax.dot_general(left, right, (((1,), (1,)), ((), ())), preferred_element_type=F32)


def nn(left, right):
    return lax.dot_general(left, right, (((1,), (0,)), ((), ())), preferred_element_type=F32)


def tn(left, right):
    return lax.dot_general(left, right, (((0,), (0,)), ((), ())), preferred_element_type=F32)


def exact(left, right, dims):
    return lax.dot_general(
        left, right, (dims, ((), ())), precision=lax.Precision.HIGHEST, preferred_element_type=F32
    )


WIDE = 1024


def windows(width, size=WIN):
    return [(s, min(size, width - s)) for s in range(0, width, size)]


def part_of(full, tail, i):
    return full.at[i] if i < full.shape[0] else tail


def forward_kernel(
    grid,
    table_ref,
    mask_ref,
    x_hbm,
    w1_hbm,
    noise_ref,
    gid_ref,
    w2_ref,
    head_ref,
    headb_ref,
    d1_ref,
    d2_ref,
    gain_ref,
    shift_ref,
    nrm0,
    nrm1,
    nrm2,
    nrm3,
    inv_out,
    act1,
    act2,
    zlat,
    act3,
    act4,
    head_out,
    ggroup_out,
    xt_out,
    offsets_out,
    x_all,
    xt,
    w_win,
    w_tail,
    pre,
    moments,
    *rest,
):
    levels = len(grid.digits)
    small = rest[:levels]
    wide = rest[levels : 2 * levels]
    s_send, s_recv, g_send, g_recv = (
        rest[2 * levels : 3 * levels],
        rest[3 * levels : 4 * levels],
        rest[4 * levels : 5 * levels],
        rest[5 * levels : 6 * levels],
    )
    in_sems, xt_sems = rest[6 * levels :]
    gather = Gather(grid, small, s_send, s_recv)
    group_gather = Gather(grid, wide, g_send, g_recv)
    latent = d1_ref.shape[0]
    genes = x_hbm.shape[1]
    spans = windows(genes, WIDE)

    loads = []
    for i, (s, size) in enumerate(spans):
        a = pltpu.make_async_copy(x_hbm.at[:, pl.ds(s, size)], x_all.at[:, pl.ds(s, size)], in_sems.at[0, i])
        b = pltpu.make_async_copy(w1_hbm.at[:, pl.ds(s, size)], part_of(w_win, w_tail, i), in_sems.at[1, i])
        a.start()
        b.start()
        loads.append((a, b))
    entry_barrier(grid, digit_peers(grid))

    for i, (s, size) in enumerate(spans):
        loads[i][0].wait()
        loads[i][1].wait()
        part = nt(x_all[:, s : s + size], part_of(w_win, w_tail, i)[...])
        pre[...] = part if i == 0 else pre[...] + part

    starts = [(genes * j) // PARTS for j in range(PARTS)]
    parts_left = list(range(PARTS))

    def save(j):
        return pltpu.make_async_copy(xt.at[j], xt_out.at[j], xt_sems.at[j])

    def transpose(level):
        for j in parts_left[: -(-PARTS // 6)]:
            at = starts[j] // 128 * 128
            size = min(384, genes - at)
            lane = lax.broadcasted_iota(jnp.int32, (xt.shape[1], size), 1)
            line = lax.broadcasted_iota(jnp.int32, (xt.shape[1], size), 0)
            select = jnp.where(lane == line + (starts[j] - at), 1.0, 0.0).astype(BF16)
            xt[j] = nt(select, x_all[:, at : at + size]).astype(BF16)
            save(j).start()
            parts_left.remove(j)

    def norm(k, nrm, act, idle=transpose):
        batch_norm(
            pre,
            nrm,
            act,
            gather,
            k,
            gain_ref[k : k + 1, :],
            shift_ref[k : k + 1, :],
            inv_out.at[k : k + 1, :],
            idle,
        )

    norm(0, nrm0, act1)
    pre[...] = nn(act1[...], w2_ref[...])
    norm(1, nrm1, act2)
    head = nt(act2[...], head_ref[...]) + headb_ref[...]
    head_out[...] = head
    mu = head[:, 0:latent]
    logvar = head[:, latent : 2 * latent]
    zlat[...] = (mu + jnp.exp(0.5 * logvar) * noise_ref[...].T).astype(BF16)

    groups = ggroup_out.shape[0]
    pops = groups // 2
    cells_here = gid_ref.shape[1]
    member = (lax.broadcasted_iota(jnp.int32, (groups, cells_here), 0) == gid_ref[...]).astype(F32)
    own = group_gather.own(0, 0)
    own[:, 0:latent] = exact(member, mu, ((1,), (0,)))
    own[:, latent : latent + 1] = jnp.sum(member, axis=1, keepdims=True)
    group_gather.start(0, 0)

    pre[...] = nn(zlat[...], d1_ref[...])
    norm(2, nrm2, act3)

    def group_level(level):
        group_gather.wait(level, 0)
        size = grid.digits[level][1]
        buffer = wide[level].at[0]
        total = sum([buffer[g] for g in range(1, size)], buffer[0])
        if level + 1 < levels:
            group_gather.own(level + 1, 0)[...] = total
            group_gather.start(level + 1, 0)
            return
        counted = jnp.maximum(total[:, latent : latent + 1], 1.0)
        moments[...] = total / counted
        odd, even = pl.ds(1, pops, stride=2), pl.ds(0, pops, stride=2)
        offset = moments[odd, :] - moments[even, :]
        centre = jnp.sum(offset, axis=0, keepdims=True) * (1.0 / pops)
        grad_offset = (2.0 * OFFSET_WEIGHT / pops) * (offset - centre)
        row = lax.axis_index("cells")
        slots = offsets_out.shape[0]
        lane = lax.broadcasted_iota(jnp.int32, (1, pops), 1)
        picks = jnp.concatenate(
            [jnp.where(lane == table_ref[s, row], mask_ref[s, row].astype(F32), 0.0) for s in range(slots)], axis=0
        )
        offsets_out[...] = exact(picks, offset, ((1,), (0,)))[:, 0:latent]
        moments[odd, :] = grad_offset
        moments[even, :] = -grad_offset
        ggroup_out[...] = moments[...] / counted

    group_level(0)
    pre[...] = nn(act3[...], d2_ref[...])
    norm(3, nrm3, act4, lambda level: group_level(level) if level else None)
    while parts_left:
        transpose(0)

    for j in range(PARTS):
        save(j).wait()
    for level in range(levels):
        for k in range(4):
            gather.finish(level, k)
        group_gather.finish(level, 0)


XT_ROWS = 224


def call_forward(grid, cells_x, w1t, noise, gid, table, mask, w2, headt, headb, d1, d2, gain, shift):
    rows, genes = cells_x.shape
    hidden = w2.shape[0]
    latent = d1.shape[0]
    groups = 2 * POP_DEV * grid.cells
    spans = windows(genes, WIDE)
    count = len(spans)
    levels = len(grid.digits)
    vm = pl.BlockSpec(memory_space=pltpu.VMEM)
    hbm = pl.BlockSpec(memory_space=pl.ANY)
    sm = pl.BlockSpec(memory_space=pltpu.SMEM)
    wide_f = jax.ShapeDtypeStruct((rows, hidden), F32)
    wide_b = jax.ShapeDtypeStruct((rows, hidden), BF16)
    out_shape = (
        wide_f,
        wide_f,
        wide_f,
        wide_f,
        jax.ShapeDtypeStruct((4, hidden), F32),
        wide_b,
        wide_b,
        jax.ShapeDtypeStruct((rows, latent), BF16),
        wide_b,
        wide_b,
        jax.ShapeDtypeStruct((rows, 2 * latent), F32),
        jax.ShapeDtypeStruct((groups, 128), F32),
        jax.ShapeDtypeStruct((PARTS, XT_ROWS, rows), BF16),
        jax.ShapeDtypeStruct((table.shape[0], latent), F32),
    )
    scratch = (
        [
            pltpu.VMEM((rows, genes), BF16),
            pltpu.VMEM((PARTS, XT_ROWS, rows), BF16),
            pltpu.VMEM((count - 1, hidden, WIDE), BF16),
            pltpu.VMEM((hidden, spans[-1][1]), BF16),
            pltpu.VMEM((rows, hidden), F32),
            pltpu.VMEM((groups, 128), F32),
        ]
        + [pltpu.VMEM((4, size, 16, 128), F32) for _, size in grid.digits]
        + [pltpu.VMEM((1, size, groups, 128), F32) for _, size in grid.digits]
        + [pltpu.SemaphoreType.DMA((4, size - 1)) for _, size in grid.digits]
        + [pltpu.SemaphoreType.DMA((4, size - 1)) for _, size in grid.digits]
        + [pltpu.SemaphoreType.DMA((1, size - 1)) for _, size in grid.digits]
        + [pltpu.SemaphoreType.DMA((1, size - 1)) for _, size in grid.digits]
        + [pltpu.SemaphoreType.DMA((2, count)), pltpu.SemaphoreType.DMA((PARTS,))]
    )
    return pl.pallas_call(
        functools.partial(forward_kernel, grid),
        out_shape=out_shape,
        in_specs=[sm, sm, hbm, hbm] + [vm] * 9,
        out_specs=[vm] * (len(out_shape) - 2) + [hbm, vm],
        scratch_shapes=scratch,
        name="forward",
        compiler_params=pltpu.CompilerParams(
            collective_id=0, has_side_effects=True, vmem_limit_bytes=60 * 2**20
        ),
    )(table, mask, cells_x, w1t, noise, gid, w2, headt, headb, d1, d2, gain, shift)


ORDERS = (
    (0, 1, 2, 3, 4),
    (0, 2, 3, 1, 4),
    (0, 1, 2, 3, 4),
    (0, 2, 3, 1, 4),
    (0, 2, 3, 1, 4),
    (0, 1, 2, 3, 4),
    (0, 1, 2, 3, 4),
    (0, 1, 3, 2, 4),
    (0, 2, 3, 1, 4),
    (0, 2, 3, 1, 4),
    (0, 1, 2, 3, 4),
    (0, 1, 2, 3, 4),
    (0, 1, 3, 2, 4),
    (0, 2, 3, 1, 4),
    (0, 2, 3, 1, 4),
    (0, 1, 2, 3, 4),
)
C, U, L, S, F, X = range(6)
PLAN = (
    (C,),
    (U, 0),
    (C,),
    (C,),
    (L, 0),
    (S, 0, 1, 0, 2),
    (S, 0, 1, 2, 1),
    (U, 1),
    (C,),
    (S, 0, 1, 3, 1),
    (C,),
    (L, 1),
    (S, 0, 1, 4, 2),
    (S, 1, 1, 0, 2),
    (U, 2),
    (C,),
    (S, 0, 1, 6, 1),
    (S, 1, 1, 2, 1),
    (C,),
    (L, 2),
    (S, 0, 1, 7, 1),
    (S, 2, 1, 0, 1),
    (S, 1, 1, 3, 2),
    (U, 3),
    (C,),
    (S, 2, 1, 1, 1),
    (S, 1, 1, 5, 1),
    (C,),
    (F, 0, 1),
    (S, 2, 1, 2, 2),
    (S, 1, 1, 6, 2),
    (L, 3),
    (C,),
    (U, 4),
    (S, 2, 1, 4, 1),
    (S, 0, 2, 0, 1),
    (C,),
    (C,),
    (F, 1, 1),
    (S, 2, 1, 5, 2),
    (S, 0, 2, 1, 2),
    (S, 1, 2, 0, 2),
    (L, 4),
    (C,),
    (S, 2, 1, 7, 1),
    (S, 0, 2, 3, 1),
    (S, 1, 2, 2, 1),
    (U, 5),
    (C,),
    (S, 3, 1, 0, 1),
    (S, 1, 2, 3, 1),
    (C,),
    (C,),
    (S, 3, 1, 1, 4),
    (F, 0, 2),
    (S, 0, 3, 0, 2),
    (F, 2, 1),
    (L, 5),
    (F, 1, 2),
    (S, 1, 3, 0, 2),
    (U, 6),
    (C,),
    (S, 5, 1, 0, 3),
    (S, 3, 1, 5, 2),
    (F, 0, 3),
    (S, 0, 4, 0, 1),
    (L, 6),
    (F, 1, 3),
    (S, 1, 4, 0, 1),
    (C,),
    (C,),
    (C,),
    (S, 5, 1, 3, 4),
    (S, 3, 1, 7, 1),
    (S, 2, 2, 0, 3),
    (F, 0, 4),
    (F, 1, 4),
    (C,),
    (S, 5, 1, 7, 1),
    (S, 2, 2, 3, 1),
    (F, 3, 1),
    (S, 3, 2, 0, 2),
    (S, 3, 2, 2, 1),
    (C,),
    (S, 4, 1, 0, 1),
    (S, 3, 2, 3, 1),
    (C,),
    (C,),
    (S, 4, 1, 1, 4),
    (F, 2, 2),
    (S, 2, 3, 0, 2),
    (F, 5, 1),
    (F, 3, 2),
    (S, 3, 3, 0, 2),
    (C,),
    (S, 6, 1, 0, 3),
    (S, 4, 1, 5, 1),
    (F, 2, 3),
    (S, 2, 4, 0, 1),
    (F, 3, 3),
    (S, 4, 1, 6, 1),
    (S, 3, 4, 0, 1),
    (C,),
    (C,),
    (C,),
    (S, 6, 1, 3, 4),
    (S, 4, 1, 7, 1),
    (S, 5, 2, 0, 3),
    (F, 2, 4),
    (F, 3, 4),
    (C,),
    (S, 6, 1, 7, 1),
    (S, 5, 2, 3, 1),
    (F, 4, 1),
    (S, 4, 2, 0, 2),
    (S, 4, 2, 2, 1),
    (C,),
    (S, 4, 2, 3, 1),
    (U, 7),
    (F, 5, 2),
    (S, 5, 3, 0, 2),
    (F, 6, 1),
    (S, 6, 2, 0, 4),
    (X, 0),
    (F, 4, 2),
    (S, 4, 3, 0, 2),
    (X, 1),
    (L, 7),
    (S, 7, 1, 0, 3),
    (U, 8),
    (F, 5, 3),
    (S, 7, 1, 3, 1),
    (S, 5, 4, 0, 1),
    (X, 2),
    (X, 3),
    (F, 4, 3),
    (S, 7, 1, 4, 1),
    (S, 4, 4, 0, 1),
    (L, 8),
    (S, 7, 1, 5, 1),
    (S, 8, 1, 0, 5),
    (U, 9),
    (F, 5, 4),
    (S, 7, 1, 6, 1),
    (S, 8, 1, 5, 2),
    (F, 6, 2),
    (S, 6, 3, 0, 2),
    (X, 4),
    (X, 5),
    (X, 6),
    (F, 4, 4),
    (S, 7, 1, 7, 1),
    (S, 8, 1, 7, 1),
    (L, 9),
    (S, 9, 1, 0, 1),
    (U, 10),
    (X, 7),
    (F, 6, 3),
    (S, 9, 1, 1, 2),
    (S, 6, 4, 0, 1),
    (X, 8),
    (X, 9),
    (L, 10),
    (S, 10, 1, 0, 4),
    (S, 9, 1, 3, 2),
    (X, 10),
    (F, 7, 1),
    (S, 10, 1, 4, 1),
    (S, 7, 2, 0, 4),
    (F, 8, 1),
    (S, 9, 1, 5, 1),
    (X, 11),
    (F, 6, 4),
    (S, 10, 1, 5, 1),
    (S, 8, 2, 0, 1),
    (U, 11),
    (X, 12),
    (X, 13),
    (S, 10, 1, 6, 2),
    (S, 9, 1, 6, 2),
    (S, 8, 2, 1, 3),
    (L, 11),
    (U, 12),
    (F, 7, 2),
    (S, 7, 3, 0, 2),
    (S, 11, 1, 0, 2),
    (L, 12),
    (S, 11, 1, 2, 1),
    (S, 11, 1, 3, 1),
    (F, 9, 1),
    (S, 9, 2, 0, 4),
    (F, 8, 2),
    (S, 11, 1, 4, 1),
    (F, 10, 1),
    (S, 10, 2, 0, 3),
    (U, 13),
    (S, 11, 1, 5, 1),
    (S, 10, 2, 3, 1),
    (F, 7, 3),
    (S, 7, 4, 0, 1),
    (S, 11, 1, 6, 1),
    (L, 13),
    (U, 14),
    (S, 11, 1, 7, 1),
    (S, 8, 3, 0, 1),
    (F, 9, 2),
    (S, 8, 3, 1, 1),
    (S, 13, 1, 0, 4),
    (L, 14),
    (S, 9, 3, 0, 1),
    (S, 13, 1, 4, 1),
    (F, 10, 2),
    (S, 10, 3, 0, 2),
    (F, 7, 4),
    (S, 9, 3, 1, 1),
    (S, 12, 1, 0, 1),
    (S, 13, 1, 5, 2),
    (F, 11, 1),
    (F, 10, 3),
    (S, 10, 4, 0, 1),
    (S, 12, 1, 1, 1),
    (S, 13, 1, 7, 1),
    (U, 15),
    (F, 8, 3),
    (S, 12, 1, 2, 1),
    (S, 11, 2, 0, 1),
    (S, 8, 4, 0, 1),
    (S, 12, 1, 3, 1),
    (S, 11, 2, 1, 1),
    (F, 10, 4),
    (L, 15),
    (S, 11, 2, 2, 1),
    (S, 12, 1, 4, 1),
    (F, 9, 3),
    (S, 9, 4, 0, 1),
    (F, 8, 4),
    (S, 12, 1, 5, 1),
    (S, 11, 2, 3, 1),
    (F, 13, 1),
    (S, 12, 1, 6, 1),
    (S, 14, 1, 0, 1),
    (S, 13, 2, 0, 4),
    (F, 9, 4),
    (S, 12, 1, 7, 1),
    (S, 14, 1, 1, 1),
    (F, 11, 2),
    (S, 14, 1, 2, 3),
    (S, 11, 3, 0, 2),
    (S, 15, 1, 0, 3),
    (F, 13, 2),
    (S, 15, 1, 3, 1),
    (S, 14, 1, 5, 1),
    (F, 12, 1),
    (S, 15, 1, 4, 1),
    (S, 14, 1, 6, 1),
    (S, 12, 2, 0, 4),
    (F, 11, 3),
    (S, 15, 1, 5, 1),
    (S, 14, 1, 7, 1),
    (S, 11, 4, 0, 1),
    (F, 12, 2),
    (S, 15, 1, 6, 2),
    (S, 13, 3, 0, 2),
    (S, 12, 3, 0, 2),
    (F, 14, 1),
    (S, 14, 2, 0, 4),
    (F, 11, 4),
    (F, 12, 3),
    (S, 12, 4, 0, 1),
    (F, 15, 1),
    (S, 15, 2, 0, 4),
    (F, 13, 3),
    (S, 13, 4, 0, 1),
    (F, 14, 2),
    (S, 14, 3, 0, 2),
    (F, 15, 2),
    (S, 15, 3, 0, 2),
    (F, 12, 4),
    (F, 14, 3),
    (S, 14, 4, 0, 1),
    (F, 13, 4),
    (F, 15, 3),
    (S, 15, 4, 0, 1),
    (F, 14, 4),
    (F, 15, 4),
)
CHANNELS = 4
STAGES = 5
SLOT_ROWS = 200


class Scatter:
    def __init__(self, grid, total, stage, low, landing, stage_sems, send_sems, recv_sems, credits):
        self.grid, self.total = grid, total
        self.stage, self.low, self.landing = stage, low, landing
        self.stage_sems, self.send_sems, self.recv_sems, self.credits = stage_sems, send_sems, recv_sems, credits
        self.shift = grid.bits - STAGES
        self.rows = {}

    def bit(self, b):
        return (self.grid.me() // (1 << (b + self.shift))) % 2

    def partner(self, b):
        return self.grid.place(self.grid.me() + (1 - 2 * self.bit(b)) * (1 << (b + self.shift)))

    def part(self, q, k):
        out = 0
        for t, b in enumerate(ORDERS[q]):
            own = self.bit(b)
            out = out + (1 << b) * ((1 - own) if (k >> (STAGES - 1 - t)) & 1 else own)
        return out

    def send(self, q, t, first=0, number=None):
        channel, rows = q % CHANNELS, self.rows[q]
        slots = 16 >> t
        at, size = first * rows, (slots if number is None else number) * rows
        if t == 0:
            source, sem = self.stage.at[q % 2, at : at + size], self.stage_sems.at[q % 2]
        else:
            start = slots * rows + at
            source, sem = self.landing[t - 1].at[channel, start : start + size], self.send_sems.at[channel, t]
        return pltpu.make_async_remote_copy(
            src_ref=source,
            dst_ref=self.landing[t].at[channel, at : at + size],
            send_sem=sem,
            recv_sem=self.recv_sems.at[channel, t],
            device_id=self.partner(ORDERS[q][t]),
            device_id_type=MESH_ID,
        )

    def feed(self, q, t, first, number):
        if first == 0 and q >= CHANNELS:
            pl.semaphore_wait(self.credits.at[q - CHANNELS, t], 1)
        self.send(q, t, first, number).start()

    def free(self, q, t):
        if q + CHANNELS < self.total:
            pl.semaphore_signal(
                self.credits.at[q, t],
                inc=1,
                device_id=self.partner(ORDERS[q + CHANNELS][t]),
                device_id_type=MESH_ID,
            )

    def upper(self, q, rows, fill):
        self.rows[q] = rows
        if q >= 2:
            self.send(q - 2, 0).wait_send()
        fill(self.stage.at[q % 2], True)
        self.feed(q, 0, 0, 16)
        fill(self.low, False)

    def lower(self, q):
        channel, rows = q % CHANNELS, self.rows[q]
        self.send(q, 0).wait_recv()
        mine = self.landing[0].at[channel]

        def add(i, c):
            r = pl.ds(pl.multiple_of(i * rows, 8), rows)
            mine[r, :] += self.low[r, :]
            return c

        lax.fori_loop(0, 16, add, 0)

    def fold(self, q, t):
        channel, rows = q % CHANNELS, self.rows[q]
        self.send(q, t).wait_recv()
        mine, before = self.landing[t].at[channel], self.landing[t - 1].at[channel]

        def add(i, c):
            r = pl.ds(pl.multiple_of(i * rows, 8), rows)
            mine[r, :] += before[r, :]
            return c

        lax.fori_loop(0, 16 >> t, add, 0)
        self.send(q, t).wait_send()
        self.free(q, t - 1)

    def last(self, q, done):
        channel, rows = q % CHANNELS, self.rows[q]
        t = STAGES - 1
        self.send(q, t).wait_recv()
        done(self.landing[t][channel, 0:rows, :] + self.landing[t - 1][channel, 0:rows, :])
        self.send(q, t).wait_send()
        self.free(q, t - 1)
        self.free(q, t)


class Spread:
    def __init__(self, scatter, block, landing, whole, sems):
        self.scatter, self.block, self.landing, self.whole, self.sems = scatter, block, landing, whole, sems
        self.rows = block.shape[0]

    def begin(self, t):
        out = 0
        for i in range(t):
            out = out + self.scatter.bit(i) * (self.rows >> (i + 1))
        return out

    def halving(self, t):
        size = self.rows >> (t + 1)
        at = self.begin(t) + (1 - self.scatter.bit(t)) * size
        return pltpu.make_async_remote_copy(
            src_ref=self.block.at[pl.ds(pl.multiple_of(at, 8), size)],
            dst_ref=self.landing[t],
            send_sem=self.sems.at[0, t],
            recv_sem=self.sems.at[1, t],
            device_id=self.scatter.partner(t),
            device_id_type=MESH_ID,
        )

    def doubling(self, t, arriving=False):
        size = self.rows >> (t + 1)
        at = self.begin(t + 1)
        there = self.begin(t) + (1 - self.scatter.bit(t)) * size if arriving else at
        return pltpu.make_async_remote_copy(
            src_ref=self.whole.at[pl.ds(pl.multiple_of(at, 8), size)],
            dst_ref=self.whole.at[pl.ds(pl.multiple_of(there, 8), size)],
            send_sem=self.sems.at[2, t],
            recv_sem=self.sems.at[3, t],
            device_id=self.scatter.partner(t),
            device_id_type=MESH_ID,
        )

    def step(self, i):
        if i == 0:
            self.halving(0).start()
        elif i <= STAGES:
            t = i - 1
            self.halving(t).wait_recv()
            size = self.rows >> (t + 1)
            r = pl.ds(pl.multiple_of(self.begin(t + 1), 8), size)
            target = self.whole if i == STAGES else self.block
            target[r, :] = self.block[r, :] + self.landing[t][...]
            self.halving(t).wait_send()
            if i < STAGES:
                self.halving(t + 1).start()
            else:
                self.doubling(t).start()
        else:
            t = 2 * STAGES - i
            self.doubling(t, True).wait_recv()
            self.doubling(t).wait_send()
            if t > 0:
                self.doubling(t - 1).start()


def one_hot(rows, target):
    lane = lax.broadcasted_iota(jnp.int32, (rows, target.shape[1]), 0)
    return jnp.where(lane == target, 1.0, 0.0).astype(BF16)


def column_parts(width, size):
    column = lax.broadcasted_iota(jnp.int32, (1, width), 1)
    part = jnp.zeros((1, width), jnp.int32)
    for m in range(1, width // size):
        part = part + jnp.where(column >= m * size, 1, 0)
    return column, part


def slot_of(scatter, q, bits, parts, part):
    order = [b for b in ORDERS[q] if b in bits]
    slot = jnp.zeros_like(part)
    for value in range(parts):
        at = 0
        for t, b in enumerate(order):
            own = scatter.bit(b)
            weight = 1 << (len(order) - 1 - t)
            at = at + weight * ((1 - own) if (value >> bits.index(b)) & 1 else own)
        slot = jnp.where(part == value, at, slot)
    return slot


def sum_blocks(gather, slot):
    levels = len(gather.grid.digits)
    yield
    for level in range(levels):
        gather.start(level, slot)
        if level < 2:
            yield
        gather.wait(level, slot)
        size = gather.grid.digits[level][1]
        buffer = gather.buffers[level].at[slot]
        total = sum([buffer[g] for g in range(1, size)], buffer[0])
        if level + 1 < levels:
            gather.own(level + 1, slot)[...] = total
    return total


def norm_gradient(grad, nrm, out, gather, slot, gain_row, shift_row, inv_row, scale, gain_out, shift_out):
    rows, width = grad.shape

    def gate(r, carry):
        n = nrm[r, :]
        value = gain_row * n + shift_row
        sig = jax.nn.sigmoid(value)
        g = grad[r, :] * sig * (1.0 + value * (1.0 - sig))
        grad[r, :] = g
        return carry[0] + column_sum(g), carry[1] + column_sum(g * n)

    zero = jnp.zeros((1, width), F32)
    shift_sum, gain_sum = row_loop(rows, gate, (zero, zero))
    own = gather.own(0, slot)
    put_row(own, 0, shift_sum, width)
    put_row(own, 8, gain_sum, width)
    total = yield from sum_blocks(gather, slot)
    shift_sum = take_row(total, 0, width)
    gain_sum = take_row(total, 8, width)
    shift_out[...] = shift_sum
    gain_out[...] = gain_sum
    factor = gain_row * inv_row
    shift_mean = shift_sum * scale
    gain_mean = gain_sum * scale

    def write(r, c):
        out[r, :] = (factor * (grad[r, :] - shift_mean - nrm[r, :] * gain_mean)).astype(BF16)
        return c

    row_loop(rows, write, 0)


D1_ROWS = 104
GX = 512
REP_ROWS = 2304


def backward_kernel(
    grid,
    latent,
    x_hbm,
    w1_hbm,
    outw_hbm,
    nrm_hbm0,
    nrm_hbm1,
    nrm_hbm2,
    nrm_hbm3,
    act1_hbm,
    act2_hbm,
    act3_hbm,
    xt_hbm,
    act4_ref,
    zlat_ref,
    head_ref_in,
    noise_ref,
    gid_ref,
    ggroup_ref,
    inv_ref,
    outb_ref,
    w2_ref,
    head_ref,
    d1_ref,
    d2_ref,
    gain_ref,
    shift_ref,
    g_out,
    gx_out,
    out25,
    enc_part,
    nar_part,
    d1_out,
    headw_out,
    outb_out,
    headb_out,
    gain_out,
    shift_out,
    *rest,
):
    levels = len(grid.digits)
    rest = list(rest)

    def take(n):
        got = rest[:n]
        del rest[:n]
        return got

    small, s_send, s_recv = take(levels), take(levels), take(levels)
    stage, low, *landing = take(2 + STAGES)
    stage_sems, send_sems, recv_sems, credits = take(4)
    rep_block, rep_whole, *rep_landing = take(2 + STAGES)
    (rep_sems,) = take(1)
    g_win, wide, gact, gpre4, gpre3, gpre2, gpre1, ghead, gcell, lhs, nrm_buf, fin = take(12)
    distinct = sorted(set(ORDERS[: -(-x_hbm.shape[1] // WIN)]))
    lhs_at = [distinct.index(o) if o in distinct else None for o in ORDERS]
    picked = lhs.at[0, 0:512]
    in_sems, g_sems, nrm_sems, xt_sem, act_sems, gx_sems = take(6)

    rows, genes = x_hbm.shape
    hidden = w2_ref.shape[0]
    spans = windows(genes)
    count = len(spans)
    cell_total = float(rows * grid.n)
    total = 2 * count + 2
    gather = Gather(grid, small, s_send, s_recv)
    first = count
    scatter = Scatter(grid, total, stage, low, landing, stage_sems, send_sems, recv_sems, credits)
    spread = Spread(scatter, rep_block, rep_landing, rep_whole, rep_sems)
    rep_outb = 7 * (D1_ROWS + 2 * latent)
    rep_headb = rep_outb + 8 * count

    entry_barrier(grid, digit_peers(grid))
    nrm_loads = {
        k: pltpu.make_async_copy(ref, nrm_buf.at[(k + 1) % 2], nrm_sems.at[k])
        for k, ref in enumerate((nrm_hbm0, nrm_hbm1, nrm_hbm2, nrm_hbm3))
    }
    nrm_loads[3].start()
    nrm_loads[2].start()


    def out_fill(s):
        buffer = g_win.at[s % 3]

        def fill(target, is_upper):
            first = hidden // 2 if is_upper else 0
            part = nn(lhs[lhs_at[s], first : first + hidden // 2, :], buffer[...])
            for c in range(WIN // 128):
                target[pl.ds(c, hidden // 2, stride=8), :] = part[:, 128 * c : 128 * (c + 1)]

        return fill

    def out_lhs(q):
        if ORDERS[q] in ORDERS[:q]:
            return
        mine = lhs.at[lhs_at[q]]
        column, part = column_parts(hidden, hidden // PARTS)
        slot = slot_of(scatter, q, (0, 1, 2, 3, 4), PARTS, part)
        target = column + (hidden // PARTS) * (slot - part)
        block = hidden // 5

        def some(i, c):
            at = pl.multiple_of(i * block, block)
            mine[pl.ds(at, block), :] = nt(one_hot(block, target - at), act4_ref[...]).astype(BF16)
            return c

        lax.fori_loop(0, 5, some, 0)

    def out_done(s):
        def done(value):
            fin[...] = value
            for c in range(WIN // 128):
                out25[:, WIN * s + 128 * c : WIN * s + 128 * (c + 1)] = fin[pl.ds(c, hidden // PARTS, stride=8), :]

        return done

    done = {s: out_done(s) for s in range(count)}
    pieces = {}
    for s in range(count):
        pieces[s] = (SLOT_ROWS, out_fill(s))

    plan = list(PLAN)

    def run(chain, more=None, cells=None):
        while plan:
            what, *which = plan[0]
            if what == C:
                if next(chain, None) is None:
                    return
            elif what == U:
                if which[0] < count:
                    out_lhs(which[0])
                scatter.upper(which[0], *pieces[which[0]])
            elif what == L:
                scatter.lower(which[0])
            elif what == S:
                scatter.feed(*which)
            elif what == X:
                cells(*which)
            elif which[1] < STAGES - 1:
                scatter.fold(*which)
            else:
                scatter.last(which[0], done[which[0]])
            del plan[0]
            if more is not None:
                more()

    def output_layer(w_ring, w_tail, x_ring, x_tail):
        def load(s):
            at, size = spans[s]
            tail = s == count - 1
            return (
                pltpu.make_async_copy(
                    outw_hbm.at[:, pl.ds(at, size)], w_tail if tail else w_ring.at[s % 3], in_sems.at[0, s]
                ),
                pltpu.make_async_copy(
                    x_hbm.at[:, pl.ds(at, size)], x_tail if tail else x_ring.at[s % 2], in_sems.at[1, s]
                ),
            )

        def save(s):
            return pltpu.make_async_copy(g_win.at[s % 3], g_out.at[:, pl.ds(WIN * s, WIN)], g_sems.at[s])

        def layers():
            for s in range(2):
                for copy in load(s):
                    copy.start()
            for s in range(count):
                yield from layer(s)

        def layer(s):
            at, size = spans[s]
            tail = s == count - 1
            w = w_tail if tail else w_ring.at[s % 3]
            x = x_tail if tail else x_ring.at[s % 2]
            for copy in load(s):
                copy.wait()
            wide[:, 0:size] = nn(act4_ref[...], w[...])
            bias = outb_ref[:, at : at + size]
            if s >= 3:
                save(s - 3).wait()
            g = g_win.at[s % 3]

            def residual(r, c):
                value = wide[r, 0:size] + bias - x[r, :].astype(F32)
                value = (value * (2.0 / cell_total)).astype(BF16)
                g[r, 0:size] = value
                return c + column_sum(value.astype(F32))

            put_row(rep_block, rep_outb + 8 * s, row_loop(rows, residual, jnp.zeros((1, size), F32)), size)
            if size < WIN:
                g[:, size:WIN] = jnp.zeros((rows, WIN - size), BF16)
            save(s).start()
            if s + 2 < count:
                for copy in load(s + 2):
                    copy.start()
            yield 0
            part = nt(g[:, 0:size], w[...])
            gact[...] = part if s == 0 else gact[...] + part
            yield 0

        run(layers())
        for s in range(count - 3, count):
            save(s).wait()

    pl.run_scoped(
        output_layer,
        pltpu.VMEM((3, hidden, WIN), BF16),
        pltpu.VMEM((hidden, spans[-1][1]), BF16),
        pltpu.VMEM((2, rows, WIN), BF16),
        pltpu.VMEM((rows, spans[-1][1]), BF16),
    )


    def pack(target, at, source, row, height):
        full = hidden // 128
        for c in range(full):
            target[pl.ds(pl.multiple_of(at + height * c, 8), height), :] = source[
                pl.ds(row, height), 128 * c : 128 * (c + 1)
            ]
        rest_width = hidden - 128 * full
        pieces = [source[pl.ds(row + 8 * i, 8), 128 * full : hidden] for i in range(height // 8)]
        target[pl.ds(pl.multiple_of(at + height * full, 8), 8), 0 : rest_width * len(pieces)] = jnp.concatenate(
            pieces, axis=1
        )

    def unpack(value, out, row, height):
        full = hidden // 128
        rest_width = hidden - 128 * full
        for c in range(full):
            out[row : row + height, 128 * c : 128 * (c + 1)] = value[height * c : height * (c + 1), :]
        for i in range(height // 8):
            out[row + 8 * i : row + 8 * i + 8, 128 * full : hidden] = value[
                height * full : height * full + 8, rest_width * i : rest_width * (i + 1)
            ]

    def finish(xt, act_buf, w1_ring, w1_tail, gx_ring):
        xt_load = pltpu.make_async_copy(xt_hbm, xt, xt_sem)
        xt_load.start()

        gx_spans = windows(genes, GX)

        def gx_load(i):
            at, size = gx_spans[i]
            return (
                pltpu.make_async_copy(
                    w1_hbm.at[:, pl.ds(at, size)], w1_ring.at[i % 2] if size == GX else w1_tail, gx_sems.at[0, i]
                ),
                pltpu.make_async_copy(
                    g_out.at[:, pl.ds(at, GX)], g_win.at[i % 2, :, pl.ds(0, GX)], gx_sems.at[1, i]
                ),
            )

        def gx_save(i):
            return pltpu.make_async_copy(gx_ring.at[i % 2], gx_out.at[:, pl.ds(GX * i, GX)], gx_sems.at[2, i])

        def grad_cells(i):
            at, size = gx_spans[i]
            if i == 0:
                for copy in gx_load(0):
                    copy.start()
            if i + 1 < len(gx_spans):
                for copy in gx_load(i + 1):
                    copy.start()
            for copy in gx_load(i):
                copy.wait()
            if i >= 2:
                gx_save(i - 2).wait()
            wide[:, 0:size] = nn(gpre1[...], w1_ring[i % 2] if size == GX else w1_tail[...])

            def write(r, c):
                value = wide[r, 0:size] - g_win[i % 2, r, 0:size].astype(F32)
                gx_ring[i % 2, r, 0:size] = (cell_total * value).astype(BF16)
                return c

            row_loop(rows, write, 0)
            gx_save(i).start()
            if i + 1 == len(gx_spans):
                gx_save(i - 1).wait()
                gx_save(i).wait()

        def enc_fill(q, s):
            def fill(target, is_upper):
                for i in range(16):
                    j = scatter.part(q, 16 + i if is_upper else i)
                    picked[32 * i : 32 * i + 32, :] = xt[j, 32 * s : 32 * s + 32, :]
                wide[0:512, 0:hidden] = nn(picked[...], gpre1[...])

                def one(i, c):
                    pack(target, i * SLOT_ROWS, wide, pl.multiple_of(i * 32, 32), 32)
                    return c

                lax.fori_loop(0, 16, one, 0)

            return fill

        def enc_done(s):
            return lambda value: unpack(value, enc_part, 32 * s, 32)

        each = 2 * hidden // PARTS
        skip = (0, 32)

        def nar_fill(q, which):
            height_here = 32 if which == 0 else 24
            rows_here = 25 * 8 if which == 0 else 19 * 8
            place = STAGES - 1 - ORDERS[q].index(4)

            def fill(target, is_upper):
                column, part = column_parts(hidden, each)
                slot = slot_of(scatter, q, (0, 1, 2, 3), PARTS // 2, part)
                line = column - each * part - skip[which]
                inside = (line >= 0) & (line < height_here)
                base = 8 if is_upper else 0
                place_in = jnp.where(inside, (slot - base) * height_here + line, -1)
                place_in = jnp.where((slot >= base) & (slot < base + 8), place_in, -1)
                select = one_hot(8 * height_here, place_in)
                for matrix, act_slot, grad in ((0, 0, gpre2), (1, 1, gpre4)):
                    size = 8 * height_here
                    picked[0:size, :] = nt(select, act_buf[act_slot]).astype(BF16)
                    wide[0:size, 0:hidden] = nn(picked[0:size, :], grad[...])
                    flip = scatter.bit(4) if matrix == 0 else 1 - scatter.bit(4)
                    for i in range(8):
                        k = (i >> place) * (2 << place) + (i & ((1 << place) - 1)) + flip * (1 << place)
                        pack(target, k * rows_here, wide, i * height_here, height_here)

            return rows_here, fill

        def nar_done(which):
            if which == 0:
                return lambda value: unpack(value, nar_part, 0, 32)
            return lambda value: unpack(value, nar_part, 32, 24)

        for which in range(2):
            done[first + which] = nar_done(which)
            pieces[first + which] = nar_fill(first + which, which)
        for s in range(count):
            done[first + 2 + s] = enc_done(s)
            pieces[first + 2 + s] = (SLOT_ROWS, enc_fill(first + 2 + s, s))

        def row(ref, k):
            return ref[k : k + 1, :]

        def back(k, grad, out):
            nrm_loads[k].wait()
            return norm_gradient(
                grad,
                nrm_buf.at[(k + 1) % 2],
                out,
                gather,
                k,
                row(gain_ref, k),
                row(shift_ref, k),
                row(inv_ref, k),
                1.0 / cell_total,
                gain_out.at[k : k + 1, :],
                shift_out.at[k : k + 1, :],
            )

        act_loads = [
            pltpu.make_async_copy(ref, act_buf.at[at], act_sems.at[i])
            for i, (ref, at) in enumerate(((act1_hbm, 0), (act3_hbm, 1), (act2_hbm, 0)))
        ]
        act_loads[1].start()
        act_loads[2].start()

        def latent_side():
            act_loads[2].wait()
            d1_grad = tn(zlat_ref[...], gpre3[...])
            headw_grad = tn(ghead[...], act_buf[0])
            act_loads[0].start()
            for c in range(-(-hidden // 128)):
                size = min(128, hidden - 128 * c)
                at = D1_ROWS * c
                rep_block[at : at + latent, 0:size] = d1_grad[:, 128 * c : 128 * c + size]
                at = 7 * D1_ROWS + 2 * latent * c
                rep_block[at : at + 2 * latent, 0:size] = headw_grad[:, 128 * c : 128 * c + size]
            put_row(rep_block, rep_headb, column_sum(ghead[...].astype(F32)), 2 * latent)
            waiting.extend(range(2 * STAGES + 1))

        def chain():
            for k, out in ((3, gpre4), (2, gpre3), (1, gpre2), (0, gpre1)):
                waits = back(k, gact, out)
                for at, _ in enumerate(waits):
                    if (k, at) == (3, 1):
                        groups = ggroup_ref.shape[0]
                        member = (lax.broadcasted_iota(jnp.int32, (groups, rows), 0) == gid_ref[...]).astype(F32)
                        gcell[...] = exact(member, ggroup_ref[...], ((0,), (0,)))
                    if (k, at) == (1, 1):
                        latent_side()
                    yield 0
                if k == 3:
                    nrm_loads[1].start()
                    gact[...] = nt(gpre4[...], d2_ref[...])
                elif k == 2:
                    nrm_loads[0].start()
                    grad_z = nt(gpre3[...], d1_ref[...])
                    mu = head_ref_in[:, 0:latent]
                    logvar = head_ref_in[:, latent : 2 * latent]
                    kl = KL_WEIGHT * genes / cell_total
                    deviation = jnp.exp(0.5 * logvar)
                    grad_mu = grad_z + kl * mu + gcell[:, 0:latent]
                    grad_logvar = grad_z * noise_ref[...].T * (0.5 * deviation) + 0.5 * kl * (jnp.exp(logvar) - 1.0)
                    ghead[...] = jnp.concatenate([grad_mu, grad_logvar], axis=1).astype(BF16)
                    gact[...] = nn(ghead[...], head_ref[...])
                elif k == 1:
                    gact[...] = nt(gpre2[...], w2_ref[...])
                else:
                    for copy in act_loads[:2]:
                        copy.wait()
                    xt_load.wait()
                yield 0

        waiting = []

        def more():
            if waiting and len(plan) % 18 == 0:
                spread.step(waiting.pop(0))

        run(chain(), more, grad_cells)
        for i in waiting:
            spread.step(i)
        for q in (total - 2, total - 1):
            scatter.send(q, 0).wait_send()
        for c in range(-(-hidden // 128)):
            size = min(128, hidden - 128 * c)
            at = D1_ROWS * c
            d1_out[:, 128 * c : 128 * c + size] = rep_whole[at : at + latent, 0:size]
            at = 7 * D1_ROWS + 2 * latent * c
            headw_out[:, 128 * c : 128 * c + size] = rep_whole[at : at + 2 * latent, 0:size]
        outb_out[...] = rep_whole[rep_outb : rep_outb + 8 * count, :]
        headb_out[...] = rep_whole[rep_headb : rep_headb + 8, :]
        for level in range(levels):
            for k in range(4):
                gather.finish(level, k)

    pl.run_scoped(
        finish,
        pltpu.VMEM(xt_hbm.shape, BF16),
        pltpu.VMEM((2, rows, hidden), BF16),
        pltpu.VMEM((2, hidden, GX), BF16),
        pltpu.VMEM((hidden, windows(genes, GX)[-1][1]), BF16),
        pltpu.VMEM((2, rows, GX), BF16),
    )


def call_backward(grid, kept, cells_x, w1t, out_w, noise, gid, out_b, w2, headt, d1, d2, gain, shift):
    (nrm0, nrm1, nrm2, nrm3, inv, act1, act2, zlat, act3, act4, head, ggroup, xt) = kept
    rows, genes = cells_x.shape
    hidden, latent = w2.shape[0], d1.shape[0]
    spans = windows(genes)
    count = len(spans)
    vm = pl.BlockSpec(memory_space=pltpu.VMEM)
    hbm = pl.BlockSpec(memory_space=pl.ANY)
    shape = jax.ShapeDtypeStruct
    out_shape = (
        shape((rows, WIN * count), BF16),
        shape((rows, WIN * count), BF16),
        shape((hidden // PARTS, WIN * count), F32),
        shape((32 * count, hidden), F32),
        shape((56, hidden), F32),
        shape((latent, hidden), F32),
        shape((2 * latent, hidden), F32),
        shape((8 * count, 128), F32),
        shape((8, 128), F32),
        shape((4, hidden), F32),
        shape((4, hidden), F32),
    )
    dma = pltpu.SemaphoreType.DMA
    scratch = (
        [pltpu.VMEM((4, size, 16, 128), F32) for _, size in grid.digits]
        + [dma((4, size - 1)) for _, size in grid.digits]
        + [dma((4, size - 1)) for _, size in grid.digits]
        + [pltpu.VMEM((2, 16 * SLOT_ROWS, 128), F32), pltpu.VMEM((16 * SLOT_ROWS, 128), F32)]
        + [pltpu.VMEM((CHANNELS, (16 >> t) * SLOT_ROWS, 128), F32) for t in range(STAGES)]
        + [dma((2,)), dma((CHANNELS, STAGES)), dma((CHANNELS, STAGES)), pltpu.SemaphoreType.REGULAR((2 * count + 2 - CHANNELS, STAGES))]
        + [pltpu.VMEM((REP_ROWS, 128), F32), pltpu.VMEM((REP_ROWS, 128), F32)]
        + [pltpu.VMEM((REP_ROWS >> (t + 1), 128), F32) for t in range(STAGES)]
        + [dma((4, STAGES))]
        + [
            pltpu.VMEM((3, rows, WIN), BF16),
            pltpu.VMEM((rows, WIN), F32),
            pltpu.VMEM((rows, hidden), F32),
            pltpu.VMEM((rows, hidden), BF16),
            pltpu.VMEM((rows, hidden), BF16),
            pltpu.VMEM((rows, hidden), BF16),
            pltpu.VMEM((rows, hidden), BF16),
            pltpu.VMEM((rows, 2 * latent), BF16),
            pltpu.VMEM((rows, 128), F32),
            pltpu.VMEM((len(set(ORDERS[:count])), hidden, rows), BF16),
            pltpu.VMEM((2, rows, hidden), F32),
            pltpu.VMEM((SLOT_ROWS, 128), F32),
        ]
        + [dma((2, count)), dma((count,)), dma((4,)), dma, dma((3,)), dma((3, len(windows(genes, GX))))]
    )
    return pl.pallas_call(
        functools.partial(backward_kernel, grid, latent),
        out_shape=out_shape,
        in_specs=[hbm] * 11 + [vm] * 14,
        out_specs=[hbm] * 2 + [vm] * (len(out_shape) - 2),
        scratch_shapes=scratch,
        name="backward",
        compiler_params=pltpu.CompilerParams(
            collective_id=1, has_side_effects=True, vmem_limit_bytes=63 * 2**20
        ),
    )(
        cells_x,
        w1t,
        out_w,
        nrm0,
        nrm1,
        nrm2,
        nrm3,
        act1,
        act2,
        act3,
        xt,
        act4,
        zlat,
        head,
        noise,
        gid,
        ggroup,
        inv,
        out_b,
        w2,
        headt,
        d1,
        d2,
        gain,
        shift,
    )


def flat_shard(grid, flat, columns, rows_in_all):
    value = flat.reshape(rows_in_all // PARTS, columns)
    size = grid.n // PARTS
    if size > 1:
        groups = [list(range(size * p, size * p + size)) for p in range(PARTS)]
        value = lax.psum_scatter(
            value, ("cells", "rep"), scatter_dimension=0, axis_index_groups=groups, tiled=True
        )
    return value


def group_sum(grid, values):
    size = grid.n // PARTS
    if size > 1:
        groups = [list(range(size * p, size * p + size)) for p in range(PARTS)]
        values = lax.psum(values, ("cells", "rep"), axis_index_groups=groups)
    return values


def shards(
    grid,
    cells_x,
    latent_noise,
    group_ids,
    owner_table,
    owner_mask,
    enc_w1,
    enc_w2,
    head_w,
    head_b,
    dec_w1,
    dec_w2,
    out_w,
    out_b,
    bn_gain,
    bn_shift,
):
    cell_total = float(cells_x.shape[0] * grid.n)
    genes = cells_x.shape[1]
    hidden = enc_w2.shape[0]
    gid = group_ids.reshape(1, -1)
    headt = head_w.T
    w1t = enc_w1.T
    noise = latent_noise.T
    *kept, offsets = call_forward(
        grid,
        cells_x,
        w1t,
        noise,
        gid,
        owner_table.T,
        owner_mask.T,
        enc_w2,
        headt,
        head_b.reshape(1, -1),
        dec_w1,
        dec_w2,
        bn_gain,
        bn_shift,
    )
    _, gx, out25, enc_part, nar_part, d1_grad, headw_grad, outb_grad, headb_grad, grad_gain, grad_shift = call_backward(
        grid,
        kept,
        cells_x,
        w1t,
        out_w,
        noise,
        gid,
        out_b.reshape(1, -1),
        enc_w2,
        headt,
        dec_w1,
        dec_w2,
        bn_gain,
        bn_shift,
    )
    grad_x = gx[:, :genes].astype(F32)
    part = grid.me() // (grid.n // PARTS)
    each = genes * hidden // PARTS
    enc_flat = lax.dynamic_slice_in_dim(enc_part.reshape(-1), (genes * part) % PARTS * (hidden // PARTS), each)
    shard_enc = flat_shard(grid, enc_flat, FLAT_COLS, FLAT_ROWS)
    shard_out = flat_shard(grid, out25[:, :genes], FLAT_COLS, FLAT_ROWS)
    shard_narrow = flat_shard(grid, nar_part[: 2 * hidden // PARTS], NARROW_COLS, NARROW_ROWS)
    headw_grad, d1_grad, headb_grad, outb_grad = group_sum(
        grid,
        (headw_grad.T, d1_grad, headb_grad.reshape(-1)[: head_b.shape[0]], outb_grad.reshape(-1)[:genes]),
    )
    return (
        grad_x,
        shard_enc,
        shard_narrow,
        headw_grad,
        d1_grad,
        headb_grad,
        shard_out,
        outb_grad,
        grad_gain,
        grad_shift,
        offsets[None],
    )


def solution(mesh):
    grid = Slice(mesh.shape["cells"], mesh.shape["rep"])
    lines = P(("cells", "rep"), None)
    return jax.shard_map(
        functools.partial(shards, grid),
        mesh=mesh,
        in_specs=(lines, lines, P(("cells", "rep"))) + (P(),) * 12,
        out_specs=(lines, lines, lines, P(), P(), P(), lines, P(), P(), P(), P("cells", None, None)),
        check_vma=False,
    )
```

```python
import functools

import jax
import jax.numpy as jnp
from jax import lax
from jax.experimental import pallas as pl
from jax.experimental.pallas import tpu as pltpu
from jax.sharding import PartitionSpec as P

POP_DEV = 2
FLAT_COLS = 875
NARROW_COLS = 625
FLAT_ROWS = 6400
NARROW_ROWS = 2048

NORM_EPSILON = 1e-05
KL_WEIGHT = 5e-05
OFFSET_WEIGHT = 200.0

MESH_ID = pl.DeviceIdType.MESH
WIN = 1024
ROWS = 48
F32 = jnp.float32
BF16 = jnp.bfloat16


class Slice:
    def __init__(self, cells, rep):
        self.cells, self.rep = cells, rep
        self.n = cells * rep
        self.bits = self.n.bit_length() - 1
        self.digits = []
        low = 0
        while low < self.bits:
            width = min(3, self.bits - low)
            self.digits.append((low, 1 << width))
            low += width

    def me(self):
        return lax.axis_index("cells") * self.rep + lax.axis_index("rep")

    def place(self, index):
        return (index // self.rep, index % self.rep)


def greet(grid, peers):
    barrier = pltpu.get_barrier_semaphore()
    for peer in peers:
        pl.semaphore_signal(barrier, inc=1, device_id=grid.place(peer), device_id_type=MESH_ID)


def meet(peers):
    pl.semaphore_wait(pltpu.get_barrier_semaphore(), len(peers))


def digit_peers(grid):
    me = grid.me()
    peers = []
    for low, size in grid.digits:
        rank = (me // (1 << low)) % size
        for k in range(1, size):
            other = (rank + k) % size
            peers.append(me + (other - rank) * (1 << low))
    return peers


class Gather:
    def __init__(self, grid, buffers, send_sems, recv_sems):
        self.grid, self.buffers, self.send_sems, self.recv_sems = grid, buffers, send_sems, recv_sems

    def rank(self, level):
        low, size = self.grid.digits[level]
        return (self.grid.me() // (1 << low)) % size

    def copy(self, level, slot, k, arriving=False):
        low, size = self.grid.digits[level]
        rank = self.rank(level)
        to = (rank + k) % size
        buffer = self.buffers[level].at[slot]
        return pltpu.make_async_remote_copy(
            src_ref=buffer.at[rank],
            dst_ref=buffer.at[(rank + size - k) % size if arriving else rank],
            send_sem=self.send_sems[level].at[slot, k - 1],
            recv_sem=self.recv_sems[level].at[slot, k - 1],
            device_id=self.grid.place(self.grid.me() + (to - rank) * (1 << low)),
            device_id_type=MESH_ID,
        )

    def start(self, level, slot):
        for k in range(1, self.grid.digits[level][1]):
            self.copy(level, slot, k).start()

    def wait(self, level, slot):
        for k in range(1, self.grid.digits[level][1]):
            self.copy(level, slot, k, arriving=True).wait_recv()

    def finish(self, level, slot):
        for k in range(1, self.grid.digits[level][1]):
            self.copy(level, slot, k).wait_send()

    def own(self, level, slot):
        return self.buffers[level].at[slot, self.rank(level)]


def put_row(ref, first, row, width):
    full = width // 128
    for c in range(full):
        ref[first + c : first + c + 1, :] = row[:, 128 * c : 128 * (c + 1)]
    rest = width - 128 * full
    if rest:
        ref[first + full : first + full + 1, 0:rest] = row[:, 128 * full : width]


def take_row(block, first, width):
    pieces = []
    for c in range(-(-width // 128)):
        pieces.append(block[first + c : first + c + 1, 0 : min(128, width - 128 * c)])
    return jnp.concatenate(pieces, axis=1)


def row_loop(rows, body, init):
    steps = rows // ROWS

    def step(i, carry):
        return body(pl.ds(pl.multiple_of(i * ROWS, ROWS), ROWS), carry)

    return lax.fori_loop(0, steps, step, init)


def sigmoid(value):
    return 0.5 * jnp.tanh(0.5 * value) + 0.5


def column_sum(value):
    return jnp.sum(value, axis=0, keepdims=True)


PARTS = 32


def batch_norm(pre, nrm_out, act_out, gather, slot, gain_row, shift_row, inv_out, idle):
    rows, width = pre.shape
    total = row_loop(rows, lambda r, c: c + column_sum(pre[r, :]), jnp.zeros((1, width), F32))
    mean = total * (1.0 / rows)

    def squares(r, c):
        d = pre[r, :] - mean
        return c + column_sum(d * d)

    square = row_loop(rows, squares, jnp.zeros((1, width), F32))
    own = gather.own(0, slot)
    put_row(own, 0, mean, width)
    put_row(own, 8, square, width)
    count = float(rows)
    levels = len(gather.grid.digits)
    for level in range(levels):
        size = gather.grid.digits[level][1]
        gather.start(level, slot)
        idle(level)
        gather.wait(level, slot)
        buffer = gather.buffers[level].at[slot]
        means = [buffer[g, 0:8, :] for g in range(size)]
        merged = sum(means[1:], means[0]) * (1.0 / size)
        spread = sum([buffer[g, 8:16, :] for g in range(1, size)], buffer[0, 8:16, :])
        between = sum([(m - merged) * (m - merged) for m in means[1:]], (means[0] - merged) * (means[0] - merged))
        spread = spread + count * between
        count = count * size
        if level + 1 < levels:
            own = gather.own(level + 1, slot)
            own[0:8, :] = merged
            own[8:16, :] = spread
    inv = lax.rsqrt(spread * (1.0 / count) + NORM_EPSILON)
    mean = take_row(merged, 0, width)
    inv = take_row(inv, 0, width)
    inv_out[...] = inv

    def write(r, c):
        nrm = (pre[r, :] - mean) * inv
        nrm_out[r, :] = nrm
        value = gain_row * nrm + shift_row
        act_out[r, :] = (value * sigmoid(value)).astype(BF16)
        return c

    row_loop(rows, write, 0)


def nt(left, right):
    return lax.dot_general(left, right, (((1,), (1,)), ((), ())), preferred_element_type=F32)


def nn(left, right):
    return lax.dot_general(left, right, (((1,), (0,)), ((), ())), preferred_element_type=F32)


def tn(left, right):
    return lax.dot_general(left, right, (((0,), (0,)), ((), ())), preferred_element_type=F32)


def exact(left, right, dims):
    return lax.dot_general(
        left, right, (dims, ((), ())), precision=lax.Precision.HIGHEST, preferred_element_type=F32
    )


WIDE = 1024
AHEAD = 3


def windows(width, size=WIN):
    return [(s, min(size, width - s)) for s in range(0, width, size)]


def part_of(full, tail, i):
    return full.at[i] if i < full.shape[0] else tail


def forward_kernel(
    grid,
    table_ref,
    mask_ref,
    x_hbm,
    w1_hbm,
    noise_ref,
    gid_ref,
    w2_ref,
    head_ref,
    headb_ref,
    d1_ref,
    d2_ref,
    gain_ref,
    shift_ref,
    nrm0_hbm,
    nrm1_hbm,
    nrm2_hbm,
    nrm3_hbm,
    inv_out,
    act1_hbm,
    act2_hbm,
    zlat,
    act3_hbm,
    act4,
    head_out,
    ggroup_out,
    xt_out,
    offsets_out,
    x_all,
    xt,
    w_win,
    w_tail,
    pre,
    moments,
    *rest,
):
    levels = len(grid.digits)
    small = rest[:levels]
    wide = rest[levels : 2 * levels]
    s_send, s_recv, g_send, g_recv = (
        rest[2 * levels : 3 * levels],
        rest[3 * levels : 4 * levels],
        rest[4 * levels : 5 * levels],
        rest[5 * levels : 6 * levels],
    )
    in_sems, xt_sems, nrm_keep, act_keep, keep_sems = rest[6 * levels :]
    act1, act2, act3 = (act_keep.at[i] for i in range(3))
    gather = Gather(grid, small, s_send, s_recv)
    group_gather = Gather(grid, wide, g_send, g_recv)
    latent = d1_ref.shape[0]
    genes = x_hbm.shape[1]
    spans = windows(genes, WIDE)

    peers = digit_peers(grid)
    greet(grid, peers)
    loads = []
    for i, (s, size) in enumerate(spans):
        a = pltpu.make_async_copy(x_hbm.at[:, pl.ds(s, size)], x_all.at[:, pl.ds(s, size)], in_sems.at[0, i])
        b = pltpu.make_async_copy(w1_hbm.at[:, pl.ds(s, size)], part_of(w_win, w_tail, i), in_sems.at[1, i])
        if i < AHEAD:
            a.start()
            b.start()
        loads.append((a, b))

    for i, (s, size) in enumerate(spans):
        loads[i][0].wait()
        loads[i][1].wait()
        if i + AHEAD < len(loads):
            for copy in loads[i + AHEAD]:
                copy.start()
        part = nt(x_all[:, s : s + size], part_of(w_win, w_tail, i)[...])
        pre[...] = part if i == 0 else pre[...] + part

    starts = [(genes * j) // PARTS for j in range(PARTS)]
    parts_left = list(range(PARTS))

    def save(j):
        return pltpu.make_async_copy(xt.at[j], xt_out.at[j], xt_sems.at[j])

    def transpose(level):
        for j in parts_left[: -(-PARTS // 6)]:
            at = starts[j] // 128 * 128
            size = min(384, genes - at)
            lane = lax.broadcasted_iota(jnp.int32, (xt.shape[1], size), 1)
            line = lax.broadcasted_iota(jnp.int32, (xt.shape[1], size), 0)
            select = jnp.where(lane == line + (starts[j] - at), 1.0, 0.0).astype(BF16)
            xt[j] = nt(select, x_all[:, at : at + size]).astype(BF16)
            save(j).start()
            parts_left.remove(j)

    kept = [
        pltpu.make_async_copy(nrm_keep.at[k], ref, keep_sems.at[0, k])
        for k, ref in enumerate((nrm0_hbm, nrm1_hbm, nrm2_hbm, nrm3_hbm))
    ] + [
        pltpu.make_async_copy(act_keep.at[k], ref, keep_sems.at[1, k])
        for k, ref in enumerate((act1_hbm, act2_hbm, act3_hbm))
    ]

    def norm(k, act, idle=transpose):
        batch_norm(
            pre,
            nrm_keep.at[k],
            act,
            gather,
            k,
            gain_ref[k : k + 1, :],
            shift_ref[k : k + 1, :],
            inv_out.at[k : k + 1, :],
            idle,
        )
        kept[k].start()
        if k < 3:
            kept[4 + k].start()

    meet(peers)
    norm(0, act1)
    pre[...] = nn(act1[...], w2_ref[...])
    norm(1, act2)
    head = nt(act2[...], head_ref[...]) + headb_ref[...]
    head_out[...] = head
    mu = head[:, 0:latent]
    logvar = head[:, latent : 2 * latent]
    zlat[...] = (mu + jnp.exp(0.5 * logvar) * noise_ref[...].T).astype(BF16)

    groups = ggroup_out.shape[0]
    pops = groups // 2
    cells_here = gid_ref.shape[1]
    member = (lax.broadcasted_iota(jnp.int32, (groups, cells_here), 0) == gid_ref[...]).astype(F32)
    own = group_gather.own(0, 0)
    own[:, 0:latent] = exact(member, mu, ((1,), (0,)))
    own[:, latent : latent + 1] = jnp.sum(member, axis=1, keepdims=True)
    group_gather.start(0, 0)

    pre[...] = nn(zlat[...], d1_ref[...])
    norm(2, act3)

    def group_level(level):
        group_gather.wait(level, 0)
        size = grid.digits[level][1]
        buffer = wide[level].at[0]
        total = sum([buffer[g] for g in range(1, size)], buffer[0])
        if level + 1 < levels:
            group_gather.own(level + 1, 0)[...] = total
            group_gather.start(level + 1, 0)
            return
        counted = jnp.maximum(total[:, latent : latent + 1], 1.0)
        moments[...] = total / counted
        odd, even = pl.ds(1, pops, stride=2), pl.ds(0, pops, stride=2)
        offset = moments[odd, :] - moments[even, :]
        centre = jnp.sum(offset, axis=0, keepdims=True) * (1.0 / pops)
        grad_offset = (2.0 * OFFSET_WEIGHT / pops) * (offset - centre)
        row = lax.axis_index("cells")
        slots = offsets_out.shape[0]
        lane = lax.broadcasted_iota(jnp.int32, (1, pops), 1)
        picks = jnp.concatenate(
            [jnp.where(lane == table_ref[s, row], mask_ref[s, row].astype(F32), 0.0) for s in range(slots)], axis=0
        )
        offsets_out[...] = exact(picks, offset, ((1,), (0,)))[:, 0:latent]
        moments[odd, :] = grad_offset
        moments[even, :] = -grad_offset
        ggroup_out[...] = moments[...] / counted

    group_level(0)
    pre[...] = nn(act3[...], d2_ref[...])
    norm(3, act4, lambda level: group_level(level) if level else None)
    while parts_left:
        transpose(0)

    for j in range(PARTS):
        save(j).wait()
    for copy in kept:
        copy.wait()
    for level in range(levels):
        for k in range(4):
            gather.finish(level, k)
        group_gather.finish(level, 0)


XT_ROWS = 224


def call_forward(grid, cells_x, w1t, noise, gid, table, mask, w2, headt, headb, d1, d2, gain, shift):
    rows, genes = cells_x.shape
    hidden = w2.shape[0]
    latent = d1.shape[0]
    groups = 2 * POP_DEV * grid.cells
    spans = windows(genes, WIDE)
    count = len(spans)
    levels = len(grid.digits)
    vm = pl.BlockSpec(memory_space=pltpu.VMEM)
    hbm = pl.BlockSpec(memory_space=pl.ANY)
    sm = pl.BlockSpec(memory_space=pltpu.SMEM)
    wide_f = jax.ShapeDtypeStruct((rows, hidden), F32)
    wide_b = jax.ShapeDtypeStruct((rows, hidden), BF16)
    out_shape = (
        wide_f,
        wide_f,
        wide_f,
        wide_f,
        jax.ShapeDtypeStruct((4, hidden), F32),
        wide_b,
        wide_b,
        jax.ShapeDtypeStruct((rows, latent), BF16),
        wide_b,
        wide_b,
        jax.ShapeDtypeStruct((rows, 2 * latent), F32),
        jax.ShapeDtypeStruct((groups, 128), F32),
        jax.ShapeDtypeStruct((PARTS, XT_ROWS, rows), BF16),
        jax.ShapeDtypeStruct((table.shape[0], latent), F32),
    )
    scratch = (
        [
            pltpu.VMEM((rows, genes), BF16),
            pltpu.VMEM((PARTS, XT_ROWS, rows), BF16),
            pltpu.VMEM((count - 1, hidden, WIDE), BF16),
            pltpu.VMEM((hidden, spans[-1][1]), BF16),
            pltpu.VMEM((rows, hidden), F32),
            pltpu.VMEM((groups, 128), F32),
        ]
        + [pltpu.VMEM((4, size, 16, 128), F32) for _, size in grid.digits]
        + [pltpu.VMEM((1, size, groups, 128), F32) for _, size in grid.digits]
        + [pltpu.SemaphoreType.DMA((4, size - 1)) for _, size in grid.digits]
        + [pltpu.SemaphoreType.DMA((4, size - 1)) for _, size in grid.digits]
        + [pltpu.SemaphoreType.DMA((1, size - 1)) for _, size in grid.digits]
        + [pltpu.SemaphoreType.DMA((1, size - 1)) for _, size in grid.digits]
        + [pltpu.SemaphoreType.DMA((2, count)), pltpu.SemaphoreType.DMA((PARTS,))]
        + [
            pltpu.VMEM((4, rows, hidden), F32),
            pltpu.VMEM((3, rows, hidden), BF16),
            pltpu.SemaphoreType.DMA((2, 4)),
        ]
    )
    return pl.pallas_call(
        functools.partial(forward_kernel, grid),
        out_shape=out_shape,
        in_specs=[sm, sm, hbm, hbm] + [vm] * 9,
        out_specs=[hbm] * 4 + [vm, hbm, hbm, vm, hbm, vm, vm, vm, hbm, vm],
        scratch_shapes=scratch,
        name="forward",
        compiler_params=pltpu.CompilerParams(
            collective_id=0, has_side_effects=True, vmem_limit_bytes=60 * 2**20
        ),
    )(table, mask, cells_x, w1t, noise, gid, w2, headt, headb, d1, d2, gain, shift)


ORDERS = (
    (0, 2, 3, 1, 4),
    (0, 1, 3, 2, 4),
    (0, 2, 3, 1, 4),
    (0, 1, 3, 2, 4),
    (0, 2, 3, 1, 4),
    (0, 2, 3, 1, 4),
    (0, 1, 3, 2, 4),
    (0, 2, 3, 1, 4),
    (0, 1, 2, 3, 4),
    (0, 1, 3, 2, 4),
    (0, 2, 3, 1, 4),
    (0, 1, 2, 3, 4),
    (0, 1, 2, 3, 4),
    (0, 2, 3, 4, 1),
    (0, 2, 3, 1, 4),
    (0, 1, 2, 3, 4),
)
C, U, L, S, F, X, A = range(7)
PLAN = (
    (C,),
    (U, 0),
    (C,),
    (C,),
    (L, 0),
    (S, 0, 1, 7, 1),
    (S, 0, 1, 5, 2),
    (U, 1),
    (C,),
    (S, 0, 1, 4, 1),
    (C,),
    (L, 1),
    (S, 1, 1, 7, 1),
    (S, 0, 1, 3, 1),
    (C,),
    (S, 1, 1, 6, 1),
    (S, 0, 1, 2, 1),
    (C,),
    (F, 0, 1, 0),
    (S, 1, 1, 5, 1),
    (S, 0, 2, 3, 1),
    (S, 0, 1, 1, 1),
    (C,),
    (S, 1, 1, 4, 1),
    (S, 0, 1, 0, 1),
    (S, 0, 2, 2, 1),
    (C,),
    (S, 0, 2, 1, 1),
    (C,),
    (S, 1, 1, 3, 1),
    (S, 0, 2, 0, 1),
    (U, 2),
    (F, 0, 1, 1),
    (S, 1, 1, 2, 1),
    (F, 0, 2, 0),
    (F, 1, 1, 0),
    (S, 1, 2, 3, 1),
    (S, 1, 1, 1, 1),
    (C,),
    (S, 1, 2, 2, 1),
    (C,),
    (F, 0, 2, 1),
    (S, 1, 1, 0, 1),
    (L, 2),
    (S, 2, 1, 7, 1),
    (S, 0, 3, 1, 1),
    (S, 2, 1, 6, 1),
    (S, 1, 2, 1, 1),
    (U, 3),
    (S, 0, 3, 0, 1),
    (S, 1, 2, 0, 1),
    (C,),
    (F, 1, 1, 1),
    (S, 2, 1, 5, 1),
    (F, 1, 2, 0),
    (C,),
    (F, 0, 3, 0),
    (S, 2, 1, 4, 1),
    (S, 0, 4, 0, 1),
    (L, 3),
    (S, 3, 1, 7, 1),
    (F, 1, 2, 1),
    (C,),
    (C,),
    (S, 3, 1, 5, 2),
    (S, 2, 1, 2, 2),
    (F, 0, 3, 1),
    (U, 4),
    (F, 2, 1, 0),
    (S, 2, 2, 3, 1),
    (F, 0, 4, 0),
    (C,),
    (S, 3, 1, 4, 1),
    (S, 3, 1, 3, 1),
    (S, 2, 1, 0, 2),
    (S, 2, 2, 2, 1),
    (S, 2, 2, 1, 1),
    (L, 4),
    (U, 5),
    (F, 3, 1, 0),
    (S, 3, 1, 2, 1),
    (S, 1, 3, 1, 1),
    (S, 2, 2, 0, 1),
    (S, 3, 1, 1, 1),
    (S, 1, 3, 0, 1),
    (S, 3, 2, 3, 1),
    (C,),
    (F, 2, 1, 1),
    (F, 2, 2, 0),
    (L, 5),
    (S, 3, 1, 0, 1),
    (S, 4, 1, 7, 1),
    (S, 3, 2, 2, 1),
    (F, 1, 3, 0),
    (F, 2, 2, 1),
    (C,),
    (C,),
    (S, 2, 3, 1, 1),
    (S, 2, 3, 0, 1),
    (S, 4, 1, 5, 2),
    (S, 3, 2, 0, 2),
    (F, 1, 3, 1),
    (U, 6),
    (F, 3, 1, 1),
    (F, 3, 2, 0),
    (C,),
    (S, 4, 1, 4, 1),
    (S, 4, 1, 3, 1),
    (S, 1, 4, 0, 1),
    (F, 2, 3, 0),
    (F, 2, 3, 1),
    (L, 6),
    (S, 6, 1, 7, 1),
    (F, 3, 2, 1),
    (F, 4, 1, 0),
    (S, 6, 1, 6, 1),
    (S, 4, 1, 2, 1),
    (S, 2, 4, 0, 1),
    (S, 6, 1, 5, 1),
    (S, 4, 1, 1, 1),
    (C,),
    (F, 1, 4, 0),
    (C,),
    (C,),
    (S, 6, 1, 4, 1),
    (S, 6, 1, 3, 1),
    (S, 4, 1, 0, 1),
    (S, 3, 3, 1, 1),
    (S, 4, 2, 2, 2),
    (F, 2, 4, 0),
    (C,),
    (S, 6, 1, 1, 2),
    (S, 3, 3, 0, 1),
    (S, 5, 1, 7, 1),
    (S, 4, 2, 0, 2),
    (F, 4, 1, 1),
    (F, 6, 1, 0),
    (F, 3, 3, 0),
    (F, 4, 2, 0),
    (F, 3, 3, 1),
    (S, 6, 1, 0, 1),
    (S, 5, 1, 6, 1),
    (S, 3, 4, 0, 1),
    (S, 4, 3, 1, 1),
    (S, 5, 1, 5, 1),
    (C,),
    (F, 4, 2, 1),
    (C,),
    (C,),
    (S, 4, 3, 0, 1),
    (S, 5, 1, 4, 1),
    (S, 5, 1, 3, 1),
    (S, 6, 2, 2, 2),
    (F, 6, 1, 1),
    (F, 4, 3, 0),
    (A, 0),
    (F, 3, 4, 0),
    (A, 1),
    (C,),
    (S, 5, 1, 1, 2),
    (S, 6, 2, 0, 2),
    (F, 4, 3, 1),
    (F, 5, 1, 0),
    (F, 6, 2, 0),
    (S, 5, 1, 0, 1),
    (S, 6, 3, 1, 1),
    (S, 4, 4, 0, 1),
    (C,),
    (F, 6, 2, 1),
    (S, 6, 3, 0, 1),
    (S, 5, 2, 2, 2),
    (S, 5, 2, 0, 2),
    (A, 2),
    (U, 7),
    (F, 5, 1, 1),
    (X, 0),
    (F, 4, 4, 0),
    (F, 6, 3, 0),
    (S, 6, 4, 0, 1),
    (X, 1),
    (F, 6, 3, 1),
    (L, 7),
    (S, 7, 1, 4, 4),
    (S, 7, 1, 2, 2),
    (U, 8),
    (F, 5, 2, 0),
    (S, 5, 3, 1, 1),
    (S, 5, 3, 0, 1),
    (S, 7, 1, 1, 1),
    (A, 3),
    (X, 2),
    (X, 3),
    (L, 8),
    (S, 8, 1, 4, 4),
    (S, 8, 1, 1, 3),
    (S, 7, 1, 0, 1),
    (F, 5, 2, 1),
    (F, 5, 3, 0),
    (S, 5, 4, 0, 1),
    (U, 9),
    (F, 5, 3, 1),
    (S, 8, 1, 0, 1),
    (X, 4),
    (F, 6, 4, 0),
    (X, 5),
    (F, 7, 1, 0),
    (S, 7, 2, 2, 2),
    (S, 7, 2, 0, 2),
    (A, 4),
    (L, 9),
    (S, 9, 1, 6, 2),
    (U, 10),
    (F, 8, 1, 0),
    (S, 9, 1, 5, 1),
    (S, 9, 1, 4, 1),
    (S, 8, 2, 2, 2),
    (S, 8, 2, 0, 2),
    (X, 6),
    (F, 5, 4, 0),
    (X, 7),
    (X, 8),
    (L, 10),
    (S, 9, 1, 2, 2),
    (S, 10, 1, 4, 4),
    (F, 7, 1, 1),
    (X, 9),
    (F, 7, 2, 0),
    (S, 9, 1, 1, 1),
    (F, 8, 1, 1),
    (U, 11),
    (F, 8, 2, 0),
    (S, 9, 1, 0, 1),
    (S, 10, 1, 2, 2),
    (S, 8, 3, 1, 1),
    (S, 8, 3, 0, 1),
    (X, 10),
    (F, 7, 2, 1),
    (X, 11),
    (F, 8, 2, 1),
    (S, 7, 3, 1, 1),
    (S, 10, 1, 1, 1),
    (A, 5),
    (L, 11),
    (S, 7, 3, 0, 1),
    (F, 8, 3, 0),
    (S, 8, 4, 0, 1),
    (U, 12),
    (F, 8, 3, 1),
    (S, 11, 1, 7, 1),
    (S, 10, 1, 0, 1),
    (F, 9, 1, 0),
    (S, 9, 2, 2, 2),
    (S, 9, 2, 0, 2),
    (X, 12),
    (A, 6),
    (X, 13),
    (L, 12),
    (S, 11, 1, 6, 1),
    (F, 8, 4, 0),
    (F, 10, 1, 0),
    (S, 11, 1, 5, 1),
    (S, 10, 2, 2, 2),
    (S, 11, 1, 4, 1),
    (S, 10, 2, 0, 2),
    (F, 7, 3, 0),
    (S, 11, 1, 3, 1),
    (S, 11, 1, 2, 1),
    (S, 7, 4, 0, 1),
    (F, 9, 1, 1),
    (F, 9, 2, 0),
    (S, 9, 3, 1, 1),
    (S, 9, 3, 0, 1),
    (U, 13),
    (F, 7, 3, 1),
    (S, 11, 1, 1, 1),
    (F, 9, 2, 1),
    (F, 10, 1, 1),
    (A, 7),
    (S, 11, 1, 0, 1),
    (F, 9, 3, 0),
    (S, 9, 4, 0, 1),
    (F, 9, 3, 1),
    (S, 12, 1, 7, 1),
    (L, 13),
    (S, 13, 1, 4, 4),
    (S, 13, 1, 3, 1),
    (U, 14),
    (F, 10, 2, 0),
    (S, 12, 1, 6, 1),
    (S, 13, 1, 2, 1),
    (A, 8),
    (S, 13, 1, 1, 1),
    (F, 11, 1, 0),
    (F, 10, 2, 1),
    (S, 13, 1, 0, 1),
    (L, 14),
    (F, 7, 4, 0),
    (S, 11, 2, 2, 2),
    (F, 13, 1, 0),
    (S, 12, 1, 5, 1),
    (S, 11, 2, 1, 1),
    (S, 13, 2, 2, 2),
    (S, 13, 2, 0, 2),
    (F, 11, 1, 1),
    (S, 12, 1, 4, 1),
    (U, 15),
    (F, 9, 4, 0),
    (S, 12, 1, 3, 1),
    (S, 11, 2, 0, 1),
    (S, 14, 1, 7, 1),
    (S, 12, 1, 2, 1),
    (L, 15),
    (S, 12, 1, 1, 1),
    (S, 14, 1, 6, 1),
    (F, 13, 1, 1),
    (S, 14, 1, 5, 1),
    (F, 13, 2, 0),
    (S, 13, 3, 1, 1),
    (S, 13, 3, 0, 1),
    (F, 13, 2, 1),
    (S, 12, 1, 0, 1),
    (S, 14, 1, 4, 1),
    (A, 9),
    (S, 10, 3, 1, 1),
    (F, 11, 2, 0),
    (S, 14, 1, 3, 1),
    (S, 11, 3, 1, 1),
    (S, 11, 3, 0, 1),
    (A, 10),
    (S, 10, 3, 0, 1),
    (F, 13, 3, 0),
    (S, 14, 1, 2, 1),
    (F, 12, 1, 0),
    (S, 13, 4, 0, 1),
    (F, 11, 2, 1),
    (S, 14, 1, 1, 1),
    (S, 15, 1, 7, 1),
    (F, 13, 3, 1),
    (S, 14, 1, 0, 1),
    (F, 11, 3, 0),
    (S, 15, 1, 6, 1),
    (S, 12, 2, 3, 1),
    (S, 11, 4, 0, 1),
    (F, 11, 3, 1),
    (S, 15, 1, 5, 1),
    (S, 12, 2, 2, 1),
    (F, 12, 1, 1),
    (S, 15, 1, 4, 1),
    (F, 14, 1, 0),
    (S, 12, 2, 1, 1),
    (F, 10, 3, 0),
    (S, 10, 4, 0, 1),
    (S, 15, 1, 3, 1),
    (F, 11, 4, 0),
    (S, 12, 2, 0, 1),
    (F, 10, 3, 1),
    (S, 15, 1, 2, 1),
    (S, 14, 2, 2, 2),
    (S, 14, 2, 0, 2),
    (F, 13, 4, 0),
    (F, 10, 4, 0),
    (S, 15, 1, 1, 1),
    (F, 14, 1, 1),
    (S, 15, 1, 0, 1),
    (F, 14, 2, 0),
    (S, 14, 3, 1, 1),
    (F, 12, 2, 0),
    (S, 14, 3, 0, 1),
    (S, 12, 3, 1, 1),
    (S, 12, 3, 0, 1),
    (F, 15, 1, 0),
    (S, 15, 2, 2, 2),
    (S, 15, 2, 0, 2),
    (F, 14, 2, 1),
    (F, 12, 2, 1),
    (F, 12, 3, 0),
    (S, 12, 4, 0, 1),
    (F, 12, 3, 1),
    (F, 15, 1, 1),
    (F, 15, 2, 0),
    (S, 15, 3, 1, 1),
    (S, 15, 3, 0, 1),
    (F, 12, 4, 0),
    (F, 14, 3, 0),
    (S, 14, 4, 0, 1),
    (F, 15, 2, 1),
    (F, 15, 3, 0),
    (S, 15, 4, 0, 1),
    (F, 14, 3, 1),
    (F, 15, 3, 1),
    (F, 14, 4, 0),
    (F, 15, 4, 0),
)
CHANNELS = 4
STAGES = 5
SLOT_ROWS = 200


class Scatter:
    def __init__(self, grid, total, stage, low, landing, stage_sems, send_sems, recv_sems, credits):
        self.grid, self.total = grid, total
        self.stage, self.low, self.landing = stage, low, landing
        self.stage_sems, self.send_sems, self.recv_sems, self.credits = stage_sems, send_sems, recv_sems, credits
        self.shift = grid.bits - STAGES
        self.rows = {}

    def bit(self, b):
        return (self.grid.me() // (1 << (b + self.shift))) % 2

    def partner(self, b):
        return self.grid.place(self.grid.me() + (1 - 2 * self.bit(b)) * (1 << (b + self.shift)))

    def part(self, q, k):
        out = 0
        for t, b in enumerate(ORDERS[q]):
            own = self.bit(b)
            out = out + (1 << b) * ((1 - own) if (k >> (STAGES - 1 - t)) & 1 else own)
        return out

    def send(self, q, t, first=0, number=None):
        channel, rows = q % CHANNELS, self.rows[q]
        slots = 16 >> t
        at, size = first * rows, (slots if number is None else number) * rows
        if t == 0:
            source, sem = self.stage.at[q % 2, at : at + size], self.stage_sems.at[q % 2]
        else:
            start = slots * rows + at
            source, sem = self.landing[t - 1].at[channel, start : start + size], self.send_sems.at[channel, t]
        half = 0 if t == 0 or first >= slots // 2 else 1
        return pltpu.make_async_remote_copy(
            src_ref=source,
            dst_ref=self.landing[t].at[channel, at : at + size],
            send_sem=sem,
            recv_sem=self.recv_sems.at[channel, t, half],
            device_id=self.partner(ORDERS[q][t]),
            device_id_type=MESH_ID,
        )

    def feed(self, q, t, first, number):
        if first + number == 16 >> t and q >= CHANNELS:
            pl.semaphore_wait(self.credits.at[q - CHANNELS, t], 1)
        self.send(q, t, first, number).start()

    def free(self, q, t):
        if q + CHANNELS < self.total:
            pl.semaphore_signal(
                self.credits.at[q, t],
                inc=1,
                device_id=self.partner(ORDERS[q + CHANNELS][t]),
                device_id_type=MESH_ID,
            )

    def upper(self, q, rows, fill):
        self.rows[q] = rows
        if q >= 2:
            self.send(q - 2, 0).wait_send()
        fill(self.stage.at[q % 2], True)
        self.feed(q, 0, 0, 16)
        fill(self.low, False)

    def lower(self, q):
        channel, rows = q % CHANNELS, self.rows[q]
        self.send(q, 0).wait_recv()
        mine = self.landing[0].at[channel]

        def add(i, c):
            r = pl.ds(pl.multiple_of(i * rows, 8), rows)
            mine[r, :] += self.low[r, :]
            return c

        lax.fori_loop(0, 16, add, 0)

    def fold(self, q, t, half):
        channel, rows = q % CHANNELS, self.rows[q]
        number = 8 >> t
        first = number if half == 0 else 0
        self.send(q, t, first, number).wait_recv()
        mine, before = self.landing[t].at[channel], self.landing[t - 1].at[channel]

        def add(i, c):
            r = pl.ds(pl.multiple_of(i * rows, 8), rows)
            mine[r, :] += before[r, :]
            return c

        lax.fori_loop(first, first + number, add, 0)
        if half == 1:
            self.send(q, t).wait_send()
            self.free(q, t - 1)

    def last(self, q, done):
        channel, rows = q % CHANNELS, self.rows[q]
        t = STAGES - 1
        self.send(q, t).wait_recv()
        done(self.landing[t][channel, 0:rows, :] + self.landing[t - 1][channel, 0:rows, :])
        self.send(q, t).wait_send()
        self.free(q, t - 1)
        self.free(q, t)


class Spread:
    def __init__(self, scatter, block, landing, whole, sems):
        self.scatter, self.block, self.landing, self.whole, self.sems = scatter, block, landing, whole, sems
        self.rows = block.shape[0]

    def begin(self, t):
        out = 0
        for i in range(t):
            out = out + self.scatter.bit(i) * (self.rows >> (i + 1))
        return out

    def halving(self, t):
        size = self.rows >> (t + 1)
        at = self.begin(t) + (1 - self.scatter.bit(t)) * size
        return pltpu.make_async_remote_copy(
            src_ref=self.block.at[pl.ds(pl.multiple_of(at, 8), size)],
            dst_ref=self.landing[t],
            send_sem=self.sems.at[0, t],
            recv_sem=self.sems.at[1, t],
            device_id=self.scatter.partner(t),
            device_id_type=MESH_ID,
        )

    def doubling(self, t, arriving=False):
        size = self.rows >> (t + 1)
        at = self.begin(t + 1)
        there = self.begin(t) + (1 - self.scatter.bit(t)) * size if arriving else at
        return pltpu.make_async_remote_copy(
            src_ref=self.whole.at[pl.ds(pl.multiple_of(at, 8), size)],
            dst_ref=self.whole.at[pl.ds(pl.multiple_of(there, 8), size)],
            send_sem=self.sems.at[2, t],
            recv_sem=self.sems.at[3, t],
            device_id=self.scatter.partner(t),
            device_id_type=MESH_ID,
        )

    def step(self, i):
        if i == 0:
            self.halving(0).start()
        elif i <= STAGES:
            t = i - 1
            self.halving(t).wait_recv()
            size = self.rows >> (t + 1)
            r = pl.ds(pl.multiple_of(self.begin(t + 1), 8), size)
            target = self.whole if i == STAGES else self.block
            target[r, :] = self.block[r, :] + self.landing[t][...]
            self.halving(t).wait_send()
            if i < STAGES:
                self.halving(t + 1).start()
            else:
                self.doubling(t).start()
        else:
            t = 2 * STAGES - i
            self.doubling(t, True).wait_recv()
            self.doubling(t).wait_send()
            if t > 0:
                self.doubling(t - 1).start()


def one_hot(rows, target):
    lane = lax.broadcasted_iota(jnp.int32, (rows, target.shape[1]), 0)
    return jnp.where(lane == target, 1.0, 0.0).astype(BF16)


def column_parts(width, size):
    column = lax.broadcasted_iota(jnp.int32, (1, width), 1)
    part = jnp.zeros((1, width), jnp.int32)
    for m in range(1, width // size):
        part = part + jnp.where(column >= m * size, 1, 0)
    return column, part


def slot_of(scatter, q, bits, parts, part):
    order = [b for b in ORDERS[q] if b in bits]
    slot = jnp.zeros_like(part)
    for value in range(parts):
        at = 0
        for t, b in enumerate(order):
            own = scatter.bit(b)
            weight = 1 << (len(order) - 1 - t)
            at = at + weight * ((1 - own) if (value >> bits.index(b)) & 1 else own)
        slot = jnp.where(part == value, at, slot)
    return slot


def sum_blocks(gather, slot):
    levels = len(gather.grid.digits)
    yield
    for level in range(levels):
        gather.start(level, slot)
        if level < 2:
            yield
        gather.wait(level, slot)
        size = gather.grid.digits[level][1]
        buffer = gather.buffers[level].at[slot]
        total = sum([buffer[g] for g in range(1, size)], buffer[0])
        if level + 1 < levels:
            gather.own(level + 1, slot)[...] = total
    return total


def norm_gradient(grad, nrm, out, gather, slot, gain_row, shift_row, inv_row, scale, gain_out, shift_out):
    rows, width = grad.shape

    def gate(r, carry):
        n = nrm[r, :]
        value = gain_row * n + shift_row
        sig = sigmoid(value)
        g = grad[r, :] * sig * (1.0 + value * (1.0 - sig))
        grad[r, :] = g
        return carry[0] + column_sum(g), carry[1] + column_sum(g * n)

    zero = jnp.zeros((1, width), F32)
    shift_sum, gain_sum = row_loop(rows, gate, (zero, zero))
    own = gather.own(0, slot)
    put_row(own, 0, shift_sum, width)
    put_row(own, 8, gain_sum, width)
    total = yield from sum_blocks(gather, slot)
    shift_sum = take_row(total, 0, width)
    gain_sum = take_row(total, 8, width)
    shift_out[...] = shift_sum
    gain_out[...] = gain_sum
    factor = gain_row * inv_row
    shift_mean = shift_sum * scale
    gain_mean = gain_sum * scale

    def write(r, c):
        out[r, :] = (factor * (grad[r, :] - shift_mean - nrm[r, :] * gain_mean)).astype(BF16)
        return c

    row_loop(rows, write, 0)


D1_ROWS = 104
GX = 512
REP_ROWS = 2304


def backward_kernel(
    grid,
    latent,
    x_hbm,
    w1_hbm,
    outw_hbm,
    nrm_hbm0,
    nrm_hbm1,
    nrm_hbm2,
    nrm_hbm3,
    act1_hbm,
    act2_hbm,
    act3_hbm,
    xt_hbm,
    act4_ref,
    zlat_ref,
    head_ref_in,
    noise_ref,
    gid_ref,
    ggroup_ref,
    inv_ref,
    outb_ref,
    w2_ref,
    head_ref,
    d1_ref,
    d2_ref,
    gain_ref,
    shift_ref,
    g_out,
    gx_out,
    out25,
    enc_part,
    nar_part,
    d1_out,
    headw_out,
    outb_out,
    headb_out,
    gain_out,
    shift_out,
    *rest,
):
    levels = len(grid.digits)
    rest = list(rest)

    def take(n):
        got = rest[:n]
        del rest[:n]
        return got

    small, s_send, s_recv = take(levels), take(levels), take(levels)
    stage, low, *landing = take(2 + STAGES)
    stage_sems, send_sems, recv_sems, credits = take(4)
    rep_block, rep_whole, *rep_landing = take(2 + STAGES)
    (rep_sems,) = take(1)
    g_win, wide, gact, gpre4, gpre3, gpre2, gpre1, ghead, gcell, lhs, nrm_buf, fin = take(12)
    distinct = sorted(set(ORDERS[: -(-x_hbm.shape[1] // WIN)]))
    lhs_at = [distinct.index(o) if o in distinct else None for o in ORDERS]
    picked = lhs.at[0, 0:512]
    in_sems, g_sems, nrm_sems, xt_sem, act_sems, gx_sems = take(6)

    rows, genes = x_hbm.shape
    hidden = w2_ref.shape[0]
    spans = windows(genes)
    count = len(spans)
    cell_total = float(rows * grid.n)
    total = 2 * count + 2
    gather = Gather(grid, small, s_send, s_recv)
    first = count
    scatter = Scatter(grid, total, stage, low, landing, stage_sems, send_sems, recv_sems, credits)
    spread = Spread(scatter, rep_block, rep_landing, rep_whole, rep_sems)
    rep_outb = 7 * (D1_ROWS + 2 * latent)
    rep_headb = rep_outb + 8 * count

    peers = digit_peers(grid)
    greet(grid, peers)
    nrm_loads = {
        k: pltpu.make_async_copy(ref, nrm_buf.at[(k + 1) % 2], nrm_sems.at[k])
        for k, ref in enumerate((nrm_hbm0, nrm_hbm1, nrm_hbm2, nrm_hbm3))
    }
    nrm_loads[3].start()
    nrm_loads[2].start()


    def out_fill(s):
        buffer = g_win.at[s % 3]

        def fill(target, is_upper):
            first = hidden // 2 if is_upper else 0
            part = nn(lhs[lhs_at[s], first : first + hidden // 2, :], buffer[...])
            for c in range(WIN // 128):
                target[pl.ds(c, hidden // 2, stride=8), :] = part[:, 128 * c : 128 * (c + 1)]

        return fill

    def out_lhs(q):
        if ORDERS[q] in ORDERS[:q]:
            return
        mine = lhs.at[lhs_at[q]]
        column, part = column_parts(hidden, hidden // PARTS)
        slot = slot_of(scatter, q, (0, 1, 2, 3, 4), PARTS, part)
        target = column + (hidden // PARTS) * (slot - part)
        block = hidden // 5

        def some(i, c):
            at = pl.multiple_of(i * block, block)
            mine[pl.ds(at, block), :] = nt(one_hot(block, target - at), act4_ref[...]).astype(BF16)
            return c

        lax.fori_loop(0, 5, some, 0)

    def out_done(s):
        def done(value):
            fin[...] = value
            for c in range(WIN // 128):
                out25[:, WIN * s + 128 * c : WIN * s + 128 * (c + 1)] = fin[pl.ds(c, hidden // PARTS, stride=8), :]

        return done

    done = {s: out_done(s) for s in range(count)}
    pieces = {}
    for s in range(count):
        pieces[s] = (SLOT_ROWS, out_fill(s))

    plan = list(PLAN)

    def run(chain, cells=None):
        while plan:
            what, *which = plan[0]
            if what == C:
                if next(chain, None) is None:
                    return
            elif what == U:
                if which[0] < count:
                    out_lhs(which[0])
                scatter.upper(which[0], *pieces[which[0]])
            elif what == L:
                scatter.lower(which[0])
            elif what == S:
                scatter.feed(*which)
            elif what == X:
                cells(*which)
            elif what == A:
                spread.step(*which)
            elif which[1] < STAGES - 1:
                scatter.fold(*which)
            else:
                scatter.last(which[0], done[which[0]])
            del plan[0]

    def output_layer(w_ring, w_tail, x_ring, x_tail):
        def load(s):
            at, size = spans[s]
            tail = s == count - 1
            return (
                pltpu.make_async_copy(
                    outw_hbm.at[:, pl.ds(at, size)], w_tail if tail else w_ring.at[s % 3], in_sems.at[0, s]
                ),
                pltpu.make_async_copy(
                    x_hbm.at[:, pl.ds(at, size)], x_tail if tail else x_ring.at[s % 2], in_sems.at[1, s]
                ),
            )

        def save(s):
            return pltpu.make_async_copy(g_win.at[s % 3], g_out.at[:, pl.ds(WIN * s, WIN)], g_sems.at[s])

        def layers():
            for s in range(2):
                for copy in load(s):
                    copy.start()
            for s in range(count):
                yield from layer(s)

        def layer(s):
            at, size = spans[s]
            tail = s == count - 1
            w = w_tail if tail else w_ring.at[s % 3]
            x = x_tail if tail else x_ring.at[s % 2]
            for copy in load(s):
                copy.wait()
            wide[:, 0:size] = nn(act4_ref[...], w[...])
            bias = outb_ref[:, at : at + size]
            if s >= 3:
                save(s - 3).wait()
            g = g_win.at[s % 3]

            def residual(r, c):
                value = wide[r, 0:size] + bias - x[r, :].astype(F32)
                value = (value * (2.0 / cell_total)).astype(BF16)
                g[r, 0:size] = value
                return c + column_sum(value.astype(F32))

            put_row(rep_block, rep_outb + 8 * s, row_loop(rows, residual, jnp.zeros((1, size), F32)), size)
            if size < WIN:
                g[:, size:WIN] = jnp.zeros((rows, WIN - size), BF16)
            save(s).start()
            if s == 0:
                meet(peers)
            if s + 2 < count:
                for copy in load(s + 2):
                    copy.start()
            yield 0
            part = nt(g[:, 0:size], w[...])
            gact[...] = part if s == 0 else gact[...] + part
            yield 0

        run(layers())
        for s in range(count - 3, count):
            save(s).wait()

    pl.run_scoped(
        output_layer,
        pltpu.VMEM((3, hidden, WIN), BF16),
        pltpu.VMEM((hidden, spans[-1][1]), BF16),
        pltpu.VMEM((2, rows, WIN), BF16),
        pltpu.VMEM((rows, spans[-1][1]), BF16),
    )


    def pack(target, at, source, row, height):
        full = hidden // 128
        for c in range(full):
            target[pl.ds(pl.multiple_of(at + height * c, 8), height), :] = source[
                pl.ds(row, height), 128 * c : 128 * (c + 1)
            ]
        rest_width = hidden - 128 * full
        pieces = [source[pl.ds(row + 8 * i, 8), 128 * full : hidden] for i in range(height // 8)]
        target[pl.ds(pl.multiple_of(at + height * full, 8), 8), 0 : rest_width * len(pieces)] = jnp.concatenate(
            pieces, axis=1
        )

    def unpack(value, out, row, height):
        full = hidden // 128
        rest_width = hidden - 128 * full
        for c in range(full):
            out[row : row + height, 128 * c : 128 * (c + 1)] = value[height * c : height * (c + 1), :]
        for i in range(height // 8):
            out[row + 8 * i : row + 8 * i + 8, 128 * full : hidden] = value[
                height * full : height * full + 8, rest_width * i : rest_width * (i + 1)
            ]

    def finish(xt, act_buf, w1_ring, w1_tail, gx_ring):
        xt_load = pltpu.make_async_copy(xt_hbm, xt, xt_sem)
        xt_load.start()

        gx_spans = windows(genes, GX)

        def gx_load(i):
            at, size = gx_spans[i]
            return (
                pltpu.make_async_copy(
                    w1_hbm.at[:, pl.ds(at, size)], w1_ring.at[i % 2] if size == GX else w1_tail, gx_sems.at[0, i]
                ),
                pltpu.make_async_copy(
                    g_out.at[:, pl.ds(at, GX)], g_win.at[i % 2, :, pl.ds(0, GX)], gx_sems.at[1, i]
                ),
            )

        def gx_save(i):
            return pltpu.make_async_copy(gx_ring.at[i % 2], gx_out.at[:, pl.ds(GX * i, GX)], gx_sems.at[2, i])

        def grad_cells(i):
            at, size = gx_spans[i]
            if i == 0:
                for copy in gx_load(0):
                    copy.start()
            if i + 1 < len(gx_spans):
                for copy in gx_load(i + 1):
                    copy.start()
            for copy in gx_load(i):
                copy.wait()
            if i >= 2:
                gx_save(i - 2).wait()
            wide[:, 0:size] = nn(gpre1[...], w1_ring[i % 2] if size == GX else w1_tail[...])

            def write(r, c):
                value = wide[r, 0:size] - g_win[i % 2, r, 0:size].astype(F32)
                gx_ring[i % 2, r, 0:size] = (cell_total * value).astype(BF16)
                return c

            row_loop(rows, write, 0)
            gx_save(i).start()
            if i + 1 == len(gx_spans):
                gx_save(i - 1).wait()
                gx_save(i).wait()

        def enc_fill(q, s):
            def fill(target, is_upper):
                for i in range(16):
                    j = scatter.part(q, 16 + i if is_upper else i)
                    picked[32 * i : 32 * i + 32, :] = xt[j, 32 * s : 32 * s + 32, :]
                wide[0:512, 0:hidden] = nn(picked[...], gpre1[...])

                def one(i, c):
                    pack(target, i * SLOT_ROWS, wide, pl.multiple_of(i * 32, 32), 32)
                    return c

                lax.fori_loop(0, 16, one, 0)

            return fill

        def enc_done(s):
            return lambda value: unpack(value, enc_part, 32 * s, 32)

        each = 2 * hidden // PARTS
        skip = (0, 32)

        def nar_fill(q, which):
            height_here = 32 if which == 0 else 24
            rows_here = 25 * 8 if which == 0 else 19 * 8
            place = STAGES - 1 - ORDERS[q].index(4)

            def fill(target, is_upper):
                column, part = column_parts(hidden, each)
                slot = slot_of(scatter, q, (0, 1, 2, 3), PARTS // 2, part)
                line = column - each * part - skip[which]
                inside = (line >= 0) & (line < height_here)
                base = 8 if is_upper else 0
                place_in = jnp.where(inside, (slot - base) * height_here + line, -1)
                place_in = jnp.where((slot >= base) & (slot < base + 8), place_in, -1)
                select = one_hot(8 * height_here, place_in)
                for matrix, act_slot, grad in ((0, 0, gpre2), (1, 1, gpre4)):
                    size = 8 * height_here
                    picked[0:size, :] = nt(select, act_buf[act_slot]).astype(BF16)
                    wide[0:size, 0:hidden] = nn(picked[0:size, :], grad[...])
                    flip = scatter.bit(4) if matrix == 0 else 1 - scatter.bit(4)
                    for i in range(8):
                        k = (i >> place) * (2 << place) + (i & ((1 << place) - 1)) + flip * (1 << place)
                        pack(target, k * rows_here, wide, i * height_here, height_here)

            return rows_here, fill

        def nar_done(which):
            if which == 0:
                return lambda value: unpack(value, nar_part, 0, 32)
            return lambda value: unpack(value, nar_part, 32, 24)

        for which in range(2):
            done[first + which] = nar_done(which)
            pieces[first + which] = nar_fill(first + which, which)
        for s in range(count):
            done[first + 2 + s] = enc_done(s)
            pieces[first + 2 + s] = (SLOT_ROWS, enc_fill(first + 2 + s, s))

        def row(ref, k):
            return ref[k : k + 1, :]

        def back(k, grad, out):
            nrm_loads[k].wait()
            return norm_gradient(
                grad,
                nrm_buf.at[(k + 1) % 2],
                out,
                gather,
                k,
                row(gain_ref, k),
                row(shift_ref, k),
                row(inv_ref, k),
                1.0 / cell_total,
                gain_out.at[k : k + 1, :],
                shift_out.at[k : k + 1, :],
            )

        act_loads = [
            pltpu.make_async_copy(ref, act_buf.at[at], act_sems.at[i])
            for i, (ref, at) in enumerate(((act1_hbm, 0), (act3_hbm, 1), (act2_hbm, 0)))
        ]
        act_loads[1].start()
        act_loads[2].start()

        def latent_side():
            act_loads[2].wait()
            d1_grad = tn(zlat_ref[...], gpre3[...])
            headw_grad = tn(ghead[...], act_buf[0])
            act_loads[0].start()
            for c in range(-(-hidden // 128)):
                size = min(128, hidden - 128 * c)
                at = D1_ROWS * c
                rep_block[at : at + latent, 0:size] = d1_grad[:, 128 * c : 128 * c + size]
                at = 7 * D1_ROWS + 2 * latent * c
                rep_block[at : at + 2 * latent, 0:size] = headw_grad[:, 128 * c : 128 * c + size]
            put_row(rep_block, rep_headb, column_sum(ghead[...].astype(F32)), 2 * latent)

        def chain():
            for k, out in ((3, gpre4), (2, gpre3), (1, gpre2), (0, gpre1)):
                waits = back(k, gact, out)
                for at, _ in enumerate(waits):
                    if (k, at) == (3, 1):
                        groups = ggroup_ref.shape[0]
                        member = (lax.broadcasted_iota(jnp.int32, (groups, rows), 0) == gid_ref[...]).astype(F32)
                        gcell[...] = exact(member, ggroup_ref[...], ((0,), (0,)))
                    if (k, at) == (1, 1):
                        latent_side()
                    yield 0
                if k == 3:
                    nrm_loads[1].start()
                    gact[...] = nt(gpre4[...], d2_ref[...])
                elif k == 2:
                    nrm_loads[0].start()
                    grad_z = nt(gpre3[...], d1_ref[...])
                    mu = head_ref_in[:, 0:latent]
                    logvar = head_ref_in[:, latent : 2 * latent]
                    kl = KL_WEIGHT * genes / cell_total
                    deviation = jnp.exp(0.5 * logvar)
                    grad_mu = grad_z + kl * mu + gcell[:, 0:latent]
                    grad_logvar = grad_z * noise_ref[...].T * (0.5 * deviation) + 0.5 * kl * (jnp.exp(logvar) - 1.0)
                    ghead[...] = jnp.concatenate([grad_mu, grad_logvar], axis=1).astype(BF16)
                    gact[...] = nn(ghead[...], head_ref[...])
                elif k == 1:
                    gact[...] = nt(gpre2[...], w2_ref[...])
                else:
                    for copy in act_loads[:2]:
                        copy.wait()
                    xt_load.wait()
                yield 0

        run(chain(), grad_cells)
        for q in (total - 2, total - 1):
            scatter.send(q, 0).wait_send()
        for c in range(-(-hidden // 128)):
            size = min(128, hidden - 128 * c)
            at = D1_ROWS * c
            d1_out[:, 128 * c : 128 * c + size] = rep_whole[at : at + latent, 0:size]
            at = 7 * D1_ROWS + 2 * latent * c
            headw_out[:, 128 * c : 128 * c + size] = rep_whole[at : at + 2 * latent, 0:size]
        outb_out[...] = rep_whole[rep_outb : rep_outb + 8 * count, :]
        headb_out[...] = rep_whole[rep_headb : rep_headb + 8, :]
        for level in range(levels):
            for k in range(4):
                gather.finish(level, k)

    pl.run_scoped(
        finish,
        pltpu.VMEM(xt_hbm.shape, BF16),
        pltpu.VMEM((2, rows, hidden), BF16),
        pltpu.VMEM((2, hidden, GX), BF16),
        pltpu.VMEM((hidden, windows(genes, GX)[-1][1]), BF16),
        pltpu.VMEM((2, rows, GX), BF16),
    )


def call_backward(grid, kept, cells_x, w1t, out_w, noise, gid, out_b, w2, headt, d1, d2, gain, shift):
    (nrm0, nrm1, nrm2, nrm3, inv, act1, act2, zlat, act3, act4, head, ggroup, xt) = kept
    rows, genes = cells_x.shape
    hidden, latent = w2.shape[0], d1.shape[0]
    spans = windows(genes)
    count = len(spans)
    vm = pl.BlockSpec(memory_space=pltpu.VMEM)
    hbm = pl.BlockSpec(memory_space=pl.ANY)
    shape = jax.ShapeDtypeStruct
    out_shape = (
        shape((rows, WIN * count), BF16),
        shape((rows, WIN * count), BF16),
        shape((hidden // PARTS, WIN * count), F32),
        shape((32 * count, hidden), F32),
        shape((56, hidden), F32),
        shape((latent, hidden), F32),
        shape((2 * latent, hidden), F32),
        shape((8 * count, 128), F32),
        shape((8, 128), F32),
        shape((4, hidden), F32),
        shape((4, hidden), F32),
    )
    dma = pltpu.SemaphoreType.DMA
    scratch = (
        [pltpu.VMEM((4, size, 16, 128), F32) for _, size in grid.digits]
        + [dma((4, size - 1)) for _, size in grid.digits]
        + [dma((4, size - 1)) for _, size in grid.digits]
        + [pltpu.VMEM((2, 16 * SLOT_ROWS, 128), F32), pltpu.VMEM((16 * SLOT_ROWS, 128), F32)]
        + [pltpu.VMEM((CHANNELS, (16 >> t) * SLOT_ROWS, 128), F32) for t in range(STAGES)]
        + [dma((2,)), dma((CHANNELS, STAGES)), dma((CHANNELS, STAGES, 2)), pltpu.SemaphoreType.REGULAR((2 * count + 2 - CHANNELS, STAGES))]
        + [pltpu.VMEM((REP_ROWS, 128), F32), pltpu.VMEM((REP_ROWS, 128), F32)]
        + [pltpu.VMEM((REP_ROWS >> (t + 1), 128), F32) for t in range(STAGES)]
        + [dma((4, STAGES))]
        + [
            pltpu.VMEM((3, rows, WIN), BF16),
            pltpu.VMEM((rows, WIN), F32),
            pltpu.VMEM((rows, hidden), F32),
            pltpu.VMEM((rows, hidden), BF16),
            pltpu.VMEM((rows, hidden), BF16),
            pltpu.VMEM((rows, hidden), BF16),
            pltpu.VMEM((rows, hidden), BF16),
            pltpu.VMEM((rows, 2 * latent), BF16),
            pltpu.VMEM((rows, 128), F32),
            pltpu.VMEM((len(set(ORDERS[:count])), hidden, rows), BF16),
            pltpu.VMEM((2, rows, hidden), F32),
            pltpu.VMEM((SLOT_ROWS, 128), F32),
        ]
        + [dma((2, count)), dma((count,)), dma((4,)), dma, dma((3,)), dma((3, len(windows(genes, GX))))]
    )
    return pl.pallas_call(
        functools.partial(backward_kernel, grid, latent),
        out_shape=out_shape,
        in_specs=[hbm] * 11 + [vm] * 14,
        out_specs=[hbm] * 2 + [vm] * (len(out_shape) - 2),
        scratch_shapes=scratch,
        name="backward",
        compiler_params=pltpu.CompilerParams(
            collective_id=1, has_side_effects=True, vmem_limit_bytes=63 * 2**20
        ),
    )(
        cells_x,
        w1t,
        out_w,
        nrm0,
        nrm1,
        nrm2,
        nrm3,
        act1,
        act2,
        act3,
        xt,
        act4,
        zlat,
        head,
        noise,
        gid,
        ggroup,
        inv,
        out_b,
        w2,
        headt,
        d1,
        d2,
        gain,
        shift,
    )


def flat_shard(grid, flat, columns, rows_in_all):
    value = flat.reshape(rows_in_all // PARTS, columns)
    size = grid.n // PARTS
    if size > 1:
        groups = [list(range(size * p, size * p + size)) for p in range(PARTS)]
        value = lax.psum_scatter(
            value, ("cells", "rep"), scatter_dimension=0, axis_index_groups=groups, tiled=True
        )
    return value


def group_sum(grid, values):
    size = grid.n // PARTS
    if size > 1:
        groups = [list(range(size * p, size * p + size)) for p in range(PARTS)]
        values = lax.psum(values, ("cells", "rep"), axis_index_groups=groups)
    return values


def shards(
    grid,
    cells_x,
    latent_noise,
    group_ids,
    owner_table,
    owner_mask,
    enc_w1,
    enc_w2,
    head_w,
    head_b,
    dec_w1,
    dec_w2,
    out_w,
    out_b,
    bn_gain,
    bn_shift,
):
    cell_total = float(cells_x.shape[0] * grid.n)
    genes = cells_x.shape[1]
    hidden = enc_w2.shape[0]
    gid = group_ids.reshape(1, -1)
    headt = head_w.T
    w1t = enc_w1.T
    noise = latent_noise.T
    *kept, offsets = call_forward(
        grid,
        cells_x,
        w1t,
        noise,
        gid,
        owner_table.T,
        owner_mask.T,
        enc_w2,
        headt,
        head_b.reshape(1, -1),
        dec_w1,
        dec_w2,
        bn_gain,
        bn_shift,
    )
    _, gx, out25, enc_part, nar_part, d1_grad, headw_grad, outb_grad, headb_grad, grad_gain, grad_shift = call_backward(
        grid,
        kept,
        cells_x,
        w1t,
        out_w,
        noise,
        gid,
        out_b.reshape(1, -1),
        enc_w2,
        headt,
        dec_w1,
        dec_w2,
        bn_gain,
        bn_shift,
    )
    grad_x = gx[:, :genes].astype(F32)
    part = grid.me() // (grid.n // PARTS)
    each = genes * hidden // PARTS
    enc_flat = lax.dynamic_slice_in_dim(enc_part.reshape(-1), (genes * part) % PARTS * (hidden // PARTS), each)
    shard_enc = flat_shard(grid, enc_flat, FLAT_COLS, FLAT_ROWS)
    shard_out = flat_shard(grid, out25[:, :genes], FLAT_COLS, FLAT_ROWS)
    shard_narrow = flat_shard(grid, nar_part[: 2 * hidden // PARTS], NARROW_COLS, NARROW_ROWS)
    headw_grad, d1_grad, headb_grad, outb_grad = group_sum(
        grid,
        (headw_grad.T, d1_grad, headb_grad.reshape(-1)[: head_b.shape[0]], outb_grad.reshape(-1)[:genes]),
    )
    return (
        grad_x,
        shard_enc,
        shard_narrow,
        headw_grad,
        d1_grad,
        headb_grad,
        shard_out,
        outb_grad,
        grad_gain,
        grad_shift,
        offsets[None],
    )


def solution(mesh):
    grid = Slice(mesh.shape["cells"], mesh.shape["rep"])
    lines = P(("cells", "rep"), None)
    return jax.shard_map(
        functools.partial(shards, grid),
        mesh=mesh,
        in_specs=(lines, lines, P(("cells", "rep"))) + (P(),) * 12,
        out_specs=(lines, lines, lines, P(), P(), P(), lines, P(), P(), P(), P("cells", None, None)),
        check_vma=False,
    )
```

```python
import functools

import jax
import jax.numpy as jnp
from jax import lax
from jax.experimental import pallas as pl
from jax.experimental.pallas import tpu as pltpu
from jax.sharding import PartitionSpec as P

POP_DEV = 2
FLAT_COLS = 875
NARROW_COLS = 625
FLAT_ROWS = 6400
NARROW_ROWS = 2048

NORM_EPSILON = 1e-05
KL_WEIGHT = 5e-05
OFFSET_WEIGHT = 200.0

MESH_ID = pl.DeviceIdType.MESH
WIN = 1024
ROWS = 48
F32 = jnp.float32
BF16 = jnp.bfloat16


class Slice:
    def __init__(self, cells, rep):
        self.cells, self.rep = cells, rep
        self.n = cells * rep
        self.bits = self.n.bit_length() - 1
        self.digits = []
        low = 0
        while low < self.bits:
            width = min(3, self.bits - low)
            self.digits.append((low, 1 << width))
            low += width

    def me(self):
        return lax.axis_index("cells") * self.rep + lax.axis_index("rep")

    def place(self, index):
        return (index // self.rep, index % self.rep)


def greet(grid, peers):
    barrier = pltpu.get_barrier_semaphore()
    for peer in peers:
        pl.semaphore_signal(barrier, inc=1, device_id=grid.place(peer), device_id_type=MESH_ID)


def meet(peers):
    pl.semaphore_wait(pltpu.get_barrier_semaphore(), len(peers))


def digit_peers(grid):
    me = grid.me()
    peers = []
    for low, size in grid.digits:
        rank = (me // (1 << low)) % size
        for k in range(1, size):
            other = (rank + k) % size
            peers.append(me + (other - rank) * (1 << low))
    return peers


class Gather:
    def __init__(self, grid, buffers, send_sems, recv_sems):
        self.grid, self.buffers, self.send_sems, self.recv_sems = grid, buffers, send_sems, recv_sems

    def rank(self, level):
        low, size = self.grid.digits[level]
        return (self.grid.me() // (1 << low)) % size

    def copy(self, level, slot, k, arriving=False):
        low, size = self.grid.digits[level]
        rank = self.rank(level)
        to = (rank + k) % size
        buffer = self.buffers[level].at[slot]
        return pltpu.make_async_remote_copy(
            src_ref=buffer.at[rank],
            dst_ref=buffer.at[(rank + size - k) % size if arriving else rank],
            send_sem=self.send_sems[level].at[slot, k - 1],
            recv_sem=self.recv_sems[level].at[slot, k - 1],
            device_id=self.grid.place(self.grid.me() + (to - rank) * (1 << low)),
            device_id_type=MESH_ID,
        )

    def start(self, level, slot):
        for k in range(1, self.grid.digits[level][1]):
            self.copy(level, slot, k).start()

    def wait(self, level, slot):
        for k in range(1, self.grid.digits[level][1]):
            self.copy(level, slot, k, arriving=True).wait_recv()

    def finish(self, level, slot):
        for k in range(1, self.grid.digits[level][1]):
            self.copy(level, slot, k).wait_send()

    def own(self, level, slot):
        return self.buffers[level].at[slot, self.rank(level)]


def put_row(ref, first, row, width):
    full = width // 128
    for c in range(full):
        ref[first + c : first + c + 1, :] = row[:, 128 * c : 128 * (c + 1)]
    rest = width - 128 * full
    if rest:
        ref[first + full : first + full + 1, 0:rest] = row[:, 128 * full : width]


def take_row(block, first, width):
    pieces = []
    for c in range(-(-width // 128)):
        pieces.append(block[first + c : first + c + 1, 0 : min(128, width - 128 * c)])
    return jnp.concatenate(pieces, axis=1)


def row_loop(rows, body, init):
    steps = rows // ROWS

    def step(i, carry):
        return body(pl.ds(pl.multiple_of(i * ROWS, ROWS), ROWS), carry)

    return lax.fori_loop(0, steps, step, init)


def sigmoid(value):
    return 0.5 * jnp.tanh(0.5 * value) + 0.5


def column_sum(value):
    return jnp.sum(value, axis=0, keepdims=True)


PARTS = 32


def batch_norm(pre, nrm_out, act_out, gather, slot, gain_row, shift_row, inv_out, idle):
    rows, width = pre.shape
    total = row_loop(rows, lambda r, c: c + column_sum(pre[r, :]), jnp.zeros((1, width), F32))
    mean = total * (1.0 / rows)

    def squares(r, c):
        d = pre[r, :] - mean
        return c + column_sum(d * d)

    square = row_loop(rows, squares, jnp.zeros((1, width), F32))
    own = gather.own(0, slot)
    put_row(own, 0, mean, width)
    put_row(own, 8, square, width)
    count = float(rows)
    levels = len(gather.grid.digits)
    for level in range(levels):
        size = gather.grid.digits[level][1]
        gather.start(level, slot)
        idle(level)
        gather.wait(level, slot)
        buffer = gather.buffers[level].at[slot]
        means = [buffer[g, 0:8, :] for g in range(size)]
        merged = sum(means[1:], means[0]) * (1.0 / size)
        spread = sum([buffer[g, 8:16, :] for g in range(1, size)], buffer[0, 8:16, :])
        between = sum([(m - merged) * (m - merged) for m in means[1:]], (means[0] - merged) * (means[0] - merged))
        spread = spread + count * between
        count = count * size
        if level + 1 < levels:
            own = gather.own(level + 1, slot)
            own[0:8, :] = merged
            own[8:16, :] = spread
    inv = lax.rsqrt(spread * (1.0 / count) + NORM_EPSILON)
    mean = take_row(merged, 0, width)
    inv = take_row(inv, 0, width)
    inv_out[...] = inv

    def write(r, c):
        nrm = (pre[r, :] - mean) * inv
        nrm_out[r, :] = nrm
        value = gain_row * nrm + shift_row
        act_out[r, :] = (value * sigmoid(value)).astype(BF16)
        return c

    row_loop(rows, write, 0)


def nt(left, right):
    return lax.dot_general(left, right, (((1,), (1,)), ((), ())), preferred_element_type=F32)


def nn(left, right):
    return lax.dot_general(left, right, (((1,), (0,)), ((), ())), preferred_element_type=F32)


def tn(left, right):
    return lax.dot_general(left, right, (((0,), (0,)), ((), ())), preferred_element_type=F32)


def exact(left, right, dims):
    return lax.dot_general(
        left, right, (dims, ((), ())), precision=lax.Precision.HIGHEST, preferred_element_type=F32
    )


WIDE = 1024
AHEAD = 3


def windows(width, size=WIN):
    return [(s, min(size, width - s)) for s in range(0, width, size)]


def part_of(full, tail, i):
    return full.at[i] if i < full.shape[0] else tail


def forward_kernel(
    grid,
    table_ref,
    mask_ref,
    x_hbm,
    w1_hbm,
    noise_ref,
    gid_ref,
    w2_ref,
    head_ref,
    headb_ref,
    d1_ref,
    d2_ref,
    gain_ref,
    shift_ref,
    nrm0_hbm,
    nrm1_hbm,
    nrm2_hbm,
    nrm3_hbm,
    inv_out,
    act1_hbm,
    act2_hbm,
    zlat,
    act3_hbm,
    act4,
    head_out,
    ggroup_out,
    xt_out,
    offsets_out,
    x_all,
    xt,
    w_win,
    w_tail,
    pre,
    moments,
    *rest,
):
    levels = len(grid.digits)
    small = rest[:levels]
    wide = rest[levels : 2 * levels]
    s_send, s_recv, g_send, g_recv = (
        rest[2 * levels : 3 * levels],
        rest[3 * levels : 4 * levels],
        rest[4 * levels : 5 * levels],
        rest[5 * levels : 6 * levels],
    )
    in_sems, xt_sems, nrm_keep, act_keep, keep_sems = rest[6 * levels :]
    act1, act2, act3 = (act_keep.at[i] for i in range(3))
    gather = Gather(grid, small, s_send, s_recv)
    group_gather = Gather(grid, wide, g_send, g_recv)
    latent = d1_ref.shape[0]
    genes = x_hbm.shape[1]
    spans = windows(genes, WIDE)

    peers = digit_peers(grid)
    greet(grid, peers)
    loads = []
    for i, (s, size) in enumerate(spans):
        a = pltpu.make_async_copy(x_hbm.at[:, pl.ds(s, size)], x_all.at[:, pl.ds(s, size)], in_sems.at[0, i])
        b = pltpu.make_async_copy(w1_hbm.at[:, pl.ds(s, size)], part_of(w_win, w_tail, i), in_sems.at[1, i])
        if i < AHEAD:
            a.start()
            b.start()
        loads.append((a, b))

    for i, (s, size) in enumerate(spans):
        loads[i][0].wait()
        loads[i][1].wait()
        if i + AHEAD < len(loads):
            for copy in loads[i + AHEAD]:
                copy.start()
        part = nt(x_all[:, s : s + size], part_of(w_win, w_tail, i)[...])
        pre[...] = part if i == 0 else pre[...] + part

    starts = [(genes * j) // PARTS for j in range(PARTS)]
    parts_left = list(range(PARTS))

    def save(j):
        return pltpu.make_async_copy(xt.at[j], xt_out.at[j], xt_sems.at[j])

    def transpose(level):
        for j in parts_left[: -(-PARTS // 6)]:
            at = starts[j] // 128 * 128
            size = min(384, genes - at)
            lane = lax.broadcasted_iota(jnp.int32, (xt.shape[1], size), 1)
            line = lax.broadcasted_iota(jnp.int32, (xt.shape[1], size), 0)
            select = jnp.where(lane == line + (starts[j] - at), 1.0, 0.0).astype(BF16)
            xt[j] = nt(select, x_all[:, at : at + size]).astype(BF16)
            save(j).start()
            parts_left.remove(j)

    kept = [
        pltpu.make_async_copy(nrm_keep.at[k], ref, keep_sems.at[0, k])
        for k, ref in enumerate((nrm0_hbm, nrm1_hbm, nrm2_hbm, nrm3_hbm))
    ] + [
        pltpu.make_async_copy(act_keep.at[k], ref, keep_sems.at[1, k])
        for k, ref in enumerate((act1_hbm, act2_hbm, act3_hbm))
    ]

    def norm(k, act, idle=transpose):
        batch_norm(
            pre,
            nrm_keep.at[k],
            act,
            gather,
            k,
            gain_ref[k : k + 1, :],
            shift_ref[k : k + 1, :],
            inv_out.at[k : k + 1, :],
            idle,
        )
        kept[k].start()
        if k < 3:
            kept[4 + k].start()

    meet(peers)
    norm(0, act1)
    pre[...] = nn(act1[...], w2_ref[...])
    norm(1, act2)
    head = nt(act2[...], head_ref[...]) + headb_ref[...]
    head_out[...] = head
    mu = head[:, 0:latent]
    logvar = head[:, latent : 2 * latent]
    zlat[...] = (mu + jnp.exp(0.5 * logvar) * noise_ref[...].T).astype(BF16)

    groups = ggroup_out.shape[0]
    pops = groups // 2
    cells_here = gid_ref.shape[1]
    member = (lax.broadcasted_iota(jnp.int32, (groups, cells_here), 0) == gid_ref[...]).astype(F32)
    own = group_gather.own(0, 0)
    own[:, 0:latent] = exact(member, mu, ((1,), (0,)))
    own[:, latent : latent + 1] = jnp.sum(member, axis=1, keepdims=True)
    group_gather.start(0, 0)

    pre[...] = nn(zlat[...], d1_ref[...])
    norm(2, act3)

    def group_level(level):
        group_gather.wait(level, 0)
        size = grid.digits[level][1]
        buffer = wide[level].at[0]
        total = sum([buffer[g] for g in range(1, size)], buffer[0])
        if level + 1 < levels:
            group_gather.own(level + 1, 0)[...] = total
            group_gather.start(level + 1, 0)
            return
        counted = jnp.maximum(total[:, latent : latent + 1], 1.0)
        moments[...] = total / counted
        odd, even = pl.ds(1, pops, stride=2), pl.ds(0, pops, stride=2)
        offset = moments[odd, :] - moments[even, :]
        centre = jnp.sum(offset, axis=0, keepdims=True) * (1.0 / pops)
        grad_offset = (2.0 * OFFSET_WEIGHT / pops) * (offset - centre)
        row = lax.axis_index("cells")
        slots = offsets_out.shape[0]
        lane = lax.broadcasted_iota(jnp.int32, (1, pops), 1)
        picks = jnp.concatenate(
            [jnp.where(lane == table_ref[s, row], mask_ref[s, row].astype(F32), 0.0) for s in range(slots)], axis=0
        )
        offsets_out[...] = exact(picks, offset, ((1,), (0,)))[:, 0:latent]
        moments[odd, :] = grad_offset
        moments[even, :] = -grad_offset
        ggroup_out[...] = moments[...] / counted

    group_level(0)
    pre[...] = nn(act3[...], d2_ref[...])
    norm(3, act4, lambda level: group_level(level) if level else None)
    while parts_left:
        transpose(0)

    for j in range(PARTS):
        save(j).wait()
    for copy in kept:
        copy.wait()
    for level in range(levels):
        for k in range(4):
            gather.finish(level, k)
        group_gather.finish(level, 0)


XT_ROWS = 224


def call_forward(grid, cells_x, w1t, noise, gid, table, mask, w2, headt, headb, d1, d2, gain, shift):
    rows, genes = cells_x.shape
    hidden = w2.shape[0]
    latent = d1.shape[0]
    groups = 2 * POP_DEV * grid.cells
    spans = windows(genes, WIDE)
    count = len(spans)
    levels = len(grid.digits)
    vm = pl.BlockSpec(memory_space=pltpu.VMEM)
    hbm = pl.BlockSpec(memory_space=pl.ANY)
    sm = pl.BlockSpec(memory_space=pltpu.SMEM)
    wide_f = jax.ShapeDtypeStruct((rows, hidden), F32)
    wide_b = jax.ShapeDtypeStruct((rows, hidden), BF16)
    out_shape = (
        wide_f,
        wide_f,
        wide_f,
        wide_f,
        jax.ShapeDtypeStruct((4, hidden), F32),
        wide_b,
        wide_b,
        jax.ShapeDtypeStruct((rows, latent), BF16),
        wide_b,
        wide_b,
        jax.ShapeDtypeStruct((rows, 2 * latent), F32),
        jax.ShapeDtypeStruct((groups, 128), F32),
        jax.ShapeDtypeStruct((PARTS, XT_ROWS, rows), BF16),
        jax.ShapeDtypeStruct((table.shape[0], latent), F32),
    )
    scratch = (
        [
            pltpu.VMEM((rows, genes), BF16),
            pltpu.VMEM((PARTS, XT_ROWS, rows), BF16),
            pltpu.VMEM((count - 1, hidden, WIDE), BF16),
            pltpu.VMEM((hidden, spans[-1][1]), BF16),
            pltpu.VMEM((rows, hidden), F32),
            pltpu.VMEM((groups, 128), F32),
        ]
        + [pltpu.VMEM((4, size, 16, 128), F32) for _, size in grid.digits]
        + [pltpu.VMEM((1, size, groups, 128), F32) for _, size in grid.digits]
        + [pltpu.SemaphoreType.DMA((4, size - 1)) for _, size in grid.digits]
        + [pltpu.SemaphoreType.DMA((4, size - 1)) for _, size in grid.digits]
        + [pltpu.SemaphoreType.DMA((1, size - 1)) for _, size in grid.digits]
        + [pltpu.SemaphoreType.DMA((1, size - 1)) for _, size in grid.digits]
        + [pltpu.SemaphoreType.DMA((2, count)), pltpu.SemaphoreType.DMA((PARTS,))]
        + [
            pltpu.VMEM((4, rows, hidden), F32),
            pltpu.VMEM((3, rows, hidden), BF16),
            pltpu.SemaphoreType.DMA((2, 4)),
        ]
    )
    return pl.pallas_call(
        functools.partial(forward_kernel, grid),
        out_shape=out_shape,
        in_specs=[sm, sm, hbm, hbm] + [vm] * 9,
        out_specs=[hbm] * 4 + [vm, hbm, hbm, vm, hbm, vm, vm, vm, hbm, vm],
        scratch_shapes=scratch,
        name="forward",
        compiler_params=pltpu.CompilerParams(
            collective_id=0, has_side_effects=True, vmem_limit_bytes=60 * 2**20
        ),
    )(table, mask, cells_x, w1t, noise, gid, w2, headt, headb, d1, d2, gain, shift)


ORDERS = (
    (0, 1, 3, 2, 4),
    (0, 2, 1, 3, 4),
    (0, 1, 3, 2, 4),
    (0, 2, 1, 3, 4),
    (0, 2, 1, 3, 4),
    (0, 1, 3, 2, 4),
    (0, 2, 1, 3, 4),
    (0, 1, 3, 2, 4),
    (0, 2, 1, 3, 4),
    (0, 2, 1, 3, 4),
    (0, 1, 2, 3, 4),
    (0, 3, 2, 1, 4),
    (0, 2, 1, 3, 4),
    (0, 1, 3, 2, 4),
    (0, 2, 3, 1, 4),
    (0, 1, 2, 3, 4),
)
C, U, L, S, F, X, A = range(7)
PLAN = (
    (C,),
    (U, 0),
    (C,),
    (C,),
    (L, 0),
    (S, 0, 1, 7, 1),
    (S, 0, 1, 5, 2),
    (U, 1),
    (S, 0, 1, 4, 1),
    (C,),
    (S, 0, 1, 3, 1),
    (C,),
    (L, 1),
    (S, 1, 1, 7, 1),
    (S, 0, 1, 2, 1),
    (S, 1, 1, 6, 1),
    (C,),
    (S, 0, 1, 1, 1),
    (S, 1, 1, 5, 1),
    (C,),
    (F, 0, 1, 0),
    (S, 0, 2, 3, 1),
    (S, 0, 1, 0, 1),
    (S, 1, 1, 4, 1),
    (S, 0, 2, 2, 1),
    (C,),
    (S, 1, 1, 3, 1),
    (S, 0, 2, 1, 1),
    (C,),
    (S, 0, 2, 0, 1),
    (C,),
    (S, 1, 1, 2, 1),
    (U, 2),
    (F, 0, 1, 1),
    (F, 0, 2, 0),
    (F, 1, 1, 0),
    (S, 1, 2, 3, 1),
    (S, 1, 2, 2, 1),
    (S, 1, 1, 0, 2),
    (C,),
    (S, 1, 2, 1, 1),
    (C,),
    (F, 0, 2, 1),
    (L, 2),
    (S, 1, 2, 0, 1),
    (S, 0, 3, 1, 1),
    (S, 0, 3, 0, 1),
    (U, 3),
    (S, 2, 1, 7, 1),
    (C,),
    (F, 1, 1, 1),
    (F, 1, 2, 0),
    (S, 1, 3, 1, 1),
    (S, 2, 1, 6, 1),
    (S, 1, 3, 0, 1),
    (C,),
    (F, 0, 3, 0),
    (F, 1, 2, 1),
    (L, 3),
    (S, 3, 1, 7, 1),
    (C,),
    (C,),
    (S, 2, 1, 4, 2),
    (S, 2, 1, 2, 2),
    (S, 3, 1, 4, 3),
    (S, 3, 1, 3, 1),
    (S, 0, 4, 0, 1),
    (F, 0, 3, 1),
    (F, 1, 3, 0),
    (U, 4),
    (F, 1, 3, 1),
    (C,),
    (S, 2, 1, 1, 1),
    (S, 3, 1, 2, 1),
    (S, 1, 4, 0, 1),
    (F, 2, 1, 0),
    (F, 0, 4, 0),
    (L, 4),
    (S, 2, 2, 3, 1),
    (U, 5),
    (F, 3, 1, 0),
    (S, 2, 1, 0, 1),
    (S, 3, 2, 3, 1),
    (S, 3, 1, 0, 2),
    (S, 2, 2, 2, 1),
    (S, 2, 2, 1, 1),
    (C,),
    (F, 1, 4, 0),
    (L, 5),
    (C,),
    (C,),
    (S, 3, 2, 2, 1),
    (S, 3, 2, 0, 2),
    (S, 5, 1, 7, 1),
    (S, 4, 1, 4, 4),
    (S, 2, 2, 0, 1),
    (F, 2, 1, 1),
    (F, 2, 2, 0),
    (F, 3, 1, 1),
    (U, 6),
    (C,),
    (S, 5, 1, 5, 2),
    (S, 4, 1, 3, 1),
    (S, 4, 1, 2, 1),
    (F, 2, 2, 1),
    (F, 3, 2, 0),
    (S, 3, 3, 1, 1),
    (S, 3, 3, 0, 1),
    (L, 6),
    (C,),
    (F, 3, 2, 1),
    (F, 3, 3, 0),
    (S, 3, 4, 0, 1),
    (F, 3, 3, 1),
    (F, 4, 1, 0),
    (C,),
    (C,),
    (S, 5, 1, 4, 1),
    (S, 5, 1, 1, 3),
    (S, 4, 1, 0, 2),
    (S, 2, 3, 1, 1),
    (S, 2, 3, 0, 1),
    (F, 3, 4, 0),
    (C,),
    (S, 5, 1, 0, 1),
    (S, 6, 1, 7, 1),
    (F, 5, 1, 0),
    (S, 5, 2, 3, 1),
    (F, 4, 1, 1),
    (S, 5, 2, 2, 1),
    (S, 4, 2, 3, 1),
    (S, 6, 1, 6, 1),
    (S, 5, 2, 0, 2),
    (C,),
    (F, 2, 3, 0),
    (F, 2, 3, 1),
    (C,),
    (C,),
    (S, 4, 2, 2, 1),
    (S, 4, 2, 0, 2),
    (S, 6, 1, 4, 2),
    (S, 6, 1, 2, 2),
    (S, 2, 4, 0, 1),
    (F, 5, 1, 1),
    (F, 5, 2, 0),
    (A, 0),
    (F, 5, 2, 1),
    (A, 1),
    (C,),
    (S, 6, 1, 1, 1),
    (F, 4, 2, 0),
    (S, 4, 3, 1, 1),
    (F, 6, 1, 0),
    (S, 4, 3, 0, 1),
    (F, 2, 4, 0),
    (F, 4, 2, 1),
    (F, 4, 3, 0),
    (S, 4, 4, 0, 1),
    (S, 6, 2, 3, 1),
    (S, 6, 1, 0, 1),
    (S, 5, 3, 1, 1),
    (C,),
    (F, 4, 3, 1),
    (S, 6, 2, 2, 1),
    (S, 6, 2, 0, 2),
    (S, 5, 3, 0, 1),
    (U, 7),
    (X, 0),
    (F, 4, 4, 0),
    (F, 6, 1, 1),
    (A, 2),
    (X, 1),
    (F, 5, 3, 0),
    (S, 5, 4, 0, 1),
    (L, 7),
    (S, 7, 1, 4, 4),
    (U, 8),
    (F, 5, 3, 1),
    (S, 7, 1, 3, 1),
    (F, 6, 2, 0),
    (S, 6, 3, 1, 1),
    (S, 6, 3, 0, 1),
    (X, 2),
    (X, 3),
    (F, 5, 4, 0),
    (S, 7, 1, 1, 2),
    (F, 6, 2, 1),
    (A, 3),
    (L, 8),
    (S, 8, 1, 4, 4),
    (S, 8, 1, 0, 4),
    (U, 9),
    (F, 6, 3, 0),
    (S, 7, 1, 0, 1),
    (S, 6, 4, 0, 1),
    (X, 4),
    (F, 6, 3, 1),
    (X, 5),
    (A, 4),
    (L, 9),
    (S, 9, 1, 6, 2),
    (S, 9, 1, 5, 1),
    (U, 10),
    (F, 7, 1, 0),
    (S, 9, 1, 4, 1),
    (S, 7, 2, 2, 2),
    (S, 7, 2, 0, 2),
    (F, 8, 1, 0),
    (S, 8, 2, 2, 2),
    (S, 8, 2, 0, 2),
    (X, 6),
    (F, 6, 4, 0),
    (S, 9, 1, 3, 1),
    (X, 7),
    (A, 5),
    (L, 10),
    (S, 10, 1, 6, 2),
    (X, 8),
    (X, 9),
    (F, 8, 1, 1),
    (S, 10, 1, 5, 1),
    (S, 9, 1, 1, 2),
    (X, 10),
    (F, 7, 1, 1),
    (S, 10, 1, 4, 1),
    (S, 9, 1, 0, 1),
    (F, 7, 2, 0),
    (X, 11),
    (U, 11),
    (F, 7, 2, 1),
    (S, 10, 1, 2, 2),
    (S, 7, 3, 1, 1),
    (F, 8, 2, 0),
    (S, 8, 3, 1, 1),
    (S, 8, 3, 0, 1),
    (A, 6),
    (X, 12),
    (F, 8, 2, 1),
    (S, 10, 1, 1, 1),
    (S, 7, 3, 0, 1),
    (X, 13),
    (F, 8, 3, 0),
    (S, 8, 4, 0, 1),
    (F, 9, 1, 0),
    (L, 11),
    (S, 10, 1, 0, 1),
    (S, 11, 1, 4, 4),
    (U, 12),
    (F, 8, 3, 1),
    (S, 9, 2, 3, 1),
    (S, 11, 1, 3, 1),
    (A, 7),
    (S, 9, 2, 2, 1),
    (S, 11, 1, 2, 1),
    (F, 8, 4, 0),
    (L, 12),
    (S, 12, 1, 5, 3),
    (S, 11, 1, 1, 1),
    (F, 10, 1, 0),
    (S, 9, 2, 1, 1),
    (F, 9, 1, 1),
    (U, 13),
    (F, 7, 3, 0),
    (S, 9, 2, 0, 1),
    (S, 12, 1, 4, 1),
    (S, 12, 1, 3, 1),
    (S, 11, 1, 0, 1),
    (S, 7, 4, 0, 1),
    (F, 7, 3, 1),
    (S, 12, 1, 2, 1),
    (L, 13),
    (F, 11, 1, 0),
    (S, 12, 1, 1, 1),
    (A, 8),
    (F, 10, 1, 1),
    (U, 14),
    (S, 12, 1, 0, 1),
    (F, 9, 2, 0),
    (S, 10, 2, 3, 1),
    (S, 9, 3, 1, 1),
    (S, 9, 3, 0, 1),
    (L, 14),
    (S, 10, 2, 2, 1),
    (F, 11, 1, 1),
    (S, 10, 2, 1, 1),
    (F, 12, 1, 0),
    (S, 12, 2, 2, 2),
    (S, 12, 2, 1, 1),
    (F, 9, 2, 1),
    (S, 12, 2, 0, 1),
    (U, 15),
    (S, 13, 1, 7, 1),
    (S, 10, 2, 0, 1),
    (F, 7, 4, 0),
    (S, 13, 1, 6, 1),
    (S, 11, 2, 3, 1),
    (F, 9, 3, 0),
    (S, 9, 4, 0, 1),
    (L, 15),
    (S, 11, 2, 2, 1),
    (A, 9),
    (S, 13, 1, 5, 1),
    (F, 9, 3, 1),
    (F, 12, 1, 1),
    (S, 11, 2, 1, 1),
    (A, 10),
    (S, 13, 1, 4, 1),
    (F, 12, 2, 0),
    (S, 13, 1, 3, 1),
    (S, 11, 2, 0, 1),
    (S, 12, 3, 1, 1),
    (S, 12, 3, 0, 1),
    (F, 9, 4, 0),
    (F, 10, 2, 0),
    (S, 10, 3, 1, 1),
    (S, 10, 3, 0, 1),
    (S, 13, 1, 2, 1),
    (F, 12, 2, 1),
    (S, 13, 1, 1, 1),
    (F, 12, 3, 0),
    (S, 12, 4, 0, 1),
    (F, 12, 3, 1),
    (F, 10, 2, 1),
    (S, 13, 1, 0, 1),
    (S, 14, 1, 5, 3),
    (F, 10, 3, 0),
    (S, 10, 4, 0, 1),
    (F, 10, 3, 1),
    (S, 14, 1, 4, 1),
    (F, 11, 2, 0),
    (S, 11, 3, 1, 1),
    (S, 14, 1, 3, 1),
    (F, 13, 1, 0),
    (S, 11, 3, 0, 1),
    (S, 14, 1, 2, 1),
    (S, 13, 2, 2, 2),
    (S, 13, 2, 0, 2),
    (F, 12, 4, 0),
    (F, 11, 2, 1),
    (S, 14, 1, 1, 1),
    (S, 15, 1, 6, 2),
    (F, 10, 4, 0),
    (S, 15, 1, 5, 1),
    (S, 14, 1, 0, 1),
    (F, 13, 1, 1),
    (S, 15, 1, 4, 1),
    (S, 15, 1, 3, 1),
    (F, 13, 2, 0),
    (S, 13, 3, 1, 1),
    (S, 13, 3, 0, 1),
    (F, 14, 1, 0),
    (S, 14, 2, 2, 2),
    (S, 14, 2, 0, 2),
    (F, 11, 3, 0),
    (S, 15, 1, 2, 1),
    (S, 11, 4, 0, 1),
    (F, 11, 3, 1),
    (F, 13, 2, 1),
    (S, 15, 1, 1, 1),
    (S, 15, 1, 0, 1),
    (F, 13, 3, 0),
    (S, 13, 4, 0, 1),
    (F, 14, 1, 1),
    (F, 14, 2, 0),
    (S, 14, 3, 1, 1),
    (S, 14, 3, 0, 1),
    (F, 15, 1, 0),
    (S, 15, 2, 2, 2),
    (S, 15, 2, 0, 2),
    (F, 14, 2, 1),
    (F, 13, 3, 1),
    (F, 11, 4, 0),
    (F, 15, 1, 1),
    (F, 15, 2, 0),
    (S, 15, 3, 1, 1),
    (S, 15, 3, 0, 1),
    (F, 13, 4, 0),
    (F, 15, 2, 1),
    (F, 14, 3, 0),
    (S, 14, 4, 0, 1),
    (F, 15, 3, 0),
    (S, 15, 4, 0, 1),
    (F, 14, 3, 1),
    (F, 15, 3, 1),
    (F, 14, 4, 0),
    (F, 15, 4, 0),
)
CHANNELS = 4
STAGES = 5
SLOT_ROWS = 200


class Scatter:
    def __init__(self, grid, total, stage, low, landing, stage_sems, send_sems, recv_sems, credits):
        self.grid, self.total = grid, total
        self.stage, self.low, self.landing = stage, low, landing
        self.stage_sems, self.send_sems, self.recv_sems, self.credits = stage_sems, send_sems, recv_sems, credits
        self.shift = grid.bits - STAGES
        self.rows = {}

    def bit(self, b):
        return (self.grid.me() // (1 << (b + self.shift))) % 2

    def partner(self, b):
        return self.grid.place(self.grid.me() + (1 - 2 * self.bit(b)) * (1 << (b + self.shift)))

    def part(self, q, k):
        out = 0
        for t, b in enumerate(ORDERS[q]):
            own = self.bit(b)
            out = out + (1 << b) * ((1 - own) if (k >> (STAGES - 1 - t)) & 1 else own)
        return out

    def send(self, q, t, first=0, number=None):
        channel, rows = q % CHANNELS, self.rows[q]
        slots = 16 >> t
        at, size = first * rows, (slots if number is None else number) * rows
        if t == 0:
            source, sem = self.stage.at[q % 2, at : at + size], self.stage_sems.at[q % 2]
        else:
            start = slots * rows + at
            source, sem = self.landing[t - 1].at[channel, start : start + size], self.send_sems.at[channel, t]
        half = 0 if t == 0 or first >= slots // 2 else 1
        return pltpu.make_async_remote_copy(
            src_ref=source,
            dst_ref=self.landing[t].at[channel, at : at + size],
            send_sem=sem,
            recv_sem=self.recv_sems.at[channel, t, half],
            device_id=self.partner(ORDERS[q][t]),
            device_id_type=MESH_ID,
        )

    def feed(self, q, t, first, number):
        if first + number == 16 >> t and q >= CHANNELS:
            pl.semaphore_wait(self.credits.at[q - CHANNELS, t], 1)
        self.send(q, t, first, number).start()

    def free(self, q, t):
        if q + CHANNELS < self.total:
            pl.semaphore_signal(
                self.credits.at[q, t],
                inc=1,
                device_id=self.partner(ORDERS[q + CHANNELS][t]),
                device_id_type=MESH_ID,
            )

    def upper(self, q, rows, fill):
        self.rows[q] = rows
        if q >= 2:
            self.send(q - 2, 0).wait_send()
        fill(self.stage.at[q % 2], True)
        self.feed(q, 0, 0, 16)
        fill(self.low, False)

    def lower(self, q):
        channel, rows = q % CHANNELS, self.rows[q]
        self.send(q, 0).wait_recv()
        mine = self.landing[0].at[channel]

        def add(i, c):
            r = pl.ds(pl.multiple_of(i * rows, 8), rows)
            mine[r, :] += self.low[r, :]
            return c

        lax.fori_loop(0, 16, add, 0)

    def fold(self, q, t, half):
        channel, rows = q % CHANNELS, self.rows[q]
        number = 8 >> t
        first = number if half == 0 else 0
        self.send(q, t, first, number).wait_recv()
        mine, before = self.landing[t].at[channel], self.landing[t - 1].at[channel]

        def add(i, c):
            r = pl.ds(pl.multiple_of(i * rows, 8), rows)
            mine[r, :] += before[r, :]
            return c

        lax.fori_loop(first, first + number, add, 0)
        if half == 1:
            self.send(q, t).wait_send()
            self.free(q, t - 1)

    def last(self, q, done):
        channel, rows = q % CHANNELS, self.rows[q]
        t = STAGES - 1
        self.send(q, t).wait_recv()
        done(self.landing[t][channel, 0:rows, :] + self.landing[t - 1][channel, 0:rows, :])
        self.send(q, t).wait_send()
        self.free(q, t - 1)
        self.free(q, t)


class Spread:
    def __init__(self, scatter, block, landing, whole, sems):
        self.scatter, self.block, self.landing, self.whole, self.sems = scatter, block, landing, whole, sems
        self.rows = block.shape[0]

    def begin(self, t):
        out = 0
        for i in range(t):
            out = out + self.scatter.bit(i) * (self.rows >> (i + 1))
        return out

    def halving(self, t):
        size = self.rows >> (t + 1)
        at = self.begin(t) + (1 - self.scatter.bit(t)) * size
        return pltpu.make_async_remote_copy(
            src_ref=self.block.at[pl.ds(pl.multiple_of(at, 8), size)],
            dst_ref=self.landing[t],
            send_sem=self.sems.at[0, t],
            recv_sem=self.sems.at[1, t],
            device_id=self.scatter.partner(t),
            device_id_type=MESH_ID,
        )

    def doubling(self, t, arriving=False):
        size = self.rows >> (t + 1)
        at = self.begin(t + 1)
        there = self.begin(t) + (1 - self.scatter.bit(t)) * size if arriving else at
        return pltpu.make_async_remote_copy(
            src_ref=self.whole.at[pl.ds(pl.multiple_of(at, 8), size)],
            dst_ref=self.whole.at[pl.ds(pl.multiple_of(there, 8), size)],
            send_sem=self.sems.at[2, t],
            recv_sem=self.sems.at[3, t],
            device_id=self.scatter.partner(t),
            device_id_type=MESH_ID,
        )

    def step(self, i):
        if i == 0:
            self.halving(0).start()
        elif i <= STAGES:
            t = i - 1
            self.halving(t).wait_recv()
            size = self.rows >> (t + 1)
            r = pl.ds(pl.multiple_of(self.begin(t + 1), 8), size)
            target = self.whole if i == STAGES else self.block
            target[r, :] = self.block[r, :] + self.landing[t][...]
            self.halving(t).wait_send()
            if i < STAGES:
                self.halving(t + 1).start()
            else:
                self.doubling(t).start()
        else:
            t = 2 * STAGES - i
            self.doubling(t, True).wait_recv()
            self.doubling(t).wait_send()
            if t > 0:
                self.doubling(t - 1).start()


def one_hot(rows, target):
    lane = lax.broadcasted_iota(jnp.int32, (rows, target.shape[1]), 0)
    return jnp.where(lane == target, 1.0, 0.0).astype(BF16)


def column_parts(width, size):
    column = lax.broadcasted_iota(jnp.int32, (1, width), 1)
    part = jnp.zeros((1, width), jnp.int32)
    for m in range(1, width // size):
        part = part + jnp.where(column >= m * size, 1, 0)
    return column, part


def slot_of(scatter, q, bits, parts, part):
    order = [b for b in ORDERS[q] if b in bits]
    slot = jnp.zeros_like(part)
    for value in range(parts):
        at = 0
        for t, b in enumerate(order):
            own = scatter.bit(b)
            weight = 1 << (len(order) - 1 - t)
            at = at + weight * ((1 - own) if (value >> bits.index(b)) & 1 else own)
        slot = jnp.where(part == value, at, slot)
    return slot


def sum_blocks(gather, slot):
    levels = len(gather.grid.digits)
    yield
    for level in range(levels):
        gather.start(level, slot)
        if level < 2:
            yield
        gather.wait(level, slot)
        size = gather.grid.digits[level][1]
        buffer = gather.buffers[level].at[slot]
        total = sum([buffer[g] for g in range(1, size)], buffer[0])
        if level + 1 < levels:
            gather.own(level + 1, slot)[...] = total
    return total


def norm_gradient(grad, nrm, out, gather, slot, gain_row, shift_row, inv_row, scale, gain_out, shift_out):
    rows, width = grad.shape

    def gate(r, carry):
        n = nrm[r, :]
        value = gain_row * n + shift_row
        sig = sigmoid(value)
        g = grad[r, :] * sig * (1.0 + value * (1.0 - sig))
        grad[r, :] = g
        return carry[0] + column_sum(g), carry[1] + column_sum(g * n)

    zero = jnp.zeros((1, width), F32)
    shift_sum, gain_sum = row_loop(rows, gate, (zero, zero))
    own = gather.own(0, slot)
    put_row(own, 0, shift_sum, width)
    put_row(own, 8, gain_sum, width)
    total = yield from sum_blocks(gather, slot)
    shift_sum = take_row(total, 0, width)
    gain_sum = take_row(total, 8, width)
    shift_out[...] = shift_sum
    gain_out[...] = gain_sum
    factor = gain_row * inv_row
    shift_mean = shift_sum * scale
    gain_mean = gain_sum * scale

    def write(r, c):
        out[r, :] = (factor * (grad[r, :] - shift_mean - nrm[r, :] * gain_mean)).astype(BF16)
        return c

    row_loop(rows, write, 0)


D1_ROWS = 104
GX = 512
REP_ROWS = 2304


def backward_kernel(
    grid,
    latent,
    x_hbm,
    w1_hbm,
    outw_hbm,
    nrm_hbm0,
    nrm_hbm1,
    nrm_hbm2,
    nrm_hbm3,
    act1_hbm,
    act2_hbm,
    act3_hbm,
    xt_hbm,
    act4_ref,
    zlat_ref,
    head_ref_in,
    noise_ref,
    gid_ref,
    ggroup_ref,
    inv_ref,
    outb_ref,
    w2_ref,
    head_ref,
    d1_ref,
    d2_ref,
    gain_ref,
    shift_ref,
    g_out,
    gx_out,
    out25,
    enc_part,
    nar_part,
    d1_out,
    headw_out,
    outb_out,
    headb_out,
    gain_out,
    shift_out,
    *rest,
):
    levels = len(grid.digits)
    rest = list(rest)

    def take(n):
        got = rest[:n]
        del rest[:n]
        return got

    small, s_send, s_recv = take(levels), take(levels), take(levels)
    stage, low, *landing = take(2 + STAGES)
    stage_sems, send_sems, recv_sems, credits = take(4)
    rep_block, rep_whole, *rep_landing = take(2 + STAGES)
    (rep_sems,) = take(1)
    g_win, wide, gact, gpre4, gpre3, gpre2, gpre1, ghead, gcell, lhs, nrm_buf, fin = take(12)
    distinct = sorted(set(ORDERS[: -(-x_hbm.shape[1] // WIN)]))
    lhs_at = [distinct.index(o) if o in distinct else None for o in ORDERS]
    picked = lhs.at[0, 0:512]
    in_sems, g_sems, nrm_sems, xt_sem, act_sems, gx_sems = take(6)

    rows, genes = x_hbm.shape
    hidden = w2_ref.shape[0]
    spans = windows(genes)
    count = len(spans)
    cell_total = float(rows * grid.n)
    total = 2 * count + 2
    gather = Gather(grid, small, s_send, s_recv)
    first = count
    scatter = Scatter(grid, total, stage, low, landing, stage_sems, send_sems, recv_sems, credits)
    spread = Spread(scatter, rep_block, rep_landing, rep_whole, rep_sems)
    rep_outb = 7 * (D1_ROWS + 2 * latent)
    rep_headb = rep_outb + 8 * count

    peers = digit_peers(grid)
    greet(grid, peers)
    nrm_loads = {
        k: pltpu.make_async_copy(ref, nrm_buf.at[(k + 1) % 2], nrm_sems.at[k])
        for k, ref in enumerate((nrm_hbm0, nrm_hbm1, nrm_hbm2, nrm_hbm3))
    }
    nrm_loads[3].start()
    nrm_loads[2].start()


    def out_fill(s):
        buffer = g_win.at[s % 3]

        def fill(target, is_upper):
            first = hidden // 2 if is_upper else 0
            part = nn(lhs[lhs_at[s], first : first + hidden // 2, :], buffer[...])
            for c in range(WIN // 128):
                target[pl.ds(c, hidden // 2, stride=8), :] = part[:, 128 * c : 128 * (c + 1)]

        return fill

    def out_lhs(q):
        if ORDERS[q] in ORDERS[:q]:
            return
        mine = lhs.at[lhs_at[q]]
        column, part = column_parts(hidden, hidden // PARTS)
        slot = slot_of(scatter, q, (0, 1, 2, 3, 4), PARTS, part)
        target = column + (hidden // PARTS) * (slot - part)
        block = hidden // 5

        def some(i, c):
            at = pl.multiple_of(i * block, block)
            mine[pl.ds(at, block), :] = nt(one_hot(block, target - at), act4_ref[...]).astype(BF16)
            return c

        lax.fori_loop(0, 5, some, 0)

    def out_done(s):
        def done(value):
            fin[...] = value
            for c in range(WIN // 128):
                out25[:, WIN * s + 128 * c : WIN * s + 128 * (c + 1)] = fin[pl.ds(c, hidden // PARTS, stride=8), :]

        return done

    done = {s: out_done(s) for s in range(count)}
    pieces = {}
    for s in range(count):
        pieces[s] = (SLOT_ROWS, out_fill(s))

    plan = list(PLAN)

    def run(chain, cells=None):
        while plan:
            what, *which = plan[0]
            if what == C:
                if next(chain, None) is None:
                    return
            elif what == U:
                if which[0] < count:
                    out_lhs(which[0])
                scatter.upper(which[0], *pieces[which[0]])
            elif what == L:
                scatter.lower(which[0])
            elif what == S:
                scatter.feed(*which)
            elif what == X:
                cells(*which)
            elif what == A:
                spread.step(*which)
            elif which[1] < STAGES - 1:
                scatter.fold(*which)
            else:
                scatter.last(which[0], done[which[0]])
            del plan[0]

    def output_layer(w_ring, w_tail, x_ring, x_tail):
        def load(s):
            at, size = spans[s]
            tail = s == count - 1
            return (
                pltpu.make_async_copy(
                    outw_hbm.at[:, pl.ds(at, size)], w_tail if tail else w_ring.at[s % 3], in_sems.at[0, s]
                ),
                pltpu.make_async_copy(
                    x_hbm.at[:, pl.ds(at, size)], x_tail if tail else x_ring.at[s % 2], in_sems.at[1, s]
                ),
            )

        def save(s):
            return pltpu.make_async_copy(g_win.at[s % 3], g_out.at[:, pl.ds(WIN * s, WIN)], g_sems.at[s])

        def layers():
            for s in range(2):
                for copy in load(s):
                    copy.start()
            for s in range(count):
                yield from layer(s)

        def layer(s):
            at, size = spans[s]
            tail = s == count - 1
            w = w_tail if tail else w_ring.at[s % 3]
            x = x_tail if tail else x_ring.at[s % 2]
            for copy in load(s):
                copy.wait()
            wide[:, 0:size] = nn(act4_ref[...], w[...])
            bias = outb_ref[:, at : at + size]
            if s >= 3:
                save(s - 3).wait()
            g = g_win.at[s % 3]

            def residual(r, c):
                value = wide[r, 0:size] + bias - x[r, :].astype(F32)
                value = (value * (2.0 / cell_total)).astype(BF16)
                g[r, 0:size] = value
                return c + column_sum(value.astype(F32))

            put_row(rep_block, rep_outb + 8 * s, row_loop(rows, residual, jnp.zeros((1, size), F32)), size)
            if size < WIN:
                g[:, size:WIN] = jnp.zeros((rows, WIN - size), BF16)
            save(s).start()
            if s == 0:
                meet(peers)
            if s + 2 < count:
                for copy in load(s + 2):
                    copy.start()
            yield 0
            part = nt(g[:, 0:size], w[...])
            gact[...] = part if s == 0 else gact[...] + part
            yield 0

        run(layers())
        for s in range(count - 3, count):
            save(s).wait()

    pl.run_scoped(
        output_layer,
        pltpu.VMEM((3, hidden, WIN), BF16),
        pltpu.VMEM((hidden, spans[-1][1]), BF16),
        pltpu.VMEM((2, rows, WIN), BF16),
        pltpu.VMEM((rows, spans[-1][1]), BF16),
    )


    def pack(target, at, source, row, height):
        full = hidden // 128
        for c in range(full):
            target[pl.ds(pl.multiple_of(at + height * c, 8), height), :] = source[
                pl.ds(row, height), 128 * c : 128 * (c + 1)
            ]
        rest_width = hidden - 128 * full
        pieces = [source[pl.ds(row + 8 * i, 8), 128 * full : hidden] for i in range(height // 8)]
        target[pl.ds(pl.multiple_of(at + height * full, 8), 8), 0 : rest_width * len(pieces)] = jnp.concatenate(
            pieces, axis=1
        )

    def unpack(value, out, row, height):
        full = hidden // 128
        rest_width = hidden - 128 * full
        for c in range(full):
            out[row : row + height, 128 * c : 128 * (c + 1)] = value[height * c : height * (c + 1), :]
        for i in range(height // 8):
            out[row + 8 * i : row + 8 * i + 8, 128 * full : hidden] = value[
                height * full : height * full + 8, rest_width * i : rest_width * (i + 1)
            ]

    def finish(xt, act_buf, w1_ring, w1_tail, gx_ring):
        xt_load = pltpu.make_async_copy(xt_hbm, xt, xt_sem)
        xt_load.start()

        gx_spans = windows(genes, GX)

        def gx_load(i):
            at, size = gx_spans[i]
            return (
                pltpu.make_async_copy(
                    w1_hbm.at[:, pl.ds(at, size)], w1_ring.at[i % 2] if size == GX else w1_tail, gx_sems.at[0, i]
                ),
                pltpu.make_async_copy(
                    g_out.at[:, pl.ds(at, GX)], g_win.at[i % 2, :, pl.ds(0, GX)], gx_sems.at[1, i]
                ),
            )

        def gx_save(i):
            return pltpu.make_async_copy(gx_ring.at[i % 2], gx_out.at[:, pl.ds(GX * i, GX)], gx_sems.at[2, i])

        def grad_cells(i):
            at, size = gx_spans[i]
            if i == 0:
                for copy in gx_load(0):
                    copy.start()
            if i + 1 < len(gx_spans):
                for copy in gx_load(i + 1):
                    copy.start()
            for copy in gx_load(i):
                copy.wait()
            if i >= 2:
                gx_save(i - 2).wait()
            wide[:, 0:size] = nn(gpre1[...], w1_ring[i % 2] if size == GX else w1_tail[...])

            def write(r, c):
                value = wide[r, 0:size] - g_win[i % 2, r, 0:size].astype(F32)
                gx_ring[i % 2, r, 0:size] = (cell_total * value).astype(BF16)
                return c

            row_loop(rows, write, 0)
            gx_save(i).start()
            if i + 1 == len(gx_spans):
                gx_save(i - 1).wait()
                gx_save(i).wait()

        def enc_fill(q, s):
            def fill(target, is_upper):
                for i in range(16):
                    j = scatter.part(q, 16 + i if is_upper else i)
                    picked[32 * i : 32 * i + 32, :] = xt[j, 32 * s : 32 * s + 32, :]
                wide[0:512, 0:hidden] = nn(picked[...], gpre1[...])

                def one(i, c):
                    pack(target, i * SLOT_ROWS, wide, pl.multiple_of(i * 32, 32), 32)
                    return c

                lax.fori_loop(0, 16, one, 0)

            return fill

        def enc_done(s):
            return lambda value: unpack(value, enc_part, 32 * s, 32)

        each = 2 * hidden // PARTS
        skip = (0, 32)

        def nar_fill(q, which):
            height_here = 32 if which == 0 else 24
            rows_here = 25 * 8 if which == 0 else 19 * 8
            place = STAGES - 1 - ORDERS[q].index(4)

            def fill(target, is_upper):
                column, part = column_parts(hidden, each)
                slot = slot_of(scatter, q, (0, 1, 2, 3), PARTS // 2, part)
                line = column - each * part - skip[which]
                inside = (line >= 0) & (line < height_here)
                base = 8 if is_upper else 0
                place_in = jnp.where(inside, (slot - base) * height_here + line, -1)
                place_in = jnp.where((slot >= base) & (slot < base + 8), place_in, -1)
                select = one_hot(8 * height_here, place_in)
                for matrix, act_slot, grad in ((0, 0, gpre2), (1, 1, gpre4)):
                    size = 8 * height_here
                    picked[0:size, :] = nt(select, act_buf[act_slot]).astype(BF16)
                    wide[0:size, 0:hidden] = nn(picked[0:size, :], grad[...])
                    flip = scatter.bit(4) if matrix == 0 else 1 - scatter.bit(4)
                    for i in range(8):
                        k = (i >> place) * (2 << place) + (i & ((1 << place) - 1)) + flip * (1 << place)
                        pack(target, k * rows_here, wide, i * height_here, height_here)

            return rows_here, fill

        def nar_done(which):
            if which == 0:
                return lambda value: unpack(value, nar_part, 0, 32)
            return lambda value: unpack(value, nar_part, 32, 24)

        for which in range(2):
            done[first + which] = nar_done(which)
            pieces[first + which] = nar_fill(first + which, which)
        for s in range(count):
            done[first + 2 + s] = enc_done(s)
            pieces[first + 2 + s] = (SLOT_ROWS, enc_fill(first + 2 + s, s))

        def row(ref, k):
            return ref[k : k + 1, :]

        def back(k, grad, out):
            nrm_loads[k].wait()
            return norm_gradient(
                grad,
                nrm_buf.at[(k + 1) % 2],
                out,
                gather,
                k,
                row(gain_ref, k),
                row(shift_ref, k),
                row(inv_ref, k),
                1.0 / cell_total,
                gain_out.at[k : k + 1, :],
                shift_out.at[k : k + 1, :],
            )

        act_loads = [
            pltpu.make_async_copy(ref, act_buf.at[at], act_sems.at[i])
            for i, (ref, at) in enumerate(((act1_hbm, 0), (act3_hbm, 1), (act2_hbm, 0)))
        ]
        act_loads[1].start()
        act_loads[2].start()

        def latent_side():
            act_loads[2].wait()
            d1_grad = tn(zlat_ref[...], gpre3[...])
            headw_grad = tn(ghead[...], act_buf[0])
            act_loads[0].start()
            for c in range(-(-hidden // 128)):
                size = min(128, hidden - 128 * c)
                at = D1_ROWS * c
                rep_block[at : at + latent, 0:size] = d1_grad[:, 128 * c : 128 * c + size]
                at = 7 * D1_ROWS + 2 * latent * c
                rep_block[at : at + 2 * latent, 0:size] = headw_grad[:, 128 * c : 128 * c + size]
            put_row(rep_block, rep_headb, column_sum(ghead[...].astype(F32)), 2 * latent)

        def chain():
            for k, out in ((3, gpre4), (2, gpre3), (1, gpre2), (0, gpre1)):
                waits = back(k, gact, out)
                for at, _ in enumerate(waits):
                    if (k, at) == (3, 1):
                        groups = ggroup_ref.shape[0]
                        member = (lax.broadcasted_iota(jnp.int32, (groups, rows), 0) == gid_ref[...]).astype(F32)
                        gcell[...] = exact(member, ggroup_ref[...], ((0,), (0,)))
                    if (k, at) == (1, 1):
                        latent_side()
                    yield 0
                if k == 3:
                    nrm_loads[1].start()
                    gact[...] = nt(gpre4[...], d2_ref[...])
                elif k == 2:
                    nrm_loads[0].start()
                    grad_z = nt(gpre3[...], d1_ref[...])
                    mu = head_ref_in[:, 0:latent]
                    logvar = head_ref_in[:, latent : 2 * latent]
                    kl = KL_WEIGHT * genes / cell_total
                    deviation = jnp.exp(0.5 * logvar)
                    grad_mu = grad_z + kl * mu + gcell[:, 0:latent]
                    grad_logvar = grad_z * noise_ref[...].T * (0.5 * deviation) + 0.5 * kl * (jnp.exp(logvar) - 1.0)
                    ghead[...] = jnp.concatenate([grad_mu, grad_logvar], axis=1).astype(BF16)
                    gact[...] = nn(ghead[...], head_ref[...])
                elif k == 1:
                    gact[...] = nt(gpre2[...], w2_ref[...])
                else:
                    for copy in act_loads[:2]:
                        copy.wait()
                    xt_load.wait()
                yield 0

        run(chain(), grad_cells)
        for q in (total - 2, total - 1):
            scatter.send(q, 0).wait_send()
        for c in range(-(-hidden // 128)):
            size = min(128, hidden - 128 * c)
            at = D1_ROWS * c
            d1_out[:, 128 * c : 128 * c + size] = rep_whole[at : at + latent, 0:size]
            at = 7 * D1_ROWS + 2 * latent * c
            headw_out[:, 128 * c : 128 * c + size] = rep_whole[at : at + 2 * latent, 0:size]
        outb_out[...] = rep_whole[rep_outb : rep_outb + 8 * count, :]
        headb_out[...] = rep_whole[rep_headb : rep_headb + 8, :]
        for level in range(levels):
            for k in range(4):
                gather.finish(level, k)

    pl.run_scoped(
        finish,
        pltpu.VMEM(xt_hbm.shape, BF16),
        pltpu.VMEM((2, rows, hidden), BF16),
        pltpu.VMEM((2, hidden, GX), BF16),
        pltpu.VMEM((hidden, windows(genes, GX)[-1][1]), BF16),
        pltpu.VMEM((2, rows, GX), BF16),
    )


def call_backward(grid, kept, cells_x, w1t, out_w, noise, gid, out_b, w2, headt, d1, d2, gain, shift):
    (nrm0, nrm1, nrm2, nrm3, inv, act1, act2, zlat, act3, act4, head, ggroup, xt) = kept
    rows, genes = cells_x.shape
    hidden, latent = w2.shape[0], d1.shape[0]
    spans = windows(genes)
    count = len(spans)
    vm = pl.BlockSpec(memory_space=pltpu.VMEM)
    hbm = pl.BlockSpec(memory_space=pl.ANY)
    shape = jax.ShapeDtypeStruct
    out_shape = (
        shape((rows, WIN * count), BF16),
        shape((rows, WIN * count), BF16),
        shape((hidden // PARTS, WIN * count), F32),
        shape((32 * count, hidden), F32),
        shape((56, hidden), F32),
        shape((latent, hidden), F32),
        shape((2 * latent, hidden), F32),
        shape((8 * count, 128), F32),
        shape((8, 128), F32),
        shape((4, hidden), F32),
        shape((4, hidden), F32),
    )
    dma = pltpu.SemaphoreType.DMA
    scratch = (
        [pltpu.VMEM((4, size, 16, 128), F32) for _, size in grid.digits]
        + [dma((4, size - 1)) for _, size in grid.digits]
        + [dma((4, size - 1)) for _, size in grid.digits]
        + [pltpu.VMEM((2, 16 * SLOT_ROWS, 128), F32), pltpu.VMEM((16 * SLOT_ROWS, 128), F32)]
        + [pltpu.VMEM((CHANNELS, (16 >> t) * SLOT_ROWS, 128), F32) for t in range(STAGES)]
        + [dma((2,)), dma((CHANNELS, STAGES)), dma((CHANNELS, STAGES, 2)), pltpu.SemaphoreType.REGULAR((2 * count + 2 - CHANNELS, STAGES))]
        + [pltpu.VMEM((REP_ROWS, 128), F32), pltpu.VMEM((REP_ROWS, 128), F32)]
        + [pltpu.VMEM((REP_ROWS >> (t + 1), 128), F32) for t in range(STAGES)]
        + [dma((4, STAGES))]
        + [
            pltpu.VMEM((3, rows, WIN), BF16),
            pltpu.VMEM((rows, WIN), F32),
            pltpu.VMEM((rows, hidden), F32),
            pltpu.VMEM((rows, hidden), BF16),
            pltpu.VMEM((rows, hidden), BF16),
            pltpu.VMEM((rows, hidden), BF16),
            pltpu.VMEM((rows, hidden), BF16),
            pltpu.VMEM((rows, 2 * latent), BF16),
            pltpu.VMEM((rows, 128), F32),
            pltpu.VMEM((len(set(ORDERS[:count])), hidden, rows), BF16),
            pltpu.VMEM((2, rows, hidden), F32),
            pltpu.VMEM((SLOT_ROWS, 128), F32),
        ]
        + [dma((2, count)), dma((count,)), dma((4,)), dma, dma((3,)), dma((3, len(windows(genes, GX))))]
    )
    return pl.pallas_call(
        functools.partial(backward_kernel, grid, latent),
        out_shape=out_shape,
        in_specs=[hbm] * 11 + [vm] * 14,
        out_specs=[hbm] * 2 + [vm] * (len(out_shape) - 2),
        scratch_shapes=scratch,
        name="backward",
        compiler_params=pltpu.CompilerParams(
            collective_id=1, has_side_effects=True, vmem_limit_bytes=63 * 2**20
        ),
    )(
        cells_x,
        w1t,
        out_w,
        nrm0,
        nrm1,
        nrm2,
        nrm3,
        act1,
        act2,
        act3,
        xt,
        act4,
        zlat,
        head,
        noise,
        gid,
        ggroup,
        inv,
        out_b,
        w2,
        headt,
        d1,
        d2,
        gain,
        shift,
    )


def widen(value, width):
    rows = value.shape[0]
    block = 96

    def kernel(a, b):
        b[...] = a[:, 0:width].astype(F32)

    return pl.pallas_call(
        kernel,
        out_shape=jax.ShapeDtypeStruct((rows, width), F32),
        grid=(rows // block,),
        in_specs=[pl.BlockSpec((block, value.shape[1]), lambda i: (i, 0))],
        out_specs=pl.BlockSpec((block, width), lambda i: (i, 0)),
        name="widen",
        cost_estimate=pl.CostEstimate(flops=0, bytes_accessed=6 * rows * width, transcendentals=0),
        compiler_params=pltpu.CompilerParams(vmem_limit_bytes=62 * 2**20),
    )(value)


def flat_shard(grid, flat, columns, rows_in_all):
    value = flat.reshape(rows_in_all // PARTS, columns)
    size = grid.n // PARTS
    if size > 1:
        groups = [list(range(size * p, size * p + size)) for p in range(PARTS)]
        value = lax.psum_scatter(
            value, ("cells", "rep"), scatter_dimension=0, axis_index_groups=groups, tiled=True
        )
    return value


def group_sum(grid, values):
    size = grid.n // PARTS
    if size > 1:
        groups = [list(range(size * p, size * p + size)) for p in range(PARTS)]
        values = lax.psum(values, ("cells", "rep"), axis_index_groups=groups)
    return values


def shards(
    grid,
    cells_x,
    latent_noise,
    group_ids,
    owner_table,
    owner_mask,
    enc_w1,
    enc_w2,
    head_w,
    head_b,
    dec_w1,
    dec_w2,
    out_w,
    out_b,
    bn_gain,
    bn_shift,
):
    cell_total = float(cells_x.shape[0] * grid.n)
    genes = cells_x.shape[1]
    hidden = enc_w2.shape[0]
    gid = group_ids.reshape(1, -1)
    headt = head_w.T
    w1t = enc_w1.T
    noise = latent_noise.T
    *kept, offsets = call_forward(
        grid,
        cells_x,
        w1t,
        noise,
        gid,
        owner_table.T,
        owner_mask.T,
        enc_w2,
        headt,
        head_b.reshape(1, -1),
        dec_w1,
        dec_w2,
        bn_gain,
        bn_shift,
    )
    _, gx, out25, enc_part, nar_part, d1_grad, headw_grad, outb_grad, headb_grad, grad_gain, grad_shift = call_backward(
        grid,
        kept,
        cells_x,
        w1t,
        out_w,
        noise,
        gid,
        out_b.reshape(1, -1),
        enc_w2,
        headt,
        dec_w1,
        dec_w2,
        bn_gain,
        bn_shift,
    )
    grad_x = widen(gx, genes)
    part = grid.me() // (grid.n // PARTS)
    each = genes * hidden // PARTS
    enc_flat = lax.dynamic_slice_in_dim(enc_part.reshape(-1), (genes * part) % PARTS * (hidden // PARTS), each)
    shard_enc = flat_shard(grid, enc_flat, FLAT_COLS, FLAT_ROWS)
    shard_out = flat_shard(grid, out25[:, :genes], FLAT_COLS, FLAT_ROWS)
    shard_narrow = flat_shard(grid, nar_part[: 2 * hidden // PARTS], NARROW_COLS, NARROW_ROWS)
    headw_grad, d1_grad, headb_grad, outb_grad = group_sum(
        grid,
        (headw_grad.T, d1_grad, headb_grad.reshape(-1)[: head_b.shape[0]], outb_grad.reshape(-1)[:genes]),
    )
    return (
        grad_x,
        shard_enc,
        shard_narrow,
        headw_grad,
        d1_grad,
        headb_grad,
        shard_out,
        outb_grad,
        grad_gain,
        grad_shift,
        offsets[None],
    )


def solution(mesh):
    grid = Slice(mesh.shape["cells"], mesh.shape["rep"])
    lines = P(("cells", "rep"), None)
    return jax.shard_map(
        functools.partial(shards, grid),
        mesh=mesh,
        in_specs=(lines, lines, P(("cells", "rep"))) + (P(),) * 12,
        out_specs=(lines, lines, lines, P(), P(), P(), lines, P(), P(), P(), P("cells", None, None)),
        check_vma=False,
    )
```
